128 devices in a mesh: pipe: 2 (over x_hi), group: 8 (over z, x_lo), rep: 8 (over y, core).
Axes of the slice: x: 4 (x_hi: 2, x_lo: 2; x = x_hi * 2 + x_lo), y: 4, z: 4, core: 2. Of those that a mesh axis runs over, the one named last changes fastest.
Arguments:
- block_input: bfloat16 [2, 8, 1024, 1088], P(None, 'rep', 'group'), may hold values from -6 to 6
- out_grad: bfloat16 [2, 8, 1024, 1088], P(None, 'rep', 'group'), may hold values from -6 to 6
- w_qkv: bfloat16 [2, 1088, 3264], P('pipe', 'group'), may hold values from -0.1875 to 0.1875
- w_proj: bfloat16 [2, 1088, 1088], P('pipe', 'group'), may hold values from -0.5 to 0.5
- w_up: bfloat16 [2, 1088, 4352], P('pipe', 'group'), may hold values from -0.1875 to 0.1875
- w_down: bfloat16 [2, 4352, 1088], P('pipe', 'group'), may hold values from -0.09375 to 0.09375
- vectors: bfloat16 [2, 8, 1088], P('pipe', None, 'group'), as said below
- b_up: bfloat16 [2, 4352], P('pipe', 'group'), may hold values from -3 to 3
- seq_lengths: int32 [16], replicated, may hold values from 512 to 1024, as said below
- slot_of_seq: int32 [16], replicated, may hold values from 0 to 15, as said below
Outputs:
- section_edges: float32 [2, 2, 8, 1024, 1088], P('pipe', None, 'rep', 'group')
- grad_qkv: float32 [2, 1088, 3264], P('pipe', 'group')
- grad_proj: float32 [2, 1088, 1088], P('pipe', 'group')
- grad_up: float32 [2, 1088, 4352], P('pipe', 'group')
- grad_down: float32 [2, 4352, 1088], P('pipe', 'group')
- grad_vectors: float32 [2, 8, 1088], P('pipe', None, 'group')
- grad_b_up: float32 [2, 4352], P('pipe', 'group')
The draws below stay inside these ranges and needn't reach their ends.
Inputs may be any that keep to these rules, and one draw needn't show every extreme that they name: `seq_lengths`: lengths of whole sequences; in every replica group one of its 2 sequences has exactly 1024 tokens. `slot_of_seq`: A permutation of the slots: each slot holds exactly one sequence. `vectors`: rows 0 and 5 are norm gains near one, the other rows biases.
All inputs are finite; a program needn't handle non-finite values.
Results may differ from the reference program's by a relative error of at most 0.013.
Values may be sent and summed in bfloat16 or wider, within the bound.
A program may use at most 320 MiB of HBM per device.

```python
import math
import jax
import jax.numpy as jnp
from jax import lax

D = 1088
HEADS = 17
HEAD = 64
FF = 4352
MICRO = 2
SECTIONS = 2
SLOT = 1024
SEQS = 16
N_REP = 8


def length_table(key):
    key_full, key_len, key_perm = jax.random.split(key, 3)
    rep_total = SEQS // MICRO
    full_micro = jax.random.randint(key_full, (rep_total,), 0, MICRO)
    lengths_slot = jax.random.randint(key_len, (SEQS,), SLOT // 2, SLOT + 1)
    slot_ids = jnp.arange(SEQS)
    lengths_slot = jnp.where(slot_ids // rep_total == full_micro[slot_ids % rep_total], SLOT, lengths_slot)
    placing = jax.random.permutation(key_perm, SEQS)
    return (lengths_slot[placing].astype(jnp.int32), placing.astype(jnp.int32))


def draw_seq_lengths(key, part):
    return length_table(key)[0]


def draw_slot_of_seq(key, part):
    return length_table(key)[1]


def draw_vectors(key, part):
    key = jax.random.fold_in(key, 11)
    noise = jax.random.normal(key, (SECTIONS, 8, D), jnp.float32)
    row_ids = jnp.arange(8)[None, :, None]
    is_gain = (row_ids == 0) | (row_ids == 5)
    return jnp.where(is_gain, 1.0 + 0.2 * noise, 0.5 * noise).astype(jnp.bfloat16)


def levels(stream_key, extent, pieces, smallest, high):
    loudness, own = 1.0, jax.random.fold_in(stream_key, 6)
    for axis_at, parts in pieces:
        heights = jnp.exp(jax.random.uniform(jax.random.fold_in(own, axis_at), (parts,), jnp.float32, smallest / len(pieces), high / len(pieces)))
        loudness = loudness * jnp.repeat(heights, extent[axis_at] // parts).reshape([-1 if axis == axis_at else 1 for axis in range(len(extent))])
    return loudness


def gaussian(key, dims, scale, most, shards=(), dtype=jnp.bfloat16):
    result = jax.random.normal(key, dims, jnp.float32) * scale
    if len(shards) > 0:
        result = levels(key, dims, shards, -0.22, 0.18) * result
    return jnp.clip(result, min=-most, max=most).astype(dtype)


def setup_inputs(seed: int = 0) -> dict:
    key_of = jax.random.split(jax.random.key(seed), 11)
    return {
        "block_input": gaussian(key_of[0], (MICRO, N_REP, SLOT, D), 1.0, 6.0, ((1, 8), (2, 8))),
        "out_grad": gaussian(key_of[1], (MICRO, N_REP, SLOT, D), 1.0, 6.0, ((1, 8), (2, 8))),
        "w_qkv": gaussian(key_of[2], (SECTIONS, D, 3 * D), D ** -0.5, 0.1875, ((0, 2), (1, 8))),
        "w_proj": gaussian(key_of[3], (SECTIONS, D, D), (D // 8) ** -0.5, 0.5, ((0, 2), (1, 8))),
        "w_up": gaussian(key_of[4], (SECTIONS, D, FF), D ** -0.5, 0.1875, ((0, 2), (1, 8))),
        "w_down": gaussian(key_of[5], (SECTIONS, FF, D), FF ** -0.5, 0.09375, ((0, 2), (1, 8))),
        "vectors": draw_vectors(jax.random.fold_in(key_of[10], 71), 0),
        "b_up": gaussian(key_of[7], (SECTIONS, FF), 0.3, 3.0, ((0, 2), (1, 8))),
        "seq_lengths": draw_seq_lengths(jax.random.fold_in(key_of[10], 71), 0),
        "slot_of_seq": draw_slot_of_seq(jax.random.fold_in(key_of[10], 71), 0),
    }


EPSILON = 1e-05
MASKED = -1e+30
PRECISE = lax.Precision.HIGHEST

@jax.custom_vjp
def low(v):
    return lax.optimization_barrier(v.astype(jnp.bfloat16)).astype(jnp.float32)

@jax.custom_vjp
def low_back(v):
    return v

def low_keep(v):
    return (low(v), None)

def low_pass(kept, grad):
    return (grad,)

def back_keep(v):
    return (v, None)

def back_low(kept, grad):
    return (low(grad),)
low.defvjp(low_keep, low_pass)
low_back.defvjp(back_keep, back_low)

def norm_rows(inputs, gain_row, bias_row):
    average = lax.optimization_barrier(jnp.mean(inputs, -1, keepdims=True))
    centered = inputs - average
    variance = lax.optimization_barrier(jnp.mean(centered * centered, -1, keepdims=True))
    return centered * lax.rsqrt(variance + EPSILON) * gain_row + bias_row

def product(left, right):
    return jnp.dot(left, right, precision=PRECISE, preferred_element_type=jnp.float32)

def attention_block(query_block, first_row, key_heads, value_heads, length):
    block_rows = query_block.shape[0]
    query_pos = first_row + jnp.arange(block_rows).astype(jnp.int32)
    key_pos = jnp.arange(key_heads.shape[0]).astype(jnp.int32)
    scores = low_back(HEAD ** (-0.5) * jnp.einsum('qhd,khd->hqk', query_block, key_heads, precision=PRECISE))
    allowed = (key_pos[None, :] <= query_pos[:, None]) & (key_pos[None, :] < length)
    scores = jnp.where(allowed[None], scores, MASKED)
    row_max = lax.optimization_barrier(jnp.max(scores, -1, keepdims=True))
    exponent = jnp.exp(scores - row_max)
    attn_probs = exponent / lax.optimization_barrier(jnp.sum(exponent, -1, keepdims=True))
    return jnp.einsum('hqk,khd->qhd', low(attn_probs), value_heads, precision=PRECISE)

def layer(weights, inputs, length):
    qkv_weight, proj_weight, up_weight, down_weight, vector_rows, up_bias = weights
    normed = low(norm_rows(inputs, vector_rows[0], vector_rows[1]))
    qkv_bias = jnp.concatenate([vector_rows[2], jnp.zeros_like(vector_rows[2]), vector_rows[3]])
    qkv_rows = low_back(low(product(normed, qkv_weight) + qkv_bias))
    query_heads = qkv_rows[:, :D].reshape(SLOT, HEADS, HEAD)
    key_heads = qkv_rows[:, D:2 * D].reshape(SLOT, HEADS, HEAD)
    value_heads = qkv_rows[:, 2 * D:].reshape(SLOT, HEADS, HEAD)
    block_rows = math.gcd(SLOT, 512)
    blocks = query_heads.reshape(SLOT // block_rows, block_rows, HEADS, HEAD)
    firsts = (jnp.arange(SLOT // block_rows) * block_rows).astype(jnp.int32)
    attn_mixed = lax.map(jax.checkpoint(lambda operands: attention_block(operands[0], operands[1], key_heads, value_heads, length)), (blocks, firsts))
    attn_mixed = low_back(low(attn_mixed.reshape(SLOT, D)))
    branch = low_back(product(attn_mixed, proj_weight) + vector_rows[4])
    hidden_in = inputs + branch
    normed_two = low(norm_rows(hidden_in, vector_rows[5], vector_rows[6]))
    pre_act = low_back(product(normed_two, up_weight) + up_bias)
    activated = low(jax.nn.gelu(pre_act, approximate=True))
    return hidden_in + low_back(product(activated, down_weight) + vector_rows[7])

def reference(block_input, out_grad, w_qkv, w_proj, w_up, w_down, vectors, b_up, seq_lengths, slot_of_seq):
    slot_ids = jnp.arange(SEQS).astype(jnp.int32)
    slot_len = lax.optimization_barrier(jnp.sum(seq_lengths[:, None] * (slot_of_seq[:, None] == slot_ids[None, :]).astype(jnp.int32), axis=0))
    weights = tuple((matrix.astype(jnp.float32) for matrix in (w_qkv, w_proj, w_up, w_down, vectors, b_up)))
    inputs = block_input.astype(jnp.float32).reshape(SEQS, SLOT, D)

    def forward(weights, inputs):

        def one_slot(operands):
            slot_rows, length = operands
            first_out = layer(tuple((matrix[0] for matrix in weights)), slot_rows, length)
            second_in = low_back(low(first_out))
            return layer(tuple((matrix[1] for matrix in weights)), second_in, length)
        return lax.map(jax.checkpoint(one_slot), (inputs, slot_len))
    outputs, pullback = jax.vjp(forward, weights, inputs)
    valid = (jnp.arange(SLOT).astype(jnp.int32)[None, :] < slot_len[:, None]).astype(jnp.float32)
    cotangent = out_grad.astype(jnp.float32).reshape(SEQS, SLOT, D) * valid[:, :, None]
    gradients, grad_inputs = pullback(cotangent)
    full_shape = (MICRO, N_REP, SLOT, D)
    section_edges = jnp.stack([grad_inputs.reshape(full_shape), outputs.reshape(full_shape)])
    return (section_edges, gradients[0], gradients[1], gradients[2], gradients[3], gradients[4], gradients[5])
```

```python
import functools
import jax
import jax.numpy as jnp
from jax import lax
from jax.experimental import pallas as pl
from jax.experimental.pallas import tpu as pltpu
from jax.sharding import PartitionSpec as P

HEAD = 64
LANES = 128
EPSILON = 1e-05
MASKED = -1e30
MESH = pl.DeviceIdType.MESH
RING = 4


def remote(src, dst, send_sem, recv_sem, device):
    return pltpu.make_async_remote_copy(
        src_ref=src,
        dst_ref=dst,
        send_sem=send_sem,
        recv_sem=recv_sem,
        device_id=device,
        device_id_type=MESH,
    )


def greet(devices):
    barrier = pltpu.get_barrier_semaphore()
    for device in devices:
        pl.semaphore_signal(barrier, inc=1, device_id=device, device_id_type=MESH)
    pl.semaphore_wait(barrier, len(devices))


def place():
    member, replica = lax.axis_index("group"), lax.axis_index("rep")
    return (member // 2, member % 2, replica // 2, replica % 2)


def gather_kernel(count, *refs):
    ins, outs = refs[:count], refs[count : 2 * count]
    send, recv, local = refs[2 * count :]
    z, x, y, c = place()
    me = 2 * z + x
    xc = (x + c) % 2
    zp, zm, zo = (z + 1) % RING, (z + 3) % RING, (z + 2) % RING
    base, above, below, across = 2 * z + xc, 2 * zp + xc, 2 * zm + xc, 2 * zo + xc
    to_above = {"group": 2 * zp + x}
    to_below = {"group": 2 * zm + x}
    sibling = {"rep": 2 * y + 1 - c}
    partner = {"group": 2 * z + 1 - x}
    greet([to_above, to_below, sibling, partner])

    def part(array, slot, kind):
        half = ins[array].shape[0] // 2
        ref = outs[array].at[slot]
        if kind == "low":
            return ref.at[pl.ds(0, half)]
        if kind == "high":
            return ref.at[pl.ds(half, ins[array].shape[0] - half)]
        return ref

    def across_x(i):
        return remote(ins[i], part(i, me, ""), send.at[i, 0], recv.at[i, 0], partner)

    def first_up(i):
        src = part(i, base, "")
        return remote(src, part(i, base, ""), send.at[i, 1], recv.at[i, 1], to_above)

    def first_down(i):
        src = part(i, base, "")
        return remote(src, part(i, base, ""), send.at[i, 2], recv.at[i, 2], to_below)

    def second_up(i):
        src = part(i, below, "low")
        return remote(src, src, send.at[i, 3], recv.at[i, 3], to_above)

    def second_down(i):
        src = part(i, above, "high")
        return remote(src, src, send.at[i, 4], recv.at[i, 4], to_below)

    def hand(i, slot, kind, sem):
        src = part(i, slot, kind)
        return remote(src, src, send.at[i, sem], recv.at[i, sem], sibling)

    def own(i):
        return pltpu.make_async_copy(ins[i], part(i, me, ""), local.at[i])

    def own_up(i):
        return remote(ins[i], part(i, me, ""), send.at[i, 1], recv.at[i, 1], to_above)

    def own_down(i):
        return remote(ins[i], part(i, me, ""), send.at[i, 2], recv.at[i, 2], to_below)

    arrays = range(count)

    @pl.when(c == 0)
    def _():
        for i in arrays:
            own_up(i).start()
            own_down(i).start()

    @pl.when(c == 1)
    def _():
        for i in arrays:
            across_x(i).start()

    for i in arrays:
        own(i).start()

    @pl.when(c == 1)
    def _():
        for i in arrays:
            remote(ins[i], part(i, base, ""), send.at[i, 0], recv.at[i, 0], partner).wait_recv()
            first_up(i).start()
            first_down(i).start()
            hand(i, base, "", 5).start()

    for i in arrays:
        remote(ins[i], part(i, below, ""), send.at[i, 1], recv.at[i, 1], to_above).wait_recv()
        second_up(i).start()
        hand(i, below, "", 6).start()
        remote(ins[i], part(i, above, ""), send.at[i, 2], recv.at[i, 2], to_below).wait_recv()
        second_down(i).start()
        hand(i, above, "", 7).start()
    for i in arrays:
        src = part(i, across, "low")
        remote(src, src, send.at[i, 3], recv.at[i, 3], to_above).wait_recv()
        hand(i, across, "low", 8).start()
        src = part(i, across, "high")
        remote(src, src, send.at[i, 4], recv.at[i, 4], to_below).wait_recv()
        hand(i, across, "high", 9).start()

    @pl.when(c == 0)
    def _():
        for i in arrays:
            hand(i, 2 * z + 1 - xc, "", 5).wait_recv()
            own_up(i).wait_send()
            own_down(i).wait_send()

    @pl.when(c == 1)
    def _():
        for i in arrays:
            across_x(i).wait_send()
            first_up(i).wait_send()
            first_down(i).wait_send()
            hand(i, base, "", 5).wait_send()

    for i in arrays:
        hand(i, 2 * zm + 1 - xc, "", 6).wait_recv()
        hand(i, 2 * zp + 1 - xc, "", 7).wait_recv()
        hand(i, 2 * zo + 1 - xc, "low", 8).wait_recv()
        hand(i, 2 * zo + 1 - xc, "high", 9).wait_recv()
        second_up(i).wait_send()
        second_down(i).wait_send()
        hand(i, below, "", 6).wait_send()
        hand(i, above, "", 7).wait_send()
        hand(i, across, "low", 8).wait_send()
        hand(i, across, "high", 9).wait_send()
        own(i).wait()


def gather_weights(shards):
    count = len(shards)
    return pl.pallas_call(
        functools.partial(gather_kernel, count),
        out_shape=[jax.ShapeDtypeStruct((8,) + s.shape, s.dtype) for s in shards],
        in_specs=[pl.BlockSpec(memory_space=pl.ANY)] * count,
        out_specs=[pl.BlockSpec(memory_space=pl.ANY)] * count,
        scratch_shapes=[
            pltpu.SemaphoreType.DMA((count, 10)),
            pltpu.SemaphoreType.DMA((count, 10)),
            pltpu.SemaphoreType.DMA((count,)),
        ],
        compiler_params=pltpu.CompilerParams(collective_id=0, has_side_effects=True),
        name="gather_weights",
    )(*shards)


def piece_rows(blocks):
    starts = [i * blocks // RING for i in range(RING + 1)]
    return max(starts[i + 1] - starts[i] for i in range(RING))


def add_blocks(count, dst, terms):
    def step(b, carry):
        total = dst[b].astype(jnp.float32)
        for term in terms:
            total = total + term[b].astype(jnp.float32)
        dst[b] = total.astype(dst.dtype)
        return carry

    lax.fori_loop(0, count, step, 0)


PER_ARRAY = 9


def sum_kernel(count, *refs):
    ins, outs = refs[:count], refs[count : 2 * count]
    buffers = refs[2 * count : 2 * count + PER_ARRAY * count]
    send, recv, local = refs[2 * count + PER_ARRAY * count :]
    z, x, y, c = place()
    xc = (x + c) % 2
    zp, zm = (z + 1) % RING, (z + 3) % RING
    to_above = {"group": 2 * zp + x}
    to_below = {"group": 2 * zm + x}
    sibling = {"rep": 2 * y + 1 - c}
    partner = {"group": 2 * z + 1 - x, "rep": 2 * y + 1 - c}
    others = [{"rep": 2 * ((y + j) % RING) + c} for j in range(1, RING)]
    greet([to_above, to_below, sibling, partner] + others)

    def parts(i):
        return buffers[PER_ARRAY * i : PER_ARRAY * (i + 1)]

    def swap(i, k):
        own, came = ins[i].at[2 * ((z + k) % RING) + 1 - xc], parts(i)[1].at[k]
        return remote(own, came, send.at[i, k], recv.at[i, k], sibling)

    def load(i, k):
        return pltpu.make_async_copy(
            ins[i].at[2 * ((z + k) % RING) + xc], parts(i)[0].at[k], local.at[i, k]
        )

    def sizes(i):
        blocks = ins[i].shape[1]
        return (blocks, blocks // 2, piece_rows(blocks))

    def far_up(i):
        blocks, half, _ = sizes(i)
        src = parts(i)[0].at[2, pl.ds(0, half)]
        return remote(src, parts(i)[2], send.at[i, 4], recv.at[i, 4], to_above)

    def far_down(i):
        blocks, half, _ = sizes(i)
        src = parts(i)[0].at[2, pl.ds(half, blocks - half)]
        return remote(src, parts(i)[3], send.at[i, 5], recv.at[i, 5], to_below)

    def near_up(i):
        return remote(parts(i)[0].at[1], parts(i)[4], send.at[i, 6], recv.at[i, 6], to_above)

    def near_down(i):
        return remote(parts(i)[0].at[3], parts(i)[5], send.at[i, 7], recv.at[i, 7], to_below)

    def over_x(i):
        return remote(parts(i)[0].at[0], parts(i)[6], send.at[i, 8], recv.at[i, 8], partner)

    def own_piece(i, owner):
        blocks, _, rows = sizes(i)
        return parts(i)[0].at[0, pl.ds((owner * blocks) // RING, rows)]

    def over_y(i, j):
        src = own_piece(i, (y + j) % RING)
        dst = parts(i)[7].at[j - 1]
        return remote(src, dst, send.at[i, 8 + j], recv.at[i, 8 + j], others[j - 1])

    def share_y(i, j, slot):
        dst = outs[i].at[slot]
        return remote(parts(i)[8], dst, send.at[i, 11 + j], recv.at[i, 11 + j], others[j - 1])

    def keep(i):
        return pltpu.make_async_copy(parts(i)[8], outs[i].at[y], local.at[i, 4])

    def hand(i):
        return remote(outs[i], outs[i], send.at[i, 15], recv.at[i, 15], sibling)

    for i in range(count):
        for k in (2, 1, 3, 0):
            swap(i, k).start()
            load(i, k).start()

    def step_cores(i):
        blocks, half, _ = sizes(i)
        total, came = parts(i)[0], parts(i)[1]
        for k in (2, 1, 3, 0):
            load(i, k).wait()
            swap(i, k).wait_recv()
            add_blocks(blocks, total.at[k], [came.at[k]])
            if k == 2:
                far_up(i).start()
                far_down(i).start()

    def step_far(i):
        blocks, half, _ = sizes(i)
        total = parts(i)[0]
        far_up(i).wait_recv()
        add_blocks(half, total.at[1, pl.ds(0, half)], [parts(i)[2]])
        near_up(i).start()
        far_down(i).wait_recv()
        add_blocks(blocks - half, total.at[3, pl.ds(half, blocks - half)], [parts(i)[3]])
        near_down(i).start()

    def step_near(i):
        blocks, half, _ = sizes(i)
        near_up(i).wait_recv()
        near_down(i).wait_recv()
        add_blocks(blocks, parts(i)[0].at[0], [parts(i)[4], parts(i)[5]])

        @pl.when(c == 1)
        def _():
            over_x(i).start()

    def step_x(i):
        blocks, half, _ = sizes(i)

        @pl.when(c == 0)
        def _():
            over_x(i).wait_recv()
            add_blocks(blocks, parts(i)[0].at[0], [parts(i)[6]])
            for j in (2, 1, 3):
                over_y(i, j).start()

    def step_y(i):
        _, _, rows = sizes(i)

        @pl.when(c == 0)
        def _():
            for j in (1, 2, 3):
                over_y(i, j).wait_recv()
            own, came, result = own_piece(i, y), parts(i)[7], parts(i)[8]

            def step(b, carry):
                total = own[b].astype(jnp.float32)
                for j in range(RING - 1):
                    total = total + came[j, b].astype(jnp.float32)
                result[b] = total.astype(result.dtype)
                return carry

            lax.fori_loop(0, rows, step, 0)
            for j in (2, 1, 3):
                share_y(i, j, y).start()
            keep(i).start()

    def step_hand(i):
        @pl.when(c == 0)
        def _():
            keep(i).wait()
            for j in (1, 2, 3):
                share_y(i, j, (y + RING - j) % RING).wait_recv()
            hand(i).start()

    def step_last(i):
        @pl.when(c == 1)
        def _():
            hand(i).wait_recv()

    steps = [step_cores, step_far, step_near, step_x, step_y, step_hand, step_last]
    for tick in range(count + len(steps) - 1):
        for i in range(count):
            at = tick - i
            if 0 <= at < len(steps):
                steps[at](i)
    for i in range(count):
        for k in range(RING):
            swap(i, k).wait_send()
        for copy in (far_up, far_down, near_up, near_down):
            copy(i).wait_send()

        @pl.when(c == 1)
        def _():
            over_x(i).wait_send()

        @pl.when(c == 0)
        def _():
            for j in (1, 2, 3):
                over_y(i, j).wait_send()
                share_y(i, j, y).wait_send()
            hand(i).wait_send()


def sum_gradients(grads):
    count = len(grads)
    scratch = []
    for grad in grads:
        _, blocks, rows, width = grad.shape
        half, piece = blocks // 2, piece_rows(blocks)
        for lead in (
            (RING, blocks),
            (RING, blocks),
            (half,),
            (blocks - half,),
            (blocks,),
            (blocks,),
            (blocks,),
            (RING - 1, piece),
            (piece,),
        ):
            scratch.append(pltpu.VMEM(lead + (rows, width), grad.dtype))
    return pl.pallas_call(
        functools.partial(sum_kernel, count),
        out_shape=[
            jax.ShapeDtypeStruct((RING, piece_rows(g.shape[1])) + g.shape[2:], g.dtype)
            for g in grads
        ],
        in_specs=[pl.BlockSpec(memory_space=pl.ANY)] * count,
        out_specs=[pl.BlockSpec(memory_space=pl.ANY)] * count,
        scratch_shapes=scratch
        + [
            pltpu.SemaphoreType.DMA((count, 16)),
            pltpu.SemaphoreType.DMA((count, 16)),
            pltpu.SemaphoreType.DMA((count, 5)),
        ],
        compiler_params=pltpu.CompilerParams(
            collective_id=1, has_side_effects=True, vmem_limit_bytes=60 * 1024 * 1024
        ),
        name="sum_gradients",
    )(*grads)


def assemble(pieces, blocks):
    starts = [i * blocks // RING for i in range(RING + 1)]
    joined = jnp.concatenate(
        [pieces[i, : starts[i + 1] - starts[i]] for i in range(RING)], 0
    ).astype(jnp.float32)
    return joined.reshape(-1, pieces.shape[-1])


def lane_head(shape):
    return lax.broadcasted_iota(jnp.int32, shape, len(shape) - 1) // HEAD


def one_head(matrix, head):
    return jnp.where(lane_head(matrix.shape) == head, matrix, jnp.zeros_like(matrix))


def over_lanes(left, right):
    return lax.dot_general(left, right, (((1,), (1,)), ((), ())), preferred_element_type=jnp.float32)


def over_rows(left, right):
    return lax.dot_general(left, right, (((0,), (0,)), ((), ())), preferred_element_type=jnp.float32)


def plain(left, right):
    return jnp.dot(left, right, preferred_element_type=jnp.float32)


def soft_columns(key_rows, queries, first_query, length):
    scores = over_lanes(key_rows, queries) * HEAD ** (-0.5)
    key_pos = lax.broadcasted_iota(jnp.int32, scores.shape, 0)
    query_pos = first_query + lax.broadcasted_iota(jnp.int32, scores.shape, 1)
    scores = jnp.where((key_pos <= query_pos) & (key_pos < length), scores, MASKED)
    exponent = jnp.exp(scores - jnp.max(scores, 0, keepdims=True))
    return exponent * (1.0 / jnp.sum(exponent, 0, keepdims=True))


def peers(count):
    member = lax.axis_index("group")
    ahead = [(member + j) % count for j in range(1, count)]
    behind = [(member + count - j) % count for j in range(1, count)]
    return (member, ahead, behind)


def attend_kernel(
    lengths, pack, last_kv, last_q, mixed, last_mixed, kept, kept_last,
    held, held_last, staged, send, recv, send_last, recv_last, send_back, recv_back, local,
):
    count, micros, _, rows, lanes = pack.shape
    member, ahead, behind = peers(count)
    greet([{"group": peer} for peer in ahead])

    def out(m, j):
        return remote(
            pack.at[ahead[j], m], held.at[member, m], send.at[m, j], recv.at[m, j], {"group": ahead[j]}
        )

    def out_last(m, j):
        return remote(
            last_kv.at[m],
            held_last.at[member, m],
            send_last.at[m, j],
            recv_last.at[m, j],
            {"group": ahead[j]},
        )

    def back(m, j):
        return remote(
            staged.at[ahead[j], m],
            mixed.at[member, m],
            send_back.at[m, j],
            recv_back.at[m, j],
            {"group": ahead[j]},
        )

    def own(m):
        return (
            pltpu.make_async_copy(pack.at[member, m], held.at[member, m], local.at[m, 0]),
            pltpu.make_async_copy(last_kv.at[m], held_last.at[member, m], local.at[m, 1]),
        )

    def own_back(m):
        return pltpu.make_async_copy(staged.at[member, m], mixed.at[member, m], local.at[m, 2])

    def keep():
        return (
            pltpu.make_async_copy(held, kept, local.at[0, 3]),
            pltpu.make_async_copy(held_last, kept_last, local.at[1, 3]),
        )

    peer_range = range(count - 1)
    for m in range(micros):
        for j in peer_range:
            out(m, j).start()
            out_last(m, j).start()
        for copy in own(m):
            copy.start()

    def micro(m, carry):
        for copy in own(m):
            copy.wait()
        for j in peer_range:
            out(m, j).wait_recv()
            out_last(m, j).wait_recv()
        length = lengths[m]
        wide = 2
        for block in range(count // wide):
            reach = wide * (block + 1)
            queries = held[wide * block : reach, m, 0].reshape(wide * rows, lanes)
            key_rows = held[0:reach, m, 1].reshape(reach * rows, lanes)
            values = held[0:reach, m, 2].reshape(reach * rows, lanes)

            def head_step(head, total):
                probs = soft_columns(
                    key_rows, one_head(queries, head), wide * block * rows, length
                ).astype(jnp.bfloat16)
                return total + over_rows(one_head(values, head), probs)

            total = lax.fori_loop(0, 2, head_step, jnp.zeros((lanes, wide * rows), jnp.float32))
            staged[wide * block : reach, m] = (
                total.T.astype(jnp.bfloat16).reshape(wide, rows, lanes)
            )
        for j in peer_range:
            back(m, j).start()
        own_back(m).start()
        both = held_last[:, m].reshape(count * rows, lanes)
        probs = soft_columns(both, last_q[m], member * rows, length).astype(jnp.bfloat16)
        last_mixed[m] = over_rows(both, probs).T.astype(jnp.bfloat16)
        return carry

    lax.fori_loop(0, micros, micro, 0)
    for copy in keep():
        copy.start()
    for m in range(micros):
        own_back(m).wait()
        for j in peer_range:
            out(m, j).wait_send()
            out_last(m, j).wait_send()
            back(m, j).wait()
    for copy in keep():
        copy.wait()


def attend(lengths, pack, last_kv, last_q):
    count, micros, _, rows, lanes = pack.shape
    bf16 = jnp.bfloat16
    vmem, hbm = pl.BlockSpec(memory_space=pltpu.VMEM), pl.BlockSpec(memory_space=pl.ANY)
    dma = pltpu.SemaphoreType.DMA
    return pl.pallas_call(
        attend_kernel,
        out_shape=[
            jax.ShapeDtypeStruct((count, micros, rows, lanes), bf16),
            jax.ShapeDtypeStruct((micros, rows, lanes), bf16),
            jax.ShapeDtypeStruct(pack.shape, bf16),
            jax.ShapeDtypeStruct((count, micros, rows, lanes), bf16),
        ],
        in_specs=[pl.BlockSpec(memory_space=pltpu.SMEM), hbm, vmem, vmem],
        out_specs=[hbm, vmem, hbm, hbm],
        scratch_shapes=[
            pltpu.VMEM(pack.shape, bf16),
            pltpu.VMEM((count, micros, rows, lanes), bf16),
            pltpu.VMEM((count, micros, rows, lanes), bf16),
        ]
        + [dma((micros, count - 1))] * 6
        + [dma((micros, 4))],
        compiler_params=pltpu.CompilerParams(
            collective_id=2, has_side_effects=True, vmem_limit_bytes=48 * 1024 * 1024
        ),
        name="attend",
    )(lengths, pack, last_kv, last_q)


def attend_back_kernel(
    lengths, held, held_last, last_q, grad_pack, last_grad, grads, last_key_grad, last_query_grad,
    came, staged, staged_last, parts_last, key_total, value_total,
    send, recv, send_back, recv_back, send_last, recv_last, local,
):
    count, micros, _, rows, lanes = held.shape
    member, ahead, behind = peers(count)
    greet([{"group": peer} for peer in ahead])
    scale = HEAD ** (-0.5)

    def out(m, j):
        return remote(
            grad_pack.at[ahead[j], m],
            came.at[member, m],
            send.at[m, j],
            recv.at[m, j],
            {"group": ahead[j]},
        )

    def back(m, j):
        return remote(
            staged.at[ahead[j], m],
            grads.at[member, m],
            send_back.at[m, j],
            recv_back.at[m, j],
            {"group": ahead[j]},
        )

    def back_last(m, j):
        return remote(
            staged_last.at[ahead[j], m],
            parts_last.at[member, m],
            send_last.at[m, j],
            recv_last.at[m, j],
            {"group": ahead[j]},
        )

    def own(m):
        return pltpu.make_async_copy(grad_pack.at[member, m], came.at[member, m], local.at[m, 0])

    def own_back(m):
        return (
            pltpu.make_async_copy(staged.at[member, m], grads.at[member, m], local.at[m, 1]),
            pltpu.make_async_copy(
                staged_last.at[member, m], parts_last.at[member, m], local.at[m, 2]
            ),
        )

    peer_range = range(count - 1)
    for m in range(micros):
        for j in peer_range:
            out(m, j).start()
        own(m).start()

    def micro(m, carry):
        length = lengths[m]
        both = held_last[:, m].reshape(count * rows, lanes)
        probs = soft_columns(both, last_q[m], member * rows, length)
        grad_probs = over_lanes(both, last_grad[m])
        inner = jnp.sum(probs * grad_probs, 0, keepdims=True)
        grad_scores = (probs * (grad_probs - inner)).astype(jnp.bfloat16)
        last_query_grad[m] = (scale * over_rows(both, grad_scores)).T.astype(jnp.bfloat16)
        both_grad = scale * plain(grad_scores, last_q[m]) + plain(
            probs.astype(jnp.bfloat16), last_grad[m]
        )
        staged_last[:, m] = both_grad.astype(jnp.bfloat16).reshape(count, rows, lanes)
        for j in peer_range:
            back_last(m, j).start()
        own(m).wait()
        for j in peer_range:
            out(m, j).wait_recv()
        key_total[...] = jnp.zeros_like(key_total)
        value_total[...] = jnp.zeros_like(value_total)
        wide = 2
        for block in range(count // wide):
            reach = wide * (block + 1)
            queries = held[wide * block : reach, m, 0].reshape(wide * rows, lanes)
            grad_out = came[wide * block : reach, m].reshape(wide * rows, lanes)
            key_rows = held[0:reach, m, 1].reshape(reach * rows, lanes)
            values = held[0:reach, m, 2].reshape(reach * rows, lanes)

            def head_step(head, total):
                head_queries, head_grad = one_head(queries, head), one_head(grad_out, head)
                probs = soft_columns(key_rows, head_queries, wide * block * rows, length)
                grad_probs = over_lanes(values, head_grad)
                inner = jnp.sum(probs * grad_probs, 0, keepdims=True)
                grad_scores = (probs * (grad_probs - inner)).astype(jnp.bfloat16)
                value_total[0 : reach * rows] += plain(probs.astype(jnp.bfloat16), head_grad)
                key_total[0 : reach * rows] += plain(grad_scores, head_queries)
                return total + over_rows(one_head(key_rows, head), grad_scores)

            total = lax.fori_loop(0, 2, head_step, jnp.zeros((lanes, wide * rows), jnp.float32))
            staged[wide * block : reach, m, 0] = (
                (scale * total).T.astype(jnp.bfloat16).reshape(wide, rows, lanes)
            )
        staged[:, m, 1] = (scale * key_total[...]).astype(jnp.bfloat16).reshape(count, rows, lanes)
        staged[:, m, 2] = value_total[...].astype(jnp.bfloat16).reshape(count, rows, lanes)
        for j in peer_range:
            back(m, j).start()
        for copy in own_back(m):
            copy.start()
        return carry

    lax.fori_loop(0, micros, micro, 0)
    for m in range(micros):
        for copy in own_back(m):
            copy.wait()
        for j in peer_range:
            back_last(m, j).wait_recv()
        last_key_grad[m] = jnp.sum(parts_last[:, m].astype(jnp.float32), 0).astype(jnp.bfloat16)
    for m in range(micros):
        for j in peer_range:
            out(m, j).wait_send()
            back_last(m, j).wait_send()
            back(m, j).wait()


def attend_back(lengths, held, held_last, last_q, grad_pack, last_grad):
    count, micros, _, rows, lanes = held.shape
    bf16 = jnp.bfloat16
    vmem, hbm = pl.BlockSpec(memory_space=pltpu.VMEM), pl.BlockSpec(memory_space=pl.ANY)
    dma = pltpu.SemaphoreType.DMA
    return pl.pallas_call(
        attend_back_kernel,
        out_shape=[
            jax.ShapeDtypeStruct(held.shape, bf16),
            jax.ShapeDtypeStruct((micros, rows, lanes), bf16),
            jax.ShapeDtypeStruct((micros, rows, lanes), bf16),
        ],
        in_specs=[pl.BlockSpec(memory_space=pltpu.SMEM), vmem, vmem, vmem, hbm, vmem],
        out_specs=[hbm, vmem, vmem],
        scratch_shapes=[
            pltpu.VMEM((count, micros, rows, lanes), bf16),
            pltpu.VMEM(held.shape, bf16),
            pltpu.VMEM((count, micros, rows, lanes), bf16),
            pltpu.VMEM((count, micros, rows, lanes), bf16),
            pltpu.VMEM((count * rows, lanes), jnp.float32),
            pltpu.VMEM((count * rows, lanes), jnp.float32),
        ]
        + [dma((micros, count - 1))] * 6
        + [dma((micros, 3))],
        compiler_params=pltpu.CompilerParams(
            collective_id=3, has_side_effects=True, vmem_limit_bytes=48 * 1024 * 1024
        ),
        name="attend_back",
    )(lengths, held, held_last, last_q, grad_pack, last_grad)


def norm_rows(inputs, gain_row, bias_row):
    average = jnp.mean(inputs, -1, keepdims=True)
    centered = inputs - average
    variance = jnp.mean(centered * centered, -1, keepdims=True)
    return centered * lax.rsqrt(variance + EPSILON) * gain_row + bias_row


def gelu_tanh(inputs):
    return jax.nn.gelu(inputs, approximate=True)


def by_heads(matrix, micros, rows, count):
    return matrix.reshape(micros, rows, count, LANES).transpose(2, 0, 1, 3)


def by_rows(blocks):
    count, micros, rows, lanes = blocks.shape
    return blocks.transpose(1, 2, 0, 3).reshape(micros * rows, count * lanes)


def in_blocks(matrix):
    return matrix.reshape(matrix.shape[0] // 8, 8, matrix.shape[1])


def body(
    block_input, out_grad, w_qkv, w_proj, w_up, w_down, vectors, b_up, seq_lengths, slot_of_seq
):
    section = lax.axis_index("pipe")
    replica = lax.axis_index("rep")
    member = lax.axis_index("group")
    rep_count = lax.axis_size("rep")
    count = lax.axis_size("group")
    micros, rows, width = block_input.shape[0], block_input.shape[2], block_input.shape[3]
    wide = count * LANES
    slot_ids = jnp.arange(seq_lengths.shape[0], dtype=jnp.int32)
    slot_len = jnp.sum(
        seq_lengths[:, None] * (slot_of_seq[:, None] == slot_ids[None, :]).astype(jnp.int32), axis=0
    )
    mine = jnp.arange(micros, dtype=jnp.int32) * rep_count + replica
    lengths = jnp.sum(
        slot_len[None, :] * (slot_ids[None, :] == mine[:, None]).astype(jnp.int32), axis=1
    )
    query_pos = member * rows + jnp.arange(rows, dtype=jnp.int32)
    valid = (query_pos[None, :] < lengths[:, None]).astype(jnp.float32)[:, :, None]
    cotangent = (out_grad[:, 0].astype(jnp.float32) * valid).reshape(micros * rows, width)

    bias_rows = b_up.shape[1] // vectors.shape[2]
    small = jnp.concatenate(
        [
            vectors[0],
            b_up[0].reshape(bias_rows, -1),
            jnp.zeros((8 - bias_rows, vectors.shape[2]), vectors.dtype),
        ],
        0,
    )
    full = gather_weights(
        [
            in_blocks(small),
            in_blocks(w_qkv[0]),
            in_blocks(w_proj[0]),
            in_blocks(w_up[0]),
            in_blocks(w_down[0]),
        ]
    )
    vector_rows = full[0][:, 0].transpose(1, 0, 2).reshape(8, width).astype(jnp.float32)
    up_bias = full[0][:, 1, :bias_rows].reshape(-1).astype(jnp.float32)
    qkv_weight, proj_weight, up_weight, down_weight = (
        array.reshape(-1, array.shape[-1]) for array in full[1:]
    )
    qkv_bias = jnp.concatenate([vector_rows[2], jnp.zeros_like(vector_rows[2]), vector_rows[3]])

    def pad_last(matrix, before):
        block = matrix.reshape(micros, rows, HEAD)
        return jnp.pad(block, ((0, 0), (0, 0), (before, LANES - HEAD - before)))

    def forward(inputs):
        normed = norm_rows(inputs, vector_rows[0], vector_rows[1]).astype(jnp.bfloat16)
        qkv = (plain(normed, qkv_weight) + qkv_bias).astype(jnp.bfloat16)
        thirds = [qkv[:, i * width : (i + 1) * width] for i in range(3)]
        pack = jnp.stack([by_heads(t[:, :wide], micros, rows, count) for t in thirds], 2)
        last_kv = jnp.concatenate([thirds[1][:, wide:], thirds[2][:, wide:]], 1).reshape(
            micros, rows, LANES
        )
        last_q = pad_last(thirds[0][:, wide:], 0)
        mixed, last_mixed, held, held_last = attend(lengths, pack, last_kv, last_q)
        attn_mixed = jnp.concatenate(
            [by_rows(mixed), last_mixed[:, :, HEAD:].reshape(micros * rows, HEAD)], 1
        )
        hidden = inputs + plain(attn_mixed, proj_weight) + vector_rows[4]
        normed_two = norm_rows(hidden, vector_rows[5], vector_rows[6]).astype(jnp.bfloat16)
        pre_act = plain(normed_two, up_weight) + up_bias
        activated = gelu_tanh(pre_act).astype(jnp.bfloat16)
        output = hidden + plain(activated, down_weight) + vector_rows[7]
        return (output, (inputs, held, held_last, last_q, attn_mixed, hidden, pre_act, activated))

    def backward(grad_output, saved):
        inputs, held, held_last, last_q, attn_mixed, hidden, pre_act, activated = saved
        grad_two = grad_output.astype(jnp.bfloat16)
        grad_act = plain(grad_two, down_weight.T)
        grad_pre = jax.vjp(gelu_tanh, pre_act)[1](grad_act)[0].astype(jnp.bfloat16)
        normed_two, pull_two = jax.vjp(norm_rows, hidden, vector_rows[5], vector_rows[6])
        from_norm, gain_two, shift_two = pull_two(plain(grad_pre, up_weight.T))
        grad_hidden = grad_output + from_norm
        grad_one = grad_hidden.astype(jnp.bfloat16)
        grad_mixed = plain(grad_one, proj_weight.T).astype(jnp.bfloat16)
        grads, last_key_grad, last_query_grad = attend_back(
            lengths,
            held,
            held_last,
            last_q,
            by_heads(grad_mixed[:, :wide], micros, rows, count),
            pad_last(grad_mixed[:, wide:], HEAD),
        )

        def last(block, first):
            return block[:, :, first : first + HEAD].reshape(micros * rows, HEAD)

        grad_qkv = jnp.concatenate(
            [
                by_rows(grads[:, :, 0]),
                last(last_query_grad, 0),
                by_rows(grads[:, :, 1]),
                last(last_key_grad, 0),
                by_rows(grads[:, :, 2]),
                last(last_key_grad, HEAD),
            ],
            1,
        )
        normed, pull = jax.vjp(norm_rows, inputs, vector_rows[0], vector_rows[1])
        from_norm, gain, shift = pull(plain(grad_qkv, qkv_weight.T))
        grad_in = grad_hidden + from_norm

        def weight_grads():
            def outer(left, right):
                return over_rows(left, right).astype(jnp.bfloat16)

            sums = jnp.sum(grad_qkv.astype(jnp.float32), 0)
            rows_of_vectors = jnp.stack(
                [
                    gain,
                    shift,
                    sums[:width],
                    sums[2 * width :],
                    jnp.sum(grad_one.astype(jnp.float32), 0),
                    gain_two,
                    shift_two,
                    jnp.sum(grad_two.astype(jnp.float32), 0),
                ]
            )
            return (
                outer(normed.astype(jnp.bfloat16), grad_qkv),
                outer(attn_mixed, grad_one),
                outer(normed_two.astype(jnp.bfloat16), grad_pre),
                outer(activated, grad_two),
                rows_of_vectors,
                jnp.sum(grad_pre.astype(jnp.float32), 0),
            )

        return (grad_in, weight_grads)

    first_in = block_input[:, 0].reshape(micros * rows, width).astype(jnp.float32)
    first_out, _ = forward(first_in)
    arrived = lax.ppermute(first_out.astype(jnp.bfloat16), "pipe", [(0, 1)])
    output, saved = forward(jnp.where(section == 0, first_in, arrived.astype(jnp.float32)))
    last_grad, _ = backward(cotangent, saved)
    arrived = lax.ppermute(last_grad.astype(jnp.bfloat16), "pipe", [(1, 0)])
    grad_in, weight_grads = backward(
        jnp.where(section == 1, cotangent, arrived.astype(jnp.float32)), saved
    )
    grad_qkv, grad_proj, grad_up, grad_down, grad_vectors, grad_bias = weight_grads()

    def shards(matrix):
        return matrix.reshape(count, -1, 8, matrix.shape[-1])

    small_grads = jnp.concatenate(
        [
            grad_vectors.reshape(8, count, -1).transpose(1, 0, 2),
            grad_bias.reshape(count, bias_rows, -1),
            jnp.zeros((count, 24 - bias_rows, width // count), jnp.float32),
        ],
        1,
    ).reshape(count, RING, 8, width // count)
    sums = sum_gradients(
        [shards(grad_down), shards(grad_up), shards(grad_qkv), small_grads, shards(grad_proj)]
    )
    totals = [
        assemble(total, grad.shape[0] // count // 8)
        for total, grad in zip(
            (sums[2], sums[4], sums[1], sums[0]), (grad_qkv, grad_proj, grad_up, grad_down)
        )
    ]
    small_total = sums[3].reshape(RING * 8, -1)
    edges = jnp.where(section == 0, grad_in, output).reshape(1, micros, 1, rows, width)
    return (
        edges,
        totals[0][None],
        totals[1][None],
        totals[2][None],
        totals[3][None],
        small_total[None, :8],
        small_total[8 : 8 + bias_rows].reshape(1, -1),
    )


def solution(mesh):
    in_specs = (
        P(None, "rep", "group", None),
        P(None, "rep", "group", None),
        P("pipe", "group", None),
        P("pipe", "group", None),
        P("pipe", "group", None),
        P("pipe", "group", None),
        P("pipe", None, "group"),
        P("pipe", "group"),
        P(),
        P(),
    )
    out_specs = (
        P("pipe", None, "rep", "group", None),
        P("pipe", "group", None),
        P("pipe", "group", None),
        P("pipe", "group", None),
        P("pipe", "group", None),
        P("pipe", None, "group"),
        P("pipe", "group"),
    )
    return jax.shard_map(body, mesh=mesh, in_specs=in_specs, out_specs=out_specs, check_vma=False)
```

```python
import functools
import jax
import jax.numpy as jnp
from jax import lax
from jax.experimental import pallas as pl
from jax.experimental.pallas import tpu as pltpu
from jax.sharding import PartitionSpec as P

HEAD = 64
LANES = 128
EPSILON = 1e-05
MASKED = -1e30
MESH = pl.DeviceIdType.MESH
RING = 4


def remote(src, dst, send_sem, recv_sem, device):
    return pltpu.make_async_remote_copy(
        src_ref=src,
        dst_ref=dst,
        send_sem=send_sem,
        recv_sem=recv_sem,
        device_id=device,
        device_id_type=MESH,
    )


def greet(devices):
    barrier = pltpu.get_barrier_semaphore()
    for device in devices:
        pl.semaphore_signal(barrier, inc=1, device_id=device, device_id_type=MESH)
    pl.semaphore_wait(barrier, len(devices))


def place():
    member, replica = lax.axis_index("group"), lax.axis_index("rep")
    return (member // 2, member % 2, replica // 2, replica % 2)


class Links:
    def __init__(self, send, recv):
        self.send, self.recv, self.used = send, recv, 0

    def channel(self, device):
        self.used += 1
        return Channel(self.send.at[self.used - 1], self.recv.at[self.used - 1], device)


class Channel:
    def __init__(self, send, recv, device):
        self.send_sem, self.recv_sem, self.device = send, recv, device

    def copy(self, src, dst):
        return remote(src, dst, self.send_sem, self.recv_sem, self.device)

    def send(self, src, dst):
        self.copy(src, dst).start()

    def sent(self, src):
        self.copy(src, src).wait_send()

    def came(self, dst):
        self.copy(dst, dst).wait_recv()


def near_devices():
    z, x, y, c = place()
    return {
        "above": {"group": 2 * ((z + 1) % RING) + x},
        "below": {"group": 2 * ((z + 3) % RING) + x},
        "partner": {"group": 2 * z + 1 - x},
        "sibling": {"rep": 2 * y + 1 - c},
        "next": {"rep": 2 * ((y + 1) % RING) + c},
        "last": {"rep": 2 * ((y + 3) % RING) + c},
    }


def gather_job(links, shard, full, first, size, spread):
    z, x, y, c = place()
    near = near_devices()
    xc = (x + c) % 2
    me = 2 * z + x
    base, above, below, across = (2 * ((z + k) % RING) + xc for k in (0, 1, 3, 2))
    piece = size // RING if spread else size
    low = piece - piece // 2
    finals = []

    def region(slot, owner, part=""):
        start = first + owner * piece if spread else first
        if part == "low":
            return full.at[slot, pl.ds(start, low)]
        if part == "high":
            return full.at[slot, pl.ds(start + low, piece - low)]
        return full.at[slot, pl.ds(start, piece)]

    def on_core(core, action):
        pl.when(c == core)(action)

    def always(action):
        action()

    def relay(channel, ref, run):
        run(lambda: channel.send(ref, ref))
        finals.append(lambda: run(lambda: channel.sent(ref)))

    def hand(slot, owner, run, part=""):
        channel = links.channel(near["sibling"])
        relay(channel, region(slot, owner, part), run)
        other = region(slot + 1 - 2 * xc, owner, part)
        get = (lambda action: on_core(0, action)) if run is not always else always
        finals.append(lambda: get(lambda: channel.came(other)))

    across_x = links.channel(near["partner"])
    up, down = links.channel(near["above"]), links.channel(near["below"])
    far_up, far_down = links.channel(near["above"]), links.channel(near["below"])
    own = shard.at[pl.ds(first + y * piece if spread else first, piece)]
    second = lambda action: on_core(1, action)

    def first_core():
        up.send(own, region(base, y))
        down.send(own, region(base, y))

    on_core(0, first_core)
    on_core(1, lambda: across_x.send(own, region(me, y)))
    finals.append(lambda: on_core(1, lambda: across_x.sent(own)))
    finals.append(lambda: up.sent(own))
    finals.append(lambda: down.sent(own))
    yield

    rings = []

    def pass_on(slot, run):
        if spread:
            forth, back = links.channel(near["next"]), links.channel(near["last"])
            relay(forth, region(slot, y), run)
            relay(back, region(slot, y), run)
            rings.append((slot, run, forth, back))
        hand(slot, y, run)

    def second_core():
        across_x.came(region(base, y))
        up.send(region(base, y), region(base, y))
        down.send(region(base, y), region(base, y))

    on_core(1, second_core)
    pass_on(base, second)
    yield

    up.came(region(below, y))
    relay(far_up, region(below, y, "low"), always)
    pass_on(below, always)
    down.came(region(above, y))
    if piece > low:
        relay(far_down, region(above, y, "high"), always)
    pass_on(above, always)
    yield

    far_up.came(region(across, y, "low"))
    if piece > low:
        far_down.came(region(across, y, "high"))
    pass_on(across, always)
    yield

    if spread:
        ends = []
        for slot, run, forth, back in rings:
            far_forth, far_back = links.channel(near["next"]), links.channel(near["last"])
            behind, ahead = (y + 3) % RING, (y + 1) % RING
            run(lambda: forth.came(region(slot, behind)))
            relay(far_forth, region(slot, behind, "low"), run)
            hand(slot, behind, run)
            run(lambda: back.came(region(slot, ahead)))
            if piece > low:
                relay(far_back, region(slot, ahead, "high"), run)
            hand(slot, ahead, run)
            ends.append((slot, run, far_forth, far_back))
        yield
        for slot, run, far_forth, far_back in ends:
            far = (y + 2) % RING
            run(lambda: far_forth.came(region(slot, far, "low")))
            if piece > low:
                run(lambda: far_back.came(region(slot, far, "high")))
            hand(slot, far, run)
        yield
    for action in finals:
        action()


class Pump:
    def __init__(self, jobs):
        self.jobs = list(jobs)

    def __call__(self):
        alive = []
        for job in self.jobs:
            try:
                next(job)
                alive.append(job)
            except StopIteration:
                pass
        self.jobs = alive

    def drain(self):
        while self.jobs:
            self()


MAX_LINKS = 160


def gather_jobs(links, local, plan, ins, outs):
    member = lax.axis_index("group")

    def own(i):
        copy = pltpu.make_async_copy(ins[i], outs[i].at[member], local.at[i])
        copy.start()
        yield
        copy.wait()

    jobs = [gather_job(links, ins[i], outs[i], *rest) for i, *rest in plan]
    return Pump(jobs + [own(i) for i in range(len(ins))])


def gather_kernel(plan, count, *refs):
    ins, outs = refs[:count], refs[count : 2 * count]
    send, recv, local = refs[2 * count :]
    greet(list(near_devices().values()))
    gather_jobs(Links(send, recv), local, plan, ins, outs).drain()


def gathered_shapes(shards):
    return [jax.ShapeDtypeStruct((8,) + s.shape, s.dtype) for s in shards]


def gather_sems(count):
    dma = pltpu.SemaphoreType.DMA
    return [dma((MAX_LINKS,)), dma((MAX_LINKS,)), dma((count,))]


def gather_weights(shards, plan):
    count = len(shards)
    return pl.pallas_call(
        functools.partial(gather_kernel, plan, count),
        out_shape=gathered_shapes(shards),
        in_specs=[pl.BlockSpec(memory_space=pl.ANY)] * count,
        out_specs=[pl.BlockSpec(memory_space=pl.ANY)] * count,
        scratch_shapes=gather_sems(count),
        compiler_params=pltpu.CompilerParams(collective_id=0, has_side_effects=True),
        name="gather_weights",
    )(*shards)


def piece_rows(blocks):
    starts = [i * blocks // RING for i in range(RING + 1)]
    return max(starts[i + 1] - starts[i] for i in range(RING))


def add_blocks(count, dst, terms):
    def step(b, carry):
        total = dst[b].astype(jnp.float32)
        for term in terms:
            total = total + term[b].astype(jnp.float32)
        dst[b] = total.astype(dst.dtype)
        return carry

    lax.fori_loop(0, count, step, 0)


PER_ARRAY = 9


def sum_devices():
    z, x, y, c = place()
    near = near_devices()
    partner = {"group": 2 * z + 1 - x, "rep": 2 * y + 1 - c}
    others = [{"rep": 2 * ((y + j) % RING) + c} for j in range(1, RING)]
    return (near["above"], near["below"], near["sibling"], partner, others)


def sum_job(ins, outs, buffers, send, recv, local):
    count = len(ins)
    z, x, y, c = place()
    xc = (x + c) % 2
    to_above, to_below, sibling, partner, others = sum_devices()

    def parts(i):
        return buffers[PER_ARRAY * i : PER_ARRAY * (i + 1)]

    def swap(i, k):
        own, came = ins[i].at[2 * ((z + k) % RING) + 1 - xc], parts(i)[1].at[k]
        return remote(own, came, send.at[i, k], recv.at[i, k], sibling)

    def load(i, k):
        return pltpu.make_async_copy(
            ins[i].at[2 * ((z + k) % RING) + xc], parts(i)[0].at[k], local.at[i, k]
        )

    def sizes(i):
        blocks = ins[i].shape[1]
        return (blocks, blocks // 2, piece_rows(blocks))

    def far_up(i):
        blocks, half, _ = sizes(i)
        src = parts(i)[0].at[2, pl.ds(0, half)]
        return remote(src, parts(i)[2], send.at[i, 4], recv.at[i, 4], to_above)

    def far_down(i):
        blocks, half, _ = sizes(i)
        src = parts(i)[0].at[2, pl.ds(half, blocks - half)]
        return remote(src, parts(i)[3], send.at[i, 5], recv.at[i, 5], to_below)

    def near_up(i):
        return remote(parts(i)[0].at[1], parts(i)[4], send.at[i, 6], recv.at[i, 6], to_above)

    def near_down(i):
        return remote(parts(i)[0].at[3], parts(i)[5], send.at[i, 7], recv.at[i, 7], to_below)

    def over_x(i):
        return remote(parts(i)[0].at[0], parts(i)[6], send.at[i, 8], recv.at[i, 8], partner)

    def own_piece(i, owner):
        blocks, _, rows = sizes(i)
        return parts(i)[0].at[0, pl.ds((owner * blocks) // RING, rows)]

    def over_y(i, j):
        src = own_piece(i, (y + j) % RING)
        dst = parts(i)[7].at[j - 1]
        return remote(src, dst, send.at[i, 8 + j], recv.at[i, 8 + j], others[j - 1])

    def share_y(i, j, slot):
        dst = outs[i].at[slot]
        return remote(parts(i)[8], dst, send.at[i, 11 + j], recv.at[i, 11 + j], others[j - 1])

    def keep(i):
        return pltpu.make_async_copy(parts(i)[8], outs[i].at[y], local.at[i, 4])

    def hand(i):
        return remote(outs[i], outs[i], send.at[i, 15], recv.at[i, 15], sibling)

    for i in range(count):
        for k in (2, 1, 3, 0):
            swap(i, k).start()
            load(i, k).start()
    yield

    def step_cores(i):
        blocks, half, _ = sizes(i)
        total, came = parts(i)[0], parts(i)[1]
        for k in (2, 1, 3, 0):
            load(i, k).wait()
            swap(i, k).wait_recv()
            add_blocks(blocks, total.at[k], [came.at[k]])
            if k == 2:
                far_up(i).start()
                far_down(i).start()

    def step_far(i):
        blocks, half, _ = sizes(i)
        total = parts(i)[0]
        far_up(i).wait_recv()
        add_blocks(half, total.at[1, pl.ds(0, half)], [parts(i)[2]])
        near_up(i).start()
        far_down(i).wait_recv()
        add_blocks(blocks - half, total.at[3, pl.ds(half, blocks - half)], [parts(i)[3]])
        near_down(i).start()

    def step_near(i):
        blocks, half, _ = sizes(i)
        near_up(i).wait_recv()
        near_down(i).wait_recv()
        add_blocks(blocks, parts(i)[0].at[0], [parts(i)[4], parts(i)[5]])

        @pl.when(c == 1)
        def _():
            over_x(i).start()

    def step_x(i):
        blocks, half, _ = sizes(i)

        @pl.when(c == 0)
        def _():
            over_x(i).wait_recv()
            add_blocks(blocks, parts(i)[0].at[0], [parts(i)[6]])
            for j in (2, 1, 3):
                over_y(i, j).start()

    def step_y(i):
        _, _, rows = sizes(i)

        @pl.when(c == 0)
        def _():
            for j in (1, 2, 3):
                over_y(i, j).wait_recv()
            own, came, result = own_piece(i, y), parts(i)[7], parts(i)[8]

            def step(b, carry):
                total = own[b].astype(jnp.float32)
                for j in range(RING - 1):
                    total = total + came[j, b].astype(jnp.float32)
                result[b] = total.astype(result.dtype)
                return carry

            lax.fori_loop(0, rows, step, 0)
            for j in (2, 1, 3):
                share_y(i, j, y).start()
            keep(i).start()

    def step_hand(i):
        @pl.when(c == 0)
        def _():
            keep(i).wait()
            for j in (1, 2, 3):
                share_y(i, j, (y + RING - j) % RING).wait_recv()
            hand(i).start()

    def step_last(i):
        @pl.when(c == 1)
        def _():
            hand(i).wait_recv()

    steps = [step_cores, step_far, step_near, step_x, step_y, step_hand, step_last]
    for tick in range(count + len(steps) - 1):
        for i in range(count):
            at = tick - i
            if 0 <= at < len(steps):
                steps[at](i)
        yield
    for i in range(count):
        for k in range(RING):
            swap(i, k).wait_send()
        for copy in (far_up, far_down, near_up, near_down):
            copy(i).wait_send()

        @pl.when(c == 1)
        def _():
            over_x(i).wait_send()

        @pl.when(c == 0)
        def _():
            for j in (1, 2, 3):
                over_y(i, j).wait_send()
                share_y(i, j, y).wait_send()
            hand(i).wait_send()


def sum_kernel(count, *refs):
    above, below, sibling, partner, others = sum_devices()
    greet([above, below, sibling, partner] + others)
    split = (2 + PER_ARRAY) * count
    Pump(
        [sum_job(refs[:count], refs[count : 2 * count], refs[2 * count : split], *refs[split:])]
    ).drain()


def sum_scratch(grads):
    scratch = []
    for grad in grads:
        _, blocks, rows, width = grad.shape
        half, piece = blocks // 2, piece_rows(blocks)
        for lead in (
            (RING, blocks),
            (RING, blocks),
            (half,),
            (blocks - half,),
            (blocks,),
            (blocks,),
            (blocks,),
            (RING - 1, piece),
            (piece,),
        ):
            scratch.append(pltpu.VMEM(lead + (rows, width), grad.dtype))
    dma = pltpu.SemaphoreType.DMA
    return scratch + [dma((len(grads), 16)), dma((len(grads), 16)), dma((len(grads), 5))]


def sum_shapes(grads):
    return [
        jax.ShapeDtypeStruct((RING, piece_rows(g.shape[1])) + g.shape[2:], g.dtype) for g in grads
    ]


def sum_gradients(grads):
    count = len(grads)
    return pl.pallas_call(
        functools.partial(sum_kernel, count),
        out_shape=sum_shapes(grads),
        in_specs=[pl.BlockSpec(memory_space=pl.ANY)] * count,
        out_specs=[pl.BlockSpec(memory_space=pl.ANY)] * count,
        scratch_shapes=sum_scratch(grads),
        compiler_params=pltpu.CompilerParams(
            collective_id=1, has_side_effects=True, vmem_limit_bytes=60 * 1024 * 1024
        ),
        name="sum_gradients",
    )(*grads)


def assemble(pieces, blocks):
    starts = [i * blocks // RING for i in range(RING + 1)]
    joined = jnp.concatenate(
        [pieces[i, : starts[i + 1] - starts[i]] for i in range(RING)], 0
    ).astype(jnp.float32)
    return joined.reshape(-1, pieces.shape[-1])


def lane_head(shape):
    return lax.broadcasted_iota(jnp.int32, shape, len(shape) - 1) // HEAD


def one_head(matrix, head):
    return jnp.where(lane_head(matrix.shape) == head, matrix, jnp.zeros_like(matrix))


def over_lanes(left, right):
    return lax.dot_general(left, right, (((1,), (1,)), ((), ())), preferred_element_type=jnp.float32)


def over_rows(left, right):
    return lax.dot_general(left, right, (((0,), (0,)), ((), ())), preferred_element_type=jnp.float32)


def plain(left, right):
    return jnp.dot(left, right, preferred_element_type=jnp.float32)


def soft_columns(key_rows, queries, first_query, length):
    scores = over_lanes(key_rows, queries) * HEAD ** (-0.5)
    key_pos = lax.broadcasted_iota(jnp.int32, scores.shape, 0)
    query_pos = first_query + lax.broadcasted_iota(jnp.int32, scores.shape, 1)
    scores = jnp.where((key_pos <= query_pos) & (key_pos < length), scores, MASKED)
    exponent = jnp.exp(scores - jnp.max(scores, 0, keepdims=True))
    return exponent * (1.0 / jnp.sum(exponent, 0, keepdims=True))


def peers(count):
    member = lax.axis_index("group")
    ahead = [(member + j) % count for j in range(1, count)]
    behind = [(member + count - j) % count for j in range(1, count)]
    return (member, ahead, behind)


def attend_kernel(plan, shards, *refs):
    lengths, pack, last_kv, last_q = refs[:4]
    ins, refs = refs[4 : 4 + shards], refs[4 + shards :]
    mixed, last_mixed, kept, kept_last = refs[:4]
    outs, refs = refs[4 : 4 + shards], refs[4 + shards :]
    held, held_last, staged = refs[:3]
    send, recv, send_last, recv_last, send_back, recv_back, local = refs[3:10]
    count, micros, _, rows, lanes = pack.shape
    member, ahead, behind = peers(count)
    devices = [{"group": peer} for peer in ahead]
    pump = Pump([])
    if shards:
        near = near_devices()
        devices = devices + [near[name] for name in ("sibling", "next", "last")]
    greet(devices)
    if shards:
        pump = gather_jobs(Links(refs[10], refs[11]), refs[12], plan, ins, outs)

    def out(m, j):
        return remote(
            pack.at[ahead[j], m], held.at[member, m], send.at[m, j], recv.at[m, j], {"group": ahead[j]}
        )

    def out_last(m, j):
        return remote(
            last_kv.at[m],
            held_last.at[member, m],
            send_last.at[m, j],
            recv_last.at[m, j],
            {"group": ahead[j]},
        )

    def back(m, j):
        return remote(
            staged.at[ahead[j], m],
            mixed.at[member, m],
            send_back.at[m, j],
            recv_back.at[m, j],
            {"group": ahead[j]},
        )

    def own(m):
        return (
            pltpu.make_async_copy(pack.at[member, m], held.at[member, m], local.at[m, 0]),
            pltpu.make_async_copy(last_kv.at[m], held_last.at[member, m], local.at[m, 1]),
        )

    def own_back(m):
        return pltpu.make_async_copy(staged.at[member, m], mixed.at[member, m], local.at[m, 2])

    def keep():
        return (
            pltpu.make_async_copy(held, kept, local.at[0, 3]),
            pltpu.make_async_copy(held_last, kept_last, local.at[1, 3]),
        )

    peer_range = range(count - 1)
    for m in range(micros):
        for j in peer_range:
            out(m, j).start()
            out_last(m, j).start()
        for copy in own(m):
            copy.start()
    pump()
    pump()

    def micro(m):
        for copy in own(m):
            copy.wait()
        for j in peer_range:
            out(m, j).wait_recv()
            out_last(m, j).wait_recv()
        length = lengths[m]
        wide = 2
        for block in range(count // wide):
            reach = wide * (block + 1)
            queries = held[wide * block : reach, m, 0].reshape(wide * rows, lanes)
            key_rows = held[0:reach, m, 1].reshape(reach * rows, lanes)
            values = held[0:reach, m, 2].reshape(reach * rows, lanes)

            def head_step(head, total):
                probs = soft_columns(
                    key_rows, one_head(queries, head), wide * block * rows, length
                ).astype(jnp.bfloat16)
                return total + over_rows(one_head(values, head), probs)

            total = lax.fori_loop(0, 2, head_step, jnp.zeros((lanes, wide * rows), jnp.float32))
            staged[wide * block : reach, m] = (
                total.T.astype(jnp.bfloat16).reshape(wide, rows, lanes)
            )
        for j in peer_range:
            back(m, j).start()
        own_back(m).start()
        pump()
        both = held_last[:, m].reshape(count * rows, lanes)
        probs = soft_columns(both, last_q[m], member * rows, length).astype(jnp.bfloat16)
        last_mixed[m] = over_rows(both, probs).T.astype(jnp.bfloat16)

    for m in range(micros):
        micro(m)
    for copy in keep():
        copy.start()
    pump.drain()
    for m in range(micros):
        own_back(m).wait()
        for j in peer_range:
            out(m, j).wait_send()
            out_last(m, j).wait_send()
            back(m, j).wait()
    for copy in keep():
        copy.wait()


def attend(lengths, pack, last_kv, last_q, shards=(), plan=()):
    count, micros, _, rows, lanes = pack.shape
    bf16 = jnp.bfloat16
    vmem, hbm = pl.BlockSpec(memory_space=pltpu.VMEM), pl.BlockSpec(memory_space=pl.ANY)
    dma = pltpu.SemaphoreType.DMA
    return pl.pallas_call(
        functools.partial(attend_kernel, plan, len(shards)),
        out_shape=[
            jax.ShapeDtypeStruct((count, micros, rows, lanes), bf16),
            jax.ShapeDtypeStruct((micros, rows, lanes), bf16),
            jax.ShapeDtypeStruct(pack.shape, bf16),
            jax.ShapeDtypeStruct((count, micros, rows, lanes), bf16),
        ]
        + gathered_shapes(shards),
        in_specs=[pl.BlockSpec(memory_space=pltpu.SMEM), hbm, vmem, vmem] + [hbm] * len(shards),
        out_specs=[hbm, vmem, hbm, hbm] + [hbm] * len(shards),
        scratch_shapes=[
            pltpu.VMEM(pack.shape, bf16),
            pltpu.VMEM((count, micros, rows, lanes), bf16),
            pltpu.VMEM((count, micros, rows, lanes), bf16),
        ]
        + [dma((micros, count - 1))] * 6
        + [dma((micros, 4))]
        + (gather_sems(len(shards)) if shards else []),
        compiler_params=pltpu.CompilerParams(
            collective_id=2 + 2 * min(1, len(shards)),
            has_side_effects=True,
            vmem_limit_bytes=48 * 1024 * 1024,
        ),
        name="attend_gather" if shards else "attend",
    )(lengths, pack, last_kv, last_q, *shards)


def attend_back_kernel(extra, *refs):
    lengths, held, held_last, last_q, grad_pack, last_grad = refs[:6]
    ins, refs = refs[6 : 6 + extra], refs[6 + extra :]
    grads, last_key_grad, last_query_grad = refs[:3]
    outs, refs = refs[3 : 3 + extra], refs[3 + extra :]
    came, staged, staged_last, parts_last, key_total, value_total = refs[:6]
    send, recv, send_back, recv_back, send_last, recv_last, local = refs[6:13]
    count, micros, _, rows, lanes = held.shape
    member, ahead, behind = peers(count)
    devices = [{"group": peer} for peer in ahead]
    pump = Pump([])
    if extra:
        _, _, sibling, partner, others = sum_devices()
        devices = devices + [sibling, partner] + others
    greet(devices)
    if extra:
        split = 13 + PER_ARRAY * extra
        pump = Pump([sum_job(ins, outs, refs[13:split], *refs[split:])])
    pump()
    scale = HEAD ** (-0.5)

    def out(m, j):
        return remote(
            grad_pack.at[ahead[j], m],
            came.at[member, m],
            send.at[m, j],
            recv.at[m, j],
            {"group": ahead[j]},
        )

    def back(m, j):
        return remote(
            staged.at[ahead[j], m],
            grads.at[member, m],
            send_back.at[m, j],
            recv_back.at[m, j],
            {"group": ahead[j]},
        )

    def back_last(m, j):
        return remote(
            staged_last.at[ahead[j], m],
            parts_last.at[member, m],
            send_last.at[m, j],
            recv_last.at[m, j],
            {"group": ahead[j]},
        )

    def own(m):
        return pltpu.make_async_copy(grad_pack.at[member, m], came.at[member, m], local.at[m, 0])

    def own_back(m):
        return (
            pltpu.make_async_copy(staged.at[member, m], grads.at[member, m], local.at[m, 1]),
            pltpu.make_async_copy(
                staged_last.at[member, m], parts_last.at[member, m], local.at[m, 2]
            ),
        )

    peer_range = range(count - 1)
    for m in range(micros):
        for j in peer_range:
            out(m, j).start()
        own(m).start()

    def micro(m):
        length = lengths[m]
        both = held_last[:, m].reshape(count * rows, lanes)
        probs = soft_columns(both, last_q[m], member * rows, length)
        grad_probs = over_lanes(both, last_grad[m])
        inner = jnp.sum(probs * grad_probs, 0, keepdims=True)
        grad_scores = (probs * (grad_probs - inner)).astype(jnp.bfloat16)
        last_query_grad[m] = (scale * over_rows(both, grad_scores)).T.astype(jnp.bfloat16)
        both_grad = scale * plain(grad_scores, last_q[m]) + plain(
            probs.astype(jnp.bfloat16), last_grad[m]
        )
        staged_last[:, m] = both_grad.astype(jnp.bfloat16).reshape(count, rows, lanes)
        for j in peer_range:
            back_last(m, j).start()
        pump()
        own(m).wait()
        for j in peer_range:
            out(m, j).wait_recv()
        key_total[...] = jnp.zeros_like(key_total)
        value_total[...] = jnp.zeros_like(value_total)
        wide = 2
        for block in range(count // wide):
            reach = wide * (block + 1)
            queries = held[wide * block : reach, m, 0].reshape(wide * rows, lanes)
            grad_out = came[wide * block : reach, m].reshape(wide * rows, lanes)
            key_rows = held[0:reach, m, 1].reshape(reach * rows, lanes)
            values = held[0:reach, m, 2].reshape(reach * rows, lanes)

            def head_step(head, total):
                head_queries, head_grad = one_head(queries, head), one_head(grad_out, head)
                probs = soft_columns(key_rows, head_queries, wide * block * rows, length)
                grad_probs = over_lanes(values, head_grad)
                inner = jnp.sum(probs * grad_probs, 0, keepdims=True)
                grad_scores = (probs * (grad_probs - inner)).astype(jnp.bfloat16)
                value_total[0 : reach * rows] += plain(probs.astype(jnp.bfloat16), head_grad)
                key_total[0 : reach * rows] += plain(grad_scores, head_queries)
                return total + over_rows(one_head(key_rows, head), grad_scores)

            total = lax.fori_loop(0, 2, head_step, jnp.zeros((lanes, wide * rows), jnp.float32))
            staged[wide * block : reach, m, 0] = (
                (scale * total).T.astype(jnp.bfloat16).reshape(wide, rows, lanes)
            )
        staged[:, m, 1] = (scale * key_total[...]).astype(jnp.bfloat16).reshape(count, rows, lanes)
        staged[:, m, 2] = value_total[...].astype(jnp.bfloat16).reshape(count, rows, lanes)
        for j in peer_range:
            back(m, j).start()
        for copy in own_back(m):
            copy.start()
        pump()

    for m in range(micros):
        micro(m)
    pump.drain()
    for m in range(micros):
        for copy in own_back(m):
            copy.wait()
        for j in peer_range:
            back_last(m, j).wait_recv()
        last_key_grad[m] = jnp.sum(parts_last[:, m].astype(jnp.float32), 0).astype(jnp.bfloat16)
    for m in range(micros):
        for j in peer_range:
            out(m, j).wait_send()
            back_last(m, j).wait_send()
            back(m, j).wait()


def attend_back(lengths, held, held_last, last_q, grad_pack, last_grad, sums=()):
    count, micros, _, rows, lanes = held.shape
    bf16 = jnp.bfloat16
    vmem, hbm = pl.BlockSpec(memory_space=pltpu.VMEM), pl.BlockSpec(memory_space=pl.ANY)
    dma = pltpu.SemaphoreType.DMA
    return pl.pallas_call(
        functools.partial(attend_back_kernel, len(sums)),
        out_shape=[
            jax.ShapeDtypeStruct(held.shape, bf16),
            jax.ShapeDtypeStruct((micros, rows, lanes), bf16),
            jax.ShapeDtypeStruct((micros, rows, lanes), bf16),
        ]
        + sum_shapes(sums),
        in_specs=[pl.BlockSpec(memory_space=pltpu.SMEM), vmem, vmem, vmem, hbm, vmem]
        + [hbm] * len(sums),
        out_specs=[hbm, vmem, vmem] + [hbm] * len(sums),
        scratch_shapes=[
            pltpu.VMEM((count, micros, rows, lanes), bf16),
            pltpu.VMEM(held.shape, bf16),
            pltpu.VMEM((count, micros, rows, lanes), bf16),
            pltpu.VMEM((count, micros, rows, lanes), bf16),
            pltpu.VMEM((count * rows, lanes), jnp.float32),
            pltpu.VMEM((count * rows, lanes), jnp.float32),
        ]
        + [dma((micros, count - 1))] * 6
        + [dma((micros, 3))]
        + (sum_scratch(sums) if sums else []),
        compiler_params=pltpu.CompilerParams(
            collective_id=3 + 2 * min(1, len(sums)),
            has_side_effects=True,
            vmem_limit_bytes=58 * 1024 * 1024 if sums else 48 * 1024 * 1024,
        ),
        name="attend_back_sum" if sums else "attend_back",
    )(lengths, held, held_last, last_q, grad_pack, last_grad, *sums)


def norm_rows(inputs, gain_row, bias_row):
    average = jnp.mean(inputs, -1, keepdims=True)
    centered = inputs - average
    variance = jnp.mean(centered * centered, -1, keepdims=True)
    return centered * lax.rsqrt(variance + EPSILON) * gain_row + bias_row


def gelu_tanh(inputs):
    return jax.nn.gelu(inputs, approximate=True)


def by_heads(matrix, micros, rows, count):
    return matrix.reshape(micros, rows, count, LANES).transpose(2, 0, 1, 3)


def by_rows(blocks):
    count, micros, rows, lanes = blocks.shape
    return blocks.transpose(1, 2, 0, 3).reshape(micros * rows, count * lanes)


def in_blocks(matrix):
    return matrix.reshape(matrix.shape[0] // 8, 8, matrix.shape[1])


def body(
    block_input, out_grad, w_qkv, w_proj, w_up, w_down, vectors, b_up, seq_lengths, slot_of_seq
):
    section = lax.axis_index("pipe")
    replica = lax.axis_index("rep")
    member = lax.axis_index("group")
    rep_count = lax.axis_size("rep")
    count = lax.axis_size("group")
    micros, rows, width = block_input.shape[0], block_input.shape[2], block_input.shape[3]
    wide = count * LANES
    slot_ids = jnp.arange(seq_lengths.shape[0], dtype=jnp.int32)
    slot_len = jnp.sum(
        seq_lengths[:, None] * (slot_of_seq[:, None] == slot_ids[None, :]).astype(jnp.int32), axis=0
    )
    mine = jnp.arange(micros, dtype=jnp.int32) * rep_count + replica
    lengths = jnp.sum(
        slot_len[None, :] * (slot_ids[None, :] == mine[:, None]).astype(jnp.int32), axis=1
    )
    query_pos = member * rows + jnp.arange(rows, dtype=jnp.int32)
    valid = (query_pos[None, :] < lengths[:, None]).astype(jnp.float32)[:, :, None]
    cotangent = (out_grad[:, 0].astype(jnp.float32) * valid).reshape(micros * rows, width)

    bias_rows = b_up.shape[1] // vectors.shape[2]
    small = jnp.concatenate(
        [
            vectors[0],
            b_up[0].reshape(bias_rows, -1),
            jnp.zeros((8 - bias_rows, vectors.shape[2]), vectors.dtype),
        ],
        0,
    )
    small_full, qkv_full = gather_weights(
        [in_blocks(small), in_blocks(w_qkv[0])],
        ((0, 0, 2, False), (1, 0, 9, False), (1, 9, 8, True)),
    )
    vector_rows = small_full[:, 0].transpose(1, 0, 2).reshape(8, width).astype(jnp.float32)
    up_bias = small_full[:, 1, :bias_rows].reshape(-1).astype(jnp.float32)
    qkv_weight = qkv_full.reshape(width, -1)
    later = [in_blocks(w_proj[0]), in_blocks(w_up[0]), in_blocks(w_down[0])]
    later_plan = ((0, 0, 17, False), (1, 0, 16, True), (2, 0, 68, True), (1, 16, 1, False))
    qkv_bias = jnp.concatenate([vector_rows[2], jnp.zeros_like(vector_rows[2]), vector_rows[3]])

    def pad_last(matrix, before):
        block = matrix.reshape(micros, rows, HEAD)
        return jnp.pad(block, ((0, 0), (0, 0), (before, LANES - HEAD - before)))

    def forward(inputs, weights):
        normed = norm_rows(inputs, vector_rows[0], vector_rows[1]).astype(jnp.bfloat16)
        qkv = (plain(normed, qkv_weight) + qkv_bias).astype(jnp.bfloat16)
        thirds = [qkv[:, i * width : (i + 1) * width] for i in range(3)]
        pack = jnp.stack([by_heads(t[:, :wide], micros, rows, count) for t in thirds], 2)
        last_kv = jnp.concatenate([thirds[1][:, wide:], thirds[2][:, wide:]], 1).reshape(
            micros, rows, LANES
        )
        last_q = pad_last(thirds[0][:, wide:], 0)
        if weights is None:
            mixed, last_mixed, held, held_last, *full = attend(
                lengths, pack, last_kv, last_q, later, later_plan
            )
            weights = [array.reshape(-1, width if i != 1 else 4 * width) for i, array in enumerate(full)]
        else:
            mixed, last_mixed, held, held_last = attend(lengths, pack, last_kv, last_q)
        proj_weight, up_weight, down_weight = weights
        attn_mixed = jnp.concatenate(
            [by_rows(mixed), last_mixed[:, :, HEAD:].reshape(micros * rows, HEAD)], 1
        )
        hidden = inputs + plain(attn_mixed, proj_weight) + vector_rows[4]
        normed_two = norm_rows(hidden, vector_rows[5], vector_rows[6]).astype(jnp.bfloat16)
        pre_act = plain(normed_two, up_weight) + up_bias
        activated = gelu_tanh(pre_act).astype(jnp.bfloat16)
        output = hidden + plain(activated, down_weight) + vector_rows[7]
        return (output, weights, (inputs, held, held_last, last_q, attn_mixed, hidden, pre_act, activated))

    def outer(left, right):
        return over_rows(left, right).astype(jnp.bfloat16)

    def shards(matrix):
        return matrix.reshape(count, -1, 8, matrix.shape[-1])

    def backward(grad_output, saved, final):
        inputs, held, held_last, last_q, attn_mixed, hidden, pre_act, activated = saved
        grad_two = grad_output.astype(jnp.bfloat16)
        grad_act = plain(grad_two, down_weight.T)
        grad_pre = jax.vjp(gelu_tanh, pre_act)[1](grad_act)[0].astype(jnp.bfloat16)
        normed_two, pull_two = jax.vjp(norm_rows, hidden, vector_rows[5], vector_rows[6])
        from_norm, gain_two, shift_two = pull_two(plain(grad_pre, up_weight.T))
        grad_hidden = grad_output + from_norm
        grad_one = grad_hidden.astype(jnp.bfloat16)
        grad_mixed = plain(grad_one, proj_weight.T).astype(jnp.bfloat16)
        first_grads = ()
        if final:
            first_grads = (
                shards(outer(activated, grad_two)),
                shards(outer(normed_two.astype(jnp.bfloat16), grad_pre)),
            )
        grads, last_key_grad, last_query_grad, *first_sums = attend_back(
            lengths,
            held,
            held_last,
            last_q,
            by_heads(grad_mixed[:, :wide], micros, rows, count),
            pad_last(grad_mixed[:, wide:], HEAD),
            first_grads,
        )

        def last(block, first):
            return block[:, :, first : first + HEAD].reshape(micros * rows, HEAD)

        grad_qkv = jnp.concatenate(
            [
                by_rows(grads[:, :, 0]),
                last(last_query_grad, 0),
                by_rows(grads[:, :, 1]),
                last(last_key_grad, 0),
                by_rows(grads[:, :, 2]),
                last(last_key_grad, HEAD),
            ],
            1,
        )
        normed, pull = jax.vjp(norm_rows, inputs, vector_rows[0], vector_rows[1])
        from_norm, gain, shift = pull(plain(grad_qkv, qkv_weight.T))
        grad_in = grad_hidden + from_norm

        def weight_grads():
            sums = jnp.sum(grad_qkv.astype(jnp.float32), 0)
            rows_of_vectors = jnp.stack(
                [
                    gain,
                    shift,
                    sums[:width],
                    sums[2 * width :],
                    jnp.sum(grad_one.astype(jnp.float32), 0),
                    gain_two,
                    shift_two,
                    jnp.sum(grad_two.astype(jnp.float32), 0),
                ]
            )
            return (
                outer(normed.astype(jnp.bfloat16), grad_qkv),
                outer(attn_mixed, grad_one),
                first_sums[1],
                first_sums[0],
                rows_of_vectors,
                jnp.sum(grad_pre.astype(jnp.float32), 0),
            )

        return (grad_in, weight_grads)

    first_in = block_input[:, 0].reshape(micros * rows, width).astype(jnp.float32)
    first_out, weights, _ = forward(first_in, None)
    proj_weight, up_weight, down_weight = weights
    arrived = lax.ppermute(first_out.astype(jnp.bfloat16), "pipe", [(0, 1)])
    output, _, saved = forward(
        jnp.where(section == 0, first_in, arrived.astype(jnp.float32)), weights
    )
    last_grad, _ = backward(cotangent, saved, False)
    arrived = lax.ppermute(last_grad.astype(jnp.bfloat16), "pipe", [(1, 0)])
    grad_in, weight_grads = backward(
        jnp.where(section == 1, cotangent, arrived.astype(jnp.float32)), saved, True
    )
    grad_qkv, grad_proj, sum_up, sum_down, grad_vectors, grad_bias = weight_grads()

    small_grads = jnp.concatenate(
        [
            grad_vectors.reshape(8, count, -1).transpose(1, 0, 2),
            grad_bias.reshape(count, bias_rows, -1),
            jnp.zeros((count, 24 - bias_rows, width // count), jnp.float32),
        ],
        1,
    ).reshape(count, RING, 8, width // count)
    sum_qkv, small_sum, sum_proj = sum_gradients(
        [shards(grad_qkv), small_grads, shards(grad_proj)]
    )
    totals = [
        assemble(total, blocks)
        for total, blocks in ((sum_qkv, 17), (sum_proj, 17), (sum_up, 17), (sum_down, 68))
    ]
    small_total = small_sum.reshape(RING * 8, -1)
    edges = jnp.where(section == 0, grad_in, output).reshape(1, micros, 1, rows, width)
    return (
        edges,
        totals[0][None],
        totals[1][None],
        totals[2][None],
        totals[3][None],
        small_total[None, :8],
        small_total[8 : 8 + bias_rows].reshape(1, -1),
    )


def solution(mesh):
    in_specs = (
        P(None, "rep", "group", None),
        P(None, "rep", "group", None),
        P("pipe", "group", None),
        P("pipe", "group", None),
        P("pipe", "group", None),
        P("pipe", "group", None),
        P("pipe", None, "group"),
        P("pipe", "group"),
        P(),
        P(),
    )
    out_specs = (
        P("pipe", None, "rep", "group", None),
        P("pipe", "group", None),
        P("pipe", "group", None),
        P("pipe", "group", None),
        P("pipe", "group", None),
        P("pipe", None, "group"),
        P("pipe", "group"),
    )
    return jax.shard_map(body, mesh=mesh, in_specs=in_specs, out_specs=out_specs, check_vma=False)
```

```python
import functools
import jax
import jax.numpy as jnp
from jax import lax
from jax.experimental import pallas as pl
from jax.experimental.pallas import tpu as pltpu
from jax.sharding import PartitionSpec as P

HEAD = 64
LANES = 128
EPSILON = 1e-05
MASKED = -1e30
MESH = pl.DeviceIdType.MESH
RING = 4


def remote(src, dst, send_sem, recv_sem, device):
    return pltpu.make_async_remote_copy(
        src_ref=src,
        dst_ref=dst,
        send_sem=send_sem,
        recv_sem=recv_sem,
        device_id=device,
        device_id_type=MESH,
    )


def greet(devices):
    barrier = pltpu.get_barrier_semaphore()
    for device in devices:
        pl.semaphore_signal(barrier, inc=1, device_id=device, device_id_type=MESH)
    pl.semaphore_wait(barrier, len(devices))


def place():
    member, replica = lax.axis_index("group"), lax.axis_index("rep")
    return (member // 2, member % 2, replica // 2, replica % 2)


def gather_kernel(count, *refs):
    ins, outs = refs[:count], refs[count : 2 * count]
    send, recv, local = refs[2 * count :]
    z, x, y, c = place()
    me = 2 * z + x
    xc = (x + c) % 2
    zp, zm, zo = (z + 1) % RING, (z + 3) % RING, (z + 2) % RING
    base, above, below, across = 2 * z + xc, 2 * zp + xc, 2 * zm + xc, 2 * zo + xc
    to_above = {"group": 2 * zp + x}
    to_below = {"group": 2 * zm + x}
    sibling = {"rep": 2 * y + 1 - c}
    partner = {"group": 2 * z + 1 - x}
    greet([to_above, to_below, sibling, partner])

    def part(array, slot, kind):
        half = ins[array].shape[0] // 2
        ref = outs[array].at[slot]
        if kind == "low":
            return ref.at[pl.ds(0, half)]
        if kind == "high":
            return ref.at[pl.ds(half, ins[array].shape[0] - half)]
        return ref

    def across_x(i):
        return remote(ins[i], part(i, me, ""), send.at[i, 0], recv.at[i, 0], partner)

    def first_up(i):
        src = part(i, base, "")
        return remote(src, part(i, base, ""), send.at[i, 1], recv.at[i, 1], to_above)

    def first_down(i):
        src = part(i, base, "")
        return remote(src, part(i, base, ""), send.at[i, 2], recv.at[i, 2], to_below)

    def second_up(i):
        src = part(i, below, "low")
        return remote(src, src, send.at[i, 3], recv.at[i, 3], to_above)

    def second_down(i):
        src = part(i, above, "high")
        return remote(src, src, send.at[i, 4], recv.at[i, 4], to_below)

    def hand(i, slot, kind, sem):
        src = part(i, slot, kind)
        return remote(src, src, send.at[i, sem], recv.at[i, sem], sibling)

    def own(i):
        return pltpu.make_async_copy(ins[i], part(i, me, ""), local.at[i])

    def own_up(i):
        return remote(ins[i], part(i, me, ""), send.at[i, 1], recv.at[i, 1], to_above)

    def own_down(i):
        return remote(ins[i], part(i, me, ""), send.at[i, 2], recv.at[i, 2], to_below)

    arrays = range(count)

    @pl.when(c == 0)
    def _():
        for i in arrays:
            own_up(i).start()
            own_down(i).start()

    @pl.when(c == 1)
    def _():
        for i in arrays:
            across_x(i).start()

    for i in arrays:
        own(i).start()

    @pl.when(c == 1)
    def _():
        for i in arrays:
            remote(ins[i], part(i, base, ""), send.at[i, 0], recv.at[i, 0], partner).wait_recv()
            first_up(i).start()
            first_down(i).start()
            hand(i, base, "", 5).start()

    for i in arrays:
        remote(ins[i], part(i, below, ""), send.at[i, 1], recv.at[i, 1], to_above).wait_recv()
        second_up(i).start()
        hand(i, below, "", 6).start()
        remote(ins[i], part(i, above, ""), send.at[i, 2], recv.at[i, 2], to_below).wait_recv()
        second_down(i).start()
        hand(i, above, "", 7).start()
    for i in arrays:
        src = part(i, across, "low")
        remote(src, src, send.at[i, 3], recv.at[i, 3], to_above).wait_recv()
        hand(i, across, "low", 8).start()
        src = part(i, across, "high")
        remote(src, src, send.at[i, 4], recv.at[i, 4], to_below).wait_recv()
        hand(i, across, "high", 9).start()

    @pl.when(c == 0)
    def _():
        for i in arrays:
            hand(i, 2 * z + 1 - xc, "", 5).wait_recv()
            own_up(i).wait_send()
            own_down(i).wait_send()

    @pl.when(c == 1)
    def _():
        for i in arrays:
            across_x(i).wait_send()
            first_up(i).wait_send()
            first_down(i).wait_send()
            hand(i, base, "", 5).wait_send()

    for i in arrays:
        hand(i, 2 * zm + 1 - xc, "", 6).wait_recv()
        hand(i, 2 * zp + 1 - xc, "", 7).wait_recv()
        hand(i, 2 * zo + 1 - xc, "low", 8).wait_recv()
        hand(i, 2 * zo + 1 - xc, "high", 9).wait_recv()
        second_up(i).wait_send()
        second_down(i).wait_send()
        hand(i, below, "", 6).wait_send()
        hand(i, above, "", 7).wait_send()
        hand(i, across, "low", 8).wait_send()
        hand(i, across, "high", 9).wait_send()
        own(i).wait()


def gather_weights(shards):
    count = len(shards)
    return pl.pallas_call(
        functools.partial(gather_kernel, count),
        out_shape=[jax.ShapeDtypeStruct((8,) + s.shape, s.dtype) for s in shards],
        in_specs=[pl.BlockSpec(memory_space=pl.ANY)] * count,
        out_specs=[pl.BlockSpec(memory_space=pl.ANY)] * count,
        scratch_shapes=[
            pltpu.SemaphoreType.DMA((count, 10)),
            pltpu.SemaphoreType.DMA((count, 10)),
            pltpu.SemaphoreType.DMA((count,)),
        ],
        compiler_params=pltpu.CompilerParams(collective_id=0, has_side_effects=True),
        name="gather_weights",
    )(*shards)


def piece_rows(blocks):
    starts = [i * blocks // RING for i in range(RING + 1)]
    return max(starts[i + 1] - starts[i] for i in range(RING))


def add_blocks(count, dst, terms):
    def step(b, carry):
        total = dst[b].astype(jnp.float32)
        for term in terms:
            total = total + term[b].astype(jnp.float32)
        dst[b] = total.astype(dst.dtype)
        return carry

    lax.fori_loop(0, count, step, 0)


PER_ARRAY = 9


def sum_kernel(count, *refs):
    ins, outs = refs[:count], refs[count : 2 * count]
    buffers = refs[2 * count : 2 * count + PER_ARRAY * count]
    send, recv, local = refs[2 * count + PER_ARRAY * count :]
    z, x, y, c = place()
    xc = (x + c) % 2
    zp, zm = (z + 1) % RING, (z + 3) % RING
    to_above = {"group": 2 * zp + x}
    to_below = {"group": 2 * zm + x}
    sibling = {"rep": 2 * y + 1 - c}
    partner = {"group": 2 * z + 1 - x, "rep": 2 * y + 1 - c}
    others = [{"rep": 2 * ((y + j) % RING) + c} for j in range(1, RING)]
    greet([to_above, to_below, sibling, partner] + others)

    def parts(i):
        return buffers[PER_ARRAY * i : PER_ARRAY * (i + 1)]

    def swap(i, k):
        own, came = ins[i].at[2 * ((z + k) % RING) + 1 - xc], parts(i)[1].at[k]
        return remote(own, came, send.at[i, k], recv.at[i, k], sibling)

    def load(i, k):
        return pltpu.make_async_copy(
            ins[i].at[2 * ((z + k) % RING) + xc], parts(i)[0].at[k], local.at[i, k]
        )

    def sizes(i):
        blocks = ins[i].shape[1]
        return (blocks, blocks // 2, piece_rows(blocks))

    def far_up(i):
        blocks, half, _ = sizes(i)
        src = parts(i)[0].at[2, pl.ds(0, half)]
        return remote(src, parts(i)[2], send.at[i, 4], recv.at[i, 4], to_above)

    def far_down(i):
        blocks, half, _ = sizes(i)
        src = parts(i)[0].at[2, pl.ds(half, blocks - half)]
        return remote(src, parts(i)[3], send.at[i, 5], recv.at[i, 5], to_below)

    def near_up(i):
        return remote(parts(i)[0].at[1], parts(i)[4], send.at[i, 6], recv.at[i, 6], to_above)

    def near_down(i):
        return remote(parts(i)[0].at[3], parts(i)[5], send.at[i, 7], recv.at[i, 7], to_below)

    def over_x(i):
        return remote(parts(i)[0].at[0], parts(i)[6], send.at[i, 8], recv.at[i, 8], partner)

    def own_piece(i, owner):
        blocks, _, rows = sizes(i)
        return parts(i)[0].at[0, pl.ds((owner * blocks) // RING, rows)]

    def over_y(i, j):
        src = own_piece(i, (y + j) % RING)
        dst = parts(i)[7].at[j - 1]
        return remote(src, dst, send.at[i, 8 + j], recv.at[i, 8 + j], others[j - 1])

    def share_y(i, j, slot):
        dst = outs[i].at[slot]
        return remote(parts(i)[8], dst, send.at[i, 11 + j], recv.at[i, 11 + j], others[j - 1])

    def keep(i):
        return pltpu.make_async_copy(parts(i)[8], outs[i].at[y], local.at[i, 4])

    def hand(i):
        return remote(outs[i], outs[i], send.at[i, 15], recv.at[i, 15], sibling)

    for i in range(count):
        for k in (2, 1, 3, 0):
            swap(i, k).start()
            load(i, k).start()

    def step_cores(i):
        blocks, half, _ = sizes(i)
        total, came = parts(i)[0], parts(i)[1]
        for k in (2, 1, 3, 0):
            load(i, k).wait()
            swap(i, k).wait_recv()
            add_blocks(blocks, total.at[k], [came.at[k]])
            if k == 2:
                far_up(i).start()
                far_down(i).start()

    def step_far(i):
        blocks, half, _ = sizes(i)
        total = parts(i)[0]
        far_up(i).wait_recv()
        add_blocks(half, total.at[1, pl.ds(0, half)], [parts(i)[2]])
        near_up(i).start()
        far_down(i).wait_recv()
        add_blocks(blocks - half, total.at[3, pl.ds(half, blocks - half)], [parts(i)[3]])
        near_down(i).start()

    def step_near(i):
        blocks, half, _ = sizes(i)
        near_up(i).wait_recv()
        near_down(i).wait_recv()
        add_blocks(blocks, parts(i)[0].at[0], [parts(i)[4], parts(i)[5]])

        @pl.when(c == 1)
        def _():
            over_x(i).start()

    def step_x(i):
        blocks, half, _ = sizes(i)

        @pl.when(c == 0)
        def _():
            over_x(i).wait_recv()
            add_blocks(blocks, parts(i)[0].at[0], [parts(i)[6]])
            for j in (2, 1, 3):
                over_y(i, j).start()

    def step_y(i):
        _, _, rows = sizes(i)

        @pl.when(c == 0)
        def _():
            for j in (1, 2, 3):
                over_y(i, j).wait_recv()
            own, came, result = own_piece(i, y), parts(i)[7], parts(i)[8]

            def step(b, carry):
                total = own[b].astype(jnp.float32)
                for j in range(RING - 1):
                    total = total + came[j, b].astype(jnp.float32)
                result[b] = total.astype(result.dtype)
                return carry

            lax.fori_loop(0, rows, step, 0)
            for j in (2, 1, 3):
                share_y(i, j, y).start()
            keep(i).start()

    def step_hand(i):
        @pl.when(c == 0)
        def _():
            keep(i).wait()
            for j in (1, 2, 3):
                share_y(i, j, (y + RING - j) % RING).wait_recv()
            hand(i).start()

    def step_last(i):
        @pl.when(c == 1)
        def _():
            hand(i).wait_recv()

    steps = [step_cores, step_far, step_near, step_x, step_y, step_hand, step_last]
    for tick in range(count + len(steps) - 1):
        for i in range(count):
            at = tick - i
            if 0 <= at < len(steps):
                steps[at](i)
    for i in range(count):
        for k in range(RING):
            swap(i, k).wait_send()
        for copy in (far_up, far_down, near_up, near_down):
            copy(i).wait_send()

        @pl.when(c == 1)
        def _():
            over_x(i).wait_send()

        @pl.when(c == 0)
        def _():
            for j in (1, 2, 3):
                over_y(i, j).wait_send()
                share_y(i, j, y).wait_send()
            hand(i).wait_send()


def sum_gradients(grads):
    count = len(grads)
    scratch = []
    for grad in grads:
        _, blocks, rows, width = grad.shape
        half, piece = blocks // 2, piece_rows(blocks)
        for lead in (
            (RING, blocks),
            (RING, blocks),
            (half,),
            (blocks - half,),
            (blocks,),
            (blocks,),
            (blocks,),
            (RING - 1, piece),
            (piece,),
        ):
            scratch.append(pltpu.VMEM(lead + (rows, width), grad.dtype))
    return pl.pallas_call(
        functools.partial(sum_kernel, count),
        out_shape=[
            jax.ShapeDtypeStruct((RING, piece_rows(g.shape[1])) + g.shape[2:], g.dtype)
            for g in grads
        ],
        in_specs=[pl.BlockSpec(memory_space=pl.ANY)] * count,
        out_specs=[pl.BlockSpec(memory_space=pl.ANY)] * count,
        scratch_shapes=scratch
        + [
            pltpu.SemaphoreType.DMA((count, 16)),
            pltpu.SemaphoreType.DMA((count, 16)),
            pltpu.SemaphoreType.DMA((count, 5)),
        ],
        compiler_params=pltpu.CompilerParams(
            collective_id=1, has_side_effects=True, vmem_limit_bytes=60 * 1024 * 1024
        ),
        name="sum_gradients",
    )(*grads)


def assemble(pieces, blocks):
    starts = [i * blocks // RING for i in range(RING + 1)]
    joined = jnp.concatenate(
        [pieces[i, : starts[i + 1] - starts[i]] for i in range(RING)], 0
    ).astype(jnp.float32)
    return joined.reshape(-1, pieces.shape[-1])


def lane_head(shape):
    return lax.broadcasted_iota(jnp.int32, shape, len(shape) - 1) // HEAD


def one_head(matrix, head):
    return jnp.where(lane_head(matrix.shape) == head, matrix, jnp.zeros_like(matrix))


def over_lanes(left, right):
    return lax.dot_general(left, right, (((1,), (1,)), ((), ())), preferred_element_type=jnp.float32)


def over_rows(left, right):
    return lax.dot_general(left, right, (((0,), (0,)), ((), ())), preferred_element_type=jnp.float32)


def plain(left, right):
    return jnp.dot(left, right, preferred_element_type=jnp.float32)


def half_selector(first):
    rows = lax.broadcasted_iota(jnp.int32, (HEAD, LANES), 0)
    lanes = lax.broadcasted_iota(jnp.int32, (HEAD, LANES), 1)
    return (rows + first == lanes).astype(jnp.bfloat16)


def widen(matrix, first):
    return plain(matrix, half_selector(first)).astype(jnp.bfloat16)


def narrow(matrix, first):
    return over_lanes(matrix, half_selector(first)).astype(jnp.bfloat16)


def soft_columns(key_rows, queries, first_query, length):
    scores = over_lanes(key_rows, queries) * HEAD ** (-0.5)
    key_pos = lax.broadcasted_iota(jnp.int32, scores.shape, 0)
    query_pos = first_query + lax.broadcasted_iota(jnp.int32, scores.shape, 1)
    scores = jnp.where((key_pos <= query_pos) & (key_pos < length), scores, MASKED)
    exponent = jnp.exp(scores - jnp.max(scores, 0, keepdims=True))
    return exponent * (1.0 / jnp.sum(exponent, 0, keepdims=True))


def peers(count):
    member = lax.axis_index("group")
    ahead = [(member + j) % count for j in range(1, count)]
    return (member, ahead)


def normalize(inputs):
    average = jnp.mean(inputs, -1, keepdims=True)
    centered = inputs - average
    variance = jnp.mean(centered * centered, -1, keepdims=True)
    scale = lax.rsqrt(variance + EPSILON)
    return (centered * scale, scale)


def norm_back(unit, scale, gain, grad):
    scaled = grad * gain
    pulled = scaled - jnp.mean(scaled, -1, keepdims=True)
    pulled = pulled - unit * jnp.mean(scaled * unit, -1, keepdims=True)
    return (
        pulled * scale,
        jnp.sum(grad * unit, 0, keepdims=True),
        jnp.sum(grad, 0, keepdims=True),
    )


GELU_IN, GELU_CUBE = 0.7978845608028654, 0.044715


def gelu_parts(value):
    square = value * value
    bent = jnp.tanh(GELU_IN * value * (1.0 + GELU_CUBE * square))
    half = 0.5 * (1.0 + bent)
    slope = half + 0.5 * value * (1.0 - bent * bent) * GELU_IN * (1.0 + 3.0 * GELU_CUBE * square)
    return (value * half, slope)


def column_chunks(width, most):
    return [(first, min(most, width - first)) for first in range(0, width, most)]


FORWARD_WEIGHTS = ("q", "k", "v", "proj", "up", "down")


def forward_kernel(
    lengths, inputs, vectors, up_bias, wq, wk, wv, wproj, wup, wdown,
    output, hidden_out, pre_act, attn_mixed, last_q, kept, kept_last,
    vq, vk, vv, vproj, vup, vdown, pack, last_kv, held, held_last, staged, mixed,
    send, recv, send_last, recv_last, send_back, recv_back, local, loaded,
):
    count, micros, _, rows, lanes = pack.shape
    member, ahead = peers(count)
    wide = count * lanes
    sources, places = (wq, wk, wv, wproj, wup, wdown), (vq, vk, vv, vproj, vup, vdown)
    loads = [
        pltpu.make_async_copy(sources[i], places[i], loaded.at[i]) for i in range(len(sources))
    ]
    for load in loads:
        load.start()
    greet([{"group": peer} for peer in ahead])

    def out(m, j):
        return remote(
            pack.at[ahead[j], m], held.at[member, m], send.at[m, j], recv.at[m, j], {"group": ahead[j]}
        )

    def out_last(m, j):
        return remote(
            last_kv.at[m],
            held_last.at[member, m],
            send_last.at[m, j],
            recv_last.at[m, j],
            {"group": ahead[j]},
        )

    def back(m, j):
        return remote(
            staged.at[ahead[j], m],
            mixed.at[member, m],
            send_back.at[m, j],
            recv_back.at[m, j],
            {"group": ahead[j]},
        )

    def own(m):
        return (
            pltpu.make_async_copy(pack.at[member, m], held.at[member, m], local.at[m, 0]),
            pltpu.make_async_copy(last_kv.at[m], held_last.at[member, m], local.at[m, 1]),
        )

    def own_back(m):
        return pltpu.make_async_copy(staged.at[member, m], mixed.at[member, m], local.at[m, 2])

    def keep():
        return (
            pltpu.make_async_copy(held, kept, local.at[0, 3]),
            pltpu.make_async_copy(held_last, kept_last, local.at[1, 3]),
        )

    peer_range = range(count - 1)
    unit, _ = normalize(inputs[...])
    normed = (unit * vectors[0:1] + vectors[1:2]).astype(jnp.bfloat16)
    lasts = []
    for third, (weight, bias) in enumerate(((vq, 2), (vk, None), (vv, 3))):
        loads[third].wait()
        product = plain(normed, weight[...])
        if bias is not None:
            product = product + vectors[bias : bias + 1]
        product = product.astype(jnp.bfloat16)
        for d in range(count):
            for m in range(micros):
                pack[d, m, third] = product[m * rows : (m + 1) * rows, d * lanes : (d + 1) * lanes]
        lasts.append(product[:, wide:])
    wide_q = widen(lasts[0], 0)
    both_last = widen(lasts[1], 0) + widen(lasts[2], HEAD)
    for m in range(micros):
        last_q[m] = wide_q[m * rows : (m + 1) * rows]
        last_kv[m] = both_last[m * rows : (m + 1) * rows]
    for m in range(micros):
        for j in peer_range:
            out(m, j).start()
            out_last(m, j).start()
        for copy in own(m):
            copy.start()

    def micro(m):
        for copy in own(m):
            copy.wait()
        for j in peer_range:
            out(m, j).wait_recv()
            out_last(m, j).wait_recv()
        length = lengths[m]
        span = 2
        for block in range(count // span):
            reach = span * (block + 1)
            queries = held[span * block : reach, m, 0].reshape(span * rows, lanes)
            key_rows = held[0:reach, m, 1].reshape(reach * rows, lanes)
            values = held[0:reach, m, 2].reshape(reach * rows, lanes)

            def head_step(head, total):
                probs = soft_columns(
                    key_rows, one_head(queries, head), span * block * rows, length
                ).astype(jnp.bfloat16)
                return total + over_rows(one_head(values, head), probs)

            total = lax.fori_loop(0, 2, head_step, jnp.zeros((lanes, span * rows), jnp.float32))
            staged[span * block : reach, m] = (
                total.T.astype(jnp.bfloat16).reshape(span, rows, lanes)
            )
        for j in peer_range:
            back(m, j).start()
        own_back(m).start()
        both = held_last[:, m].reshape(count * rows, lanes)
        probs = soft_columns(both, last_q[m], member * rows, length).astype(jnp.bfloat16)
        last_out = over_rows(both, probs).T.astype(jnp.bfloat16)
        attn_mixed[m * rows : (m + 1) * rows, wide:] = narrow(last_out, HEAD)

    for m in range(micros):
        micro(m)
    for copy in keep():
        copy.start()
    for m in range(micros):
        own_back(m).wait()
        for j in peer_range:
            back(m, j).wait_recv()
        for d in range(count):
            attn_mixed[m * rows : (m + 1) * rows, d * lanes : (d + 1) * lanes] = mixed[d, m]
    loads[3].wait()
    hidden = inputs[...] + plain(attn_mixed[...], vproj[...]) + vectors[4:5]
    hidden_out[...] = hidden
    unit, _ = normalize(hidden)
    normed = (unit * vectors[5:6] + vectors[6:7]).astype(jnp.bfloat16)
    output[...] = hidden + vectors[7:8]
    loads[4].wait()
    for first, size in column_chunks(pre_act.shape[1], 1152):
        columns = slice(first, first + size)
        value = plain(normed, vup[:, columns]) + up_bias[:, columns]
        pre_act[:, columns] = value
        activated, _ = gelu_parts(value)
        if first == 0:
            loads[5].wait()
        output[...] += plain(activated.astype(jnp.bfloat16), vdown[columns, :])
    for m in range(micros):
        for j in peer_range:
            out(m, j).wait_send()
            out_last(m, j).wait_send()
            back(m, j).wait_send()
    for copy in keep():
        copy.wait()


def forward_layer(lengths, inputs, vectors, up_bias, weights, count, micros):
    total, width = inputs.shape
    rows, lanes = total // micros, LANES
    hidden = weights[4].shape[1]
    bf16, f32 = jnp.bfloat16, jnp.float32
    vmem, hbm = pl.BlockSpec(memory_space=pltpu.VMEM), pl.BlockSpec(memory_space=pl.ANY)
    dma = pltpu.SemaphoreType.DMA
    pack, blocks = (count, micros, 3, rows, lanes), (count, micros, rows, lanes)
    return pl.pallas_call(
        forward_kernel,
        out_shape=[
            jax.ShapeDtypeStruct((total, width), f32),
            jax.ShapeDtypeStruct((total, width), f32),
            jax.ShapeDtypeStruct((total, hidden), f32),
            jax.ShapeDtypeStruct((total, width), bf16),
            jax.ShapeDtypeStruct((micros, rows, lanes), bf16),
            jax.ShapeDtypeStruct(pack, bf16),
            jax.ShapeDtypeStruct(blocks, bf16),
        ],
        in_specs=[pl.BlockSpec(memory_space=pltpu.SMEM)] + [vmem] * 3 + [hbm] * 6,
        out_specs=[vmem] * 5 + [hbm] * 2,
        scratch_shapes=[pltpu.VMEM(w.shape, bf16) for w in weights]
        + [
            pltpu.VMEM(pack, bf16),
            pltpu.VMEM((micros, rows, lanes), bf16),
            pltpu.VMEM(pack, bf16),
            pltpu.VMEM(blocks, bf16),
            pltpu.VMEM(blocks, bf16),
            pltpu.VMEM(blocks, bf16),
        ]
        + [dma((micros, count - 1))] * 6
        + [dma((micros, 4)), dma((6,))],
        compiler_params=pltpu.CompilerParams(
            collective_id=2, has_side_effects=True, vmem_limit_bytes=60 * 1024 * 1024
        ),
        name="forward_layer",
    )(lengths, inputs, vectors, up_bias, *weights)


def backward_kernel(
    lengths, grad_output, inputs, hidden, vectors, pre_act, held, held_last, last_q,
    wq, wk, wv, wproj, wup, wdown,
    grad_in, grad_q, grad_k, grad_v, grad_one, grad_pre, activated, normed_one, normed_two,
    vector_grads, bias_grads,
    vproj, vup, vdown, vqkv, grad_norm, grad_pack, last_grad, came, staged, staged_last, grads, parts_last,
    key_total, value_total, last_query_grad,
    send, recv, send_back, recv_back, send_last, recv_last, local, loaded,
):
    count, micros, _, rows, lanes = held.shape
    member, ahead = peers(count)
    wide = count * lanes
    scale = HEAD ** (-0.5)
    loads = [
        pltpu.make_async_copy(source, target, loaded.at[i])
        for i, (source, target) in enumerate(
            (
                (wdown, vdown),
                (wup, vup),
                (wproj, vproj),
                (wq, vqkv.at[0]),
                (wk, vqkv.at[1]),
                (wv, vqkv.at[2]),
            )
        )
    ]
    for load in loads:
        load.start()
    greet([{"group": peer} for peer in ahead])

    def out(m, j):
        return remote(
            grad_pack.at[ahead[j], m],
            came.at[member, m],
            send.at[m, j],
            recv.at[m, j],
            {"group": ahead[j]},
        )

    def back(m, j):
        return remote(
            staged.at[ahead[j], m],
            grads.at[member, m],
            send_back.at[m, j],
            recv_back.at[m, j],
            {"group": ahead[j]},
        )

    def back_last(m, j):
        return remote(
            staged_last.at[ahead[j], m],
            parts_last.at[member, m],
            send_last.at[m, j],
            recv_last.at[m, j],
            {"group": ahead[j]},
        )

    def own(m):
        return pltpu.make_async_copy(grad_pack.at[member, m], came.at[member, m], local.at[m, 0])

    def own_back(m):
        return (
            pltpu.make_async_copy(staged.at[member, m], grads.at[member, m], local.at[m, 1]),
            pltpu.make_async_copy(
                staged_last.at[member, m], parts_last.at[member, m], local.at[m, 2]
            ),
        )

    def column_sum(matrix):
        return jnp.sum(matrix.astype(jnp.float32), 0, keepdims=True)

    peer_range = range(count - 1)
    grad_two = grad_output[...].astype(jnp.bfloat16)
    vector_grads[7:8] = column_sum(grad_two)
    loads[0].wait()
    for first, size in column_chunks(pre_act.shape[1], 1152):
        columns = slice(first, first + size)
        value, slope = gelu_parts(pre_act[:, columns])
        activated[:, columns] = value.astype(jnp.bfloat16)
        part = (slope * over_lanes(grad_two, vdown[columns, :])).astype(jnp.bfloat16)
        grad_pre[:, columns] = part
        bias_grads[:, columns] = column_sum(part)
        if first == 0:
            loads[1].wait()
            grad_norm[...] = over_lanes(part, vup[:, columns])
        else:
            grad_norm[...] += over_lanes(part, vup[:, columns])
    unit, deviation = normalize(hidden[...])
    normed_two[...] = (unit * vectors[5:6] + vectors[6:7]).astype(jnp.bfloat16)
    from_norm, gain_sum, bias_sum = norm_back(unit, deviation, vectors[5:6], grad_norm[...])
    vector_grads[5:6] = gain_sum
    vector_grads[6:7] = bias_sum
    grad_hidden = grad_output[...] + from_norm
    grad_norm[...] = grad_hidden
    one = grad_hidden.astype(jnp.bfloat16)
    grad_one[...] = one
    vector_grads[4:5] = column_sum(one)
    loads[2].wait()
    grad_mixed = over_lanes(one, vproj[...]).astype(jnp.bfloat16)
    for m in range(micros):
        for d in range(count):
            grad_pack[d, m] = grad_mixed[m * rows : (m + 1) * rows, d * lanes : (d + 1) * lanes]
        for j in peer_range:
            out(m, j).start()
        own(m).start()
    wide_last = widen(grad_mixed[:, wide:], HEAD)
    for m in range(micros):
        last_grad[m] = wide_last[m * rows : (m + 1) * rows]

    def last_head(m):
        length = lengths[m]
        both = held_last[:, m].reshape(count * rows, lanes)
        probs = soft_columns(both, last_q[m], member * rows, length)
        grad_probs = over_lanes(both, last_grad[m])
        inner = jnp.sum(probs * grad_probs, 0, keepdims=True)
        grad_scores = (probs * (grad_probs - inner)).astype(jnp.bfloat16)
        query_grad = (scale * over_rows(both, grad_scores)).T.astype(jnp.bfloat16)
        grad_q[m * rows : (m + 1) * rows, wide:] = narrow(query_grad, 0)
        both_grad = scale * plain(grad_scores, last_q[m]) + plain(
            probs.astype(jnp.bfloat16), last_grad[m]
        )
        staged_last[:, m] = both_grad.astype(jnp.bfloat16).reshape(count, rows, lanes)
        for j in peer_range:
            back_last(m, j).start()

    def micro(m):
        length = lengths[m]
        own(m).wait()
        for j in peer_range:
            out(m, j).wait_recv()
        key_total[...] = jnp.zeros_like(key_total)
        value_total[...] = jnp.zeros_like(value_total)
        span = 2
        for block in range(count // span):
            reach = span * (block + 1)
            queries = held[span * block : reach, m, 0].reshape(span * rows, lanes)
            grad_out = came[span * block : reach, m].reshape(span * rows, lanes)
            key_rows = held[0:reach, m, 1].reshape(reach * rows, lanes)
            values = held[0:reach, m, 2].reshape(reach * rows, lanes)

            def head_step(head, total):
                head_queries, head_grad = one_head(queries, head), one_head(grad_out, head)
                probs = soft_columns(key_rows, head_queries, span * block * rows, length)
                grad_probs = over_lanes(values, head_grad)
                inner = jnp.sum(probs * grad_probs, 0, keepdims=True)
                grad_scores = (probs * (grad_probs - inner)).astype(jnp.bfloat16)
                value_total[0 : reach * rows] += plain(probs.astype(jnp.bfloat16), head_grad)
                key_total[0 : reach * rows] += plain(grad_scores, head_queries)
                return total + over_rows(one_head(key_rows, head), grad_scores)

            total = lax.fori_loop(0, 2, head_step, jnp.zeros((lanes, span * rows), jnp.float32))
            staged[span * block : reach, m, 0] = (
                (scale * total).T.astype(jnp.bfloat16).reshape(span, rows, lanes)
            )
        staged[:, m, 1] = (scale * key_total[...]).astype(jnp.bfloat16).reshape(count, rows, lanes)
        staged[:, m, 2] = value_total[...].astype(jnp.bfloat16).reshape(count, rows, lanes)
        for j in peer_range:
            back(m, j).start()
        for copy in own_back(m):
            copy.start()

    for m in range(micros):
        last_head(m)
    for m in range(micros):
        micro(m)
    unit, deviation = normalize(inputs[...])
    normed_one[...] = (unit * vectors[0:1] + vectors[1:2]).astype(jnp.bfloat16)
    for m in range(micros):
        here = slice(m * rows, (m + 1) * rows)
        for copy in own_back(m):
            copy.wait()
        for j in peer_range:
            back_last(m, j).wait_recv()
            back(m, j).wait_recv()
        last = jnp.sum(parts_last[:, m].astype(jnp.float32), 0).astype(jnp.bfloat16)
        grad_k[here, wide:] = narrow(last, 0)
        grad_v[here, wide:] = narrow(last, HEAD)
        for third, target in enumerate((grad_q, grad_k, grad_v)):
            for d in range(count):
                target[here, d * lanes : (d + 1) * lanes] = grads[d, m, third]
    vector_grads[2:3] = column_sum(grad_q[...])
    vector_grads[3:4] = column_sum(grad_v[...])
    for i in (3, 4, 5):
        loads[i].wait()
    pulled = over_lanes(grad_q[...], vqkv[0])
    pulled += over_lanes(grad_k[...], vqkv[1])
    pulled += over_lanes(grad_v[...], vqkv[2])
    from_norm, gain_sum, bias_sum = norm_back(unit, deviation, vectors[0:1], pulled)
    vector_grads[0:1] = gain_sum
    vector_grads[1:2] = bias_sum
    grad_in[...] = grad_norm[...] + from_norm
    for m in range(micros):
        for j in peer_range:
            out(m, j).wait_send()
            back_last(m, j).wait_send()
            back(m, j).wait_send()


def backward_layer(lengths, grad_output, saved, vectors, weights):
    inputs, hidden, pre_act, held, held_last, last_q = saved
    count, micros, _, rows, lanes = held.shape
    total, width = inputs.shape
    bf16, f32 = jnp.bfloat16, jnp.float32
    vmem, hbm = pl.BlockSpec(memory_space=pltpu.VMEM), pl.BlockSpec(memory_space=pl.ANY)
    dma = pltpu.SemaphoreType.DMA
    narrow_out, wide_out = (total, width), pre_act.shape
    blocks, pack = (count, micros, rows, lanes), (count, micros, 3, rows, lanes)
    return pl.pallas_call(
        backward_kernel,
        out_shape=[
            jax.ShapeDtypeStruct(shape, dtype)
            for shape, dtype in (
                (narrow_out, f32),
                (narrow_out, bf16),
                (narrow_out, bf16),
                (narrow_out, bf16),
                (narrow_out, bf16),
                (wide_out, bf16),
                (wide_out, bf16),
                (narrow_out, bf16),
                (narrow_out, bf16),
                ((8, width), f32),
                ((1, pre_act.shape[1]), f32),
            )
        ],
        in_specs=[pl.BlockSpec(memory_space=pltpu.SMEM)] + [vmem] * 8 + [hbm] * 6,
        out_specs=[vmem] * 11,
        scratch_shapes=[
            pltpu.VMEM(weights[3].shape, bf16),
            pltpu.VMEM(weights[4].shape, bf16),
            pltpu.VMEM(weights[5].shape, bf16),
            pltpu.VMEM((3,) + weights[0].shape, bf16),
            pltpu.VMEM(narrow_out, f32),
            pltpu.VMEM(blocks, bf16),
            pltpu.VMEM((micros, rows, lanes), bf16),
            pltpu.VMEM(blocks, bf16),
            pltpu.VMEM(pack, bf16),
            pltpu.VMEM(blocks, bf16),
            pltpu.VMEM(pack, bf16),
            pltpu.VMEM(blocks, bf16),
            pltpu.VMEM((count * rows, lanes), f32),
            pltpu.VMEM((count * rows, lanes), f32),
            pltpu.VMEM((micros, rows, lanes), bf16),
        ]
        + [dma((micros, count - 1))] * 6
        + [dma((micros, 3)), dma((6,))],
        compiler_params=pltpu.CompilerParams(
            collective_id=3, has_side_effects=True, vmem_limit_bytes=62 * 1024 * 1024
        ),
        name="backward_layer",
    )(lengths, grad_output, inputs, hidden, vectors, pre_act, held, held_last, last_q, *weights)


def outer_kernel(left, right, out):
    out[...] = over_rows(left[...], right[...]).astype(out.dtype)


def outer(left, right):
    rows, height = left.shape
    width = right.shape[1]
    tile = 256
    if height > width:
        grid = pl.cdiv(height, tile)
        specs = [
            pl.BlockSpec((rows, tile), lambda i: (0, i)),
            pl.BlockSpec((rows, width), lambda i: (0, 0)),
        ]
        out_spec = pl.BlockSpec((tile, width), lambda i: (i, 0))
    else:
        grid = pl.cdiv(width, tile)
        specs = [
            pl.BlockSpec((rows, height), lambda i: (0, 0)),
            pl.BlockSpec((rows, tile), lambda i: (0, i)),
        ]
        out_spec = pl.BlockSpec((height, tile), lambda i: (0, i))
    return pl.pallas_call(
        outer_kernel,
        grid=(grid,),
        out_shape=jax.ShapeDtypeStruct((height, width), jnp.bfloat16),
        in_specs=specs,
        out_specs=out_spec,
        compiler_params=pltpu.CompilerParams(vmem_limit_bytes=32 * 1024 * 1024),
        name="outer",
    )(left, right)


def in_blocks(matrix):
    return matrix.reshape(matrix.shape[0] // 8, 8, matrix.shape[1])


def body(
    block_input, out_grad, w_qkv, w_proj, w_up, w_down, vectors, b_up, seq_lengths, slot_of_seq
):
    section = lax.axis_index("pipe")
    replica = lax.axis_index("rep")
    member = lax.axis_index("group")
    rep_count = lax.axis_size("rep")
    count = lax.axis_size("group")
    micros, rows, width = block_input.shape[0], block_input.shape[2], block_input.shape[3]
    slot_ids = jnp.arange(seq_lengths.shape[0], dtype=jnp.int32)
    slot_len = jnp.sum(
        seq_lengths[:, None] * (slot_of_seq[:, None] == slot_ids[None, :]).astype(jnp.int32), axis=0
    )
    mine = jnp.arange(micros, dtype=jnp.int32) * rep_count + replica
    lengths = jnp.sum(
        slot_len[None, :] * (slot_ids[None, :] == mine[:, None]).astype(jnp.int32), axis=1
    )
    query_pos = member * rows + jnp.arange(rows, dtype=jnp.int32)
    valid = (query_pos[None, :] < lengths[:, None]).astype(jnp.float32)[:, :, None]
    cotangent = (out_grad[:, 0].astype(jnp.float32) * valid).reshape(micros * rows, width)

    bias_rows = b_up.shape[1] // vectors.shape[2]
    small = jnp.concatenate(
        [
            vectors[0],
            b_up[0].reshape(bias_rows, -1),
            jnp.zeros((8 - bias_rows, vectors.shape[2]), vectors.dtype),
        ],
        0,
    )
    thirds = [w_qkv[0][:, i * width : (i + 1) * width] for i in range(3)]
    small_full, *full = gather_weights(
        [in_blocks(array) for array in (small, *thirds, w_proj[0], w_up[0], w_down[0])]
    )
    vector_rows = small_full[:, 0].transpose(1, 0, 2).reshape(8, width).astype(jnp.float32)
    up_bias = small_full[:, 1, :bias_rows].reshape(1, -1).astype(jnp.float32)
    weights = [array.reshape(-1, array.shape[-1]) for array in full]

    def forward(inputs):
        return forward_layer(lengths, inputs, vector_rows, up_bias, weights, count, micros)

    first_in = block_input[:, 0].reshape(micros * rows, width).astype(jnp.float32)
    first_out = forward(first_in)[0]
    arrived = lax.ppermute(first_out.astype(jnp.bfloat16), "pipe", [(0, 1)])
    inputs = jnp.where(section == 0, first_in, arrived.astype(jnp.float32))
    output, hidden, pre_act, attn_mixed, last_q, held, held_last = forward(inputs)
    saved = (inputs, hidden, pre_act, held, held_last, last_q)
    last_grad = backward_layer(lengths, cotangent, saved, vector_rows, weights)[0]
    arrived = lax.ppermute(last_grad.astype(jnp.bfloat16), "pipe", [(1, 0)])
    grad_output = jnp.where(section == 1, cotangent, arrived.astype(jnp.float32))
    (
        grad_in, grad_q, grad_k, grad_v, grad_one, grad_pre, activated, normed_one, normed_two,
        grad_vectors, grad_bias,
    ) = backward_layer(lengths, grad_output, saved, vector_rows, weights)

    def shards(matrix):
        return matrix.reshape(count, -1, 8, matrix.shape[-1])

    small_grads = jnp.concatenate(
        [
            grad_vectors.reshape(8, count, -1).transpose(1, 0, 2),
            grad_bias.reshape(count, bias_rows, -1),
            jnp.zeros((count, 24 - bias_rows, width // count), jnp.float32),
        ],
        1,
    ).reshape(count, RING, 8, width // count)
    grads = [
        shards(outer(activated, grad_output.astype(jnp.bfloat16))),
        shards(outer(normed_two, grad_pre)),
        shards(outer(normed_one, grad_q)),
        shards(outer(normed_one, grad_k)),
        shards(outer(normed_one, grad_v)),
        shards(outer(attn_mixed, grad_one)),
        small_grads,
    ]
    sums = sum_gradients(grads)
    down, up, grad_q, grad_k, grad_v, proj = (
        assemble(total, grad.shape[1]) for total, grad in zip(sums[:6], grads)
    )
    small_total = sums[6].reshape(RING * 8, -1)
    edges = jnp.where(section == 0, grad_in, output).reshape(1, micros, 1, rows, width)
    return (
        edges,
        jnp.concatenate([grad_q, grad_k, grad_v], 1)[None],
        proj[None],
        up[None],
        down[None],
        small_total[None, :8],
        small_total[8 : 8 + bias_rows].reshape(1, -1),
    )


def solution(mesh):
    in_specs = (
        P(None, "rep", "group", None),
        P(None, "rep", "group", None),
        P("pipe", "group", None),
        P("pipe", "group", None),
        P("pipe", "group", None),
        P("pipe", "group", None),
        P("pipe", None, "group"),
        P("pipe", "group"),
        P(),
        P(),
    )
    out_specs = (
        P("pipe", None, "rep", "group", None),
        P("pipe", "group", None),
        P("pipe", "group", None),
        P("pipe", "group", None),
        P("pipe", "group", None),
        P("pipe", None, "group"),
        P("pipe", "group"),
    )
    return jax.shard_map(body, mesh=mesh, in_specs=in_specs, out_specs=out_specs, check_vma=False)
```

```python
import functools
import jax
import jax.numpy as jnp
from jax import lax
from jax.experimental import pallas as pl
from jax.experimental.pallas import tpu as pltpu
from jax.sharding import PartitionSpec as P

HEAD = 64
LANES = 128
EPSILON = 1e-05
MASKED = -1e30
MESH = pl.DeviceIdType.MESH
RING = 4


def remote(src, dst, send_sem, recv_sem, device):
    return pltpu.make_async_remote_copy(
        src_ref=src,
        dst_ref=dst,
        send_sem=send_sem,
        recv_sem=recv_sem,
        device_id=device,
        device_id_type=MESH,
    )


def greet(devices):
    barrier = pltpu.get_barrier_semaphore()
    for device in devices:
        pl.semaphore_signal(barrier, inc=1, device_id=device, device_id_type=MESH)
    pl.semaphore_wait(barrier, len(devices))


def place():
    member, replica = lax.axis_index("group"), lax.axis_index("rep")
    return (member // 2, member % 2, replica // 2, replica % 2)


class Links:
    def __init__(self, send, recv):
        self.send, self.recv, self.used = send, recv, 0

    def channel(self, device):
        self.used += 1
        return Channel(self.send.at[self.used - 1], self.recv.at[self.used - 1], device)


class Channel:
    def __init__(self, send, recv, device):
        self.send_sem, self.recv_sem, self.device = send, recv, device

    def copy(self, src, dst):
        return remote(src, dst, self.send_sem, self.recv_sem, self.device)

    def send(self, src, dst):
        self.copy(src, dst).start()

    def sent(self, src):
        self.copy(src, src).wait_send()

    def came(self, dst):
        self.copy(dst, dst).wait_recv()


def near_devices():
    z, x, y, c = place()
    return {
        "above": {"group": 2 * ((z + 1) % RING) + x},
        "below": {"group": 2 * ((z + 3) % RING) + x},
        "partner": {"group": 2 * z + 1 - x},
        "sibling": {"rep": 2 * y + 1 - c},
        "next": {"rep": 2 * ((y + 1) % RING) + c},
        "last": {"rep": 2 * ((y + 3) % RING) + c},
    }


def gather_job(links, shard, full, first, size, spread):
    z, x, y, c = place()
    near = near_devices()
    xc = (x + c) % 2
    me = 2 * z + x
    base, above, below, across = (2 * ((z + k) % RING) + xc for k in (0, 1, 3, 2))
    piece = size // RING if spread else size
    low = piece - piece // 2
    finals = []

    def region(slot, owner, part=""):
        start = first + owner * piece if spread else first
        if part == "low":
            return full.at[slot, pl.ds(start, low)]
        if part == "high":
            return full.at[slot, pl.ds(start + low, piece - low)]
        return full.at[slot, pl.ds(start, piece)]

    def on_core(core, action):
        pl.when(c == core)(action)

    def always(action):
        action()

    def relay(channel, ref, run):
        run(lambda: channel.send(ref, ref))
        finals.append(lambda: run(lambda: channel.sent(ref)))

    def hand(slot, owner, run, part=""):
        channel = links.channel(near["sibling"])
        relay(channel, region(slot, owner, part), run)
        other = region(slot + 1 - 2 * xc, owner, part)
        get = (lambda action: on_core(0, action)) if run is not always else always
        finals.append(lambda: get(lambda: channel.came(other)))

    across_x = links.channel(near["partner"])
    up, down = links.channel(near["above"]), links.channel(near["below"])
    far_up, far_down = links.channel(near["above"]), links.channel(near["below"])
    own = shard.at[pl.ds(first + y * piece if spread else first, piece)]
    second = lambda action: on_core(1, action)

    def first_core():
        up.send(own, region(base, y))
        down.send(own, region(base, y))

    if spread:
        on_core(0, first_core)
    on_core(1, lambda: across_x.send(own, region(me, y)))
    finals.append(lambda: on_core(1, lambda: across_x.sent(own)))
    finals.append(lambda: up.sent(own))
    finals.append(lambda: down.sent(own))
    yield

    rings = []

    def pass_on(slot, run):
        if spread:
            forth, back = links.channel(near["next"]), links.channel(near["last"])
            relay(forth, region(slot, y), run)
            relay(back, region(slot, y), run)
            rings.append((slot, run, forth, back))
        hand(slot, y, run)

    def second_core():
        across_x.came(region(base, y))
        up.send(region(base, y), region(base, y))
        down.send(region(base, y), region(base, y))

    if not spread:
        on_core(0, first_core)
    on_core(1, second_core)
    pass_on(base, second)
    yield

    up.came(region(below, y))
    relay(far_up, region(below, y, "low"), always)
    pass_on(below, always)
    down.came(region(above, y))
    if piece > low:
        relay(far_down, region(above, y, "high"), always)
    pass_on(above, always)
    yield

    far_up.came(region(across, y, "low"))
    if piece > low:
        far_down.came(region(across, y, "high"))
    pass_on(across, always)
    yield

    if spread:
        ends = []
        for slot, run, forth, back in rings:
            far_forth, far_back = links.channel(near["next"]), links.channel(near["last"])
            behind, ahead = (y + 3) % RING, (y + 1) % RING
            run(lambda: forth.came(region(slot, behind)))
            relay(far_forth, region(slot, behind, "low"), run)
            hand(slot, behind, run)
            run(lambda: back.came(region(slot, ahead)))
            if piece > low:
                relay(far_back, region(slot, ahead, "high"), run)
            hand(slot, ahead, run)
            ends.append((slot, run, far_forth, far_back))
        yield
        for slot, run, far_forth, far_back in ends:
            far = (y + 2) % RING
            run(lambda: far_forth.came(region(slot, far, "low")))
            if piece > low:
                run(lambda: far_back.came(region(slot, far, "high")))
            hand(slot, far, run)
        yield
    for action in finals:
        action()


MAX_LINKS = 160


ORDER = "SPSSSPSPSP"


def gather_kernel(plan, count, *refs):
    ins, outs = refs[:count], refs[count : 2 * count]
    links = Links(*refs[2 * count :])
    member = lax.axis_index("group")
    greet(list(near_devices().values()))
    spread = [gather_job(links, ins[i], outs[i], *rest) for i, *rest in plan if rest[-1]]
    whole = [gather_job(links, ins[i], outs[i], *rest) for i, *rest in plan if not rest[-1]]
    owns = [links.channel(near_devices()["sibling"]) for _ in range(count)]
    for step, which in enumerate(ORDER):
        for job in spread if which == "S" else whole:
            next(job)
        if step == 1:
            for i in range(count):
                owns[i].send(ins[i], outs[i].at[member])
    for job in spread + whole:
        for _ in job:
            pass
    for i in range(count):
        owns[i].came(outs[i].at[member])
        owns[i].sent(ins[i])


def gather_weights(shards, plan):
    count = len(shards)
    dma = pltpu.SemaphoreType.DMA
    return pl.pallas_call(
        functools.partial(gather_kernel, plan, count),
        out_shape=[jax.ShapeDtypeStruct((8,) + s.shape, s.dtype) for s in shards],
        in_specs=[pl.BlockSpec(memory_space=pl.ANY)] * count,
        out_specs=[pl.BlockSpec(memory_space=pl.ANY)] * count,
        scratch_shapes=[dma((MAX_LINKS,)), dma((MAX_LINKS,))],
        compiler_params=pltpu.CompilerParams(collective_id=0, has_side_effects=True),
        name="gather_weights",
    )(*shards)


def piece_rows(blocks):
    starts = [i * blocks // RING for i in range(RING + 1)]
    return max(starts[i + 1] - starts[i] for i in range(RING))


def add_blocks(count, dst, terms):
    def step(b, carry):
        total = dst[b].astype(jnp.float32)
        for term in terms:
            total = total + term[b].astype(jnp.float32)
        dst[b] = total.astype(dst.dtype)
        return carry

    lax.fori_loop(0, count, step, 0)


TILE = 256


def product_into(left, right, whole, stage, sems):
    def copy(tile, first, size):
        src = stage.at[tile % 2, pl.ds(0, size // 8)]
        return pltpu.make_async_copy(src, whole.at[pl.ds(first // 8, size // 8)], sems.at[tile % 2])

    tiles = [(t, *chunk) for t, chunk in enumerate(column_chunks(left.shape[1], TILE))]
    for t, first, size in tiles:
        if t >= 2:
            copy(*tiles[t - 2]).wait()
        for column, width in column_chunks(right.shape[1], 1152):
            tile = over_rows(left[:, first : first + size], right[:, column : column + width])
            stage[t % 2, 0 : size // 8, :, column : column + width] = tile.reshape(
                size // 8, 8, width
            ).astype(stage.dtype)
        copy(t, first, size).start()
    for tile in tiles[-2:]:
        copy(*tile).wait()


def sum_job(links, fill, whole, blocks, spread, total, stage, loads, buffers, out, kept):
    z, x, y, c = place()
    near = near_devices()
    xc = (x + c) % 2
    cross_core = {"group": 2 * z + 1 - x, "rep": 2 * y + 1 - c}
    others = [{"rep": 2 * ((y + j) % RING) + c} for j in range(1, RING)]
    far_low, far_high, from_below, from_above, cross = buffers[:5]
    size = blocks // RING if spread else blocks
    first = y * size if spread else 0
    low = size // 2
    order = (2, 1, 3, 0)
    finals = []

    def on_core(core, action):
        def run():
            action()

        pl.when(c == core)(run)

    def launch(device, src, dst):
        channel = links.channel(device)
        channel.send(src, dst)
        finals.append(lambda: channel.sent(src))
        return channel

    def shard(k, column):
        return whole.at[pl.ds((2 * ((z + k) % RING) + column) * blocks, blocks)]

    def rows(k, start, count):
        return total.at[k, pl.ds(start, count)]

    fill()
    swaps = [launch(near["sibling"], shard(k, 1 - xc), total.at[k]) for k in order]
    yield

    def load(n):
        return pltpu.make_async_copy(shard(order[n], xc), stage.at[n % 2], loads.at[n % 2])

    def send_far():
        up = launch(near["above"], rows(2, first, low), far_low)
        down = launch(near["below"], rows(2, first + low, size - low), far_high)
        return (up, down)

    load(0).start()
    load(1).start()
    for n, k in enumerate(order):
        load(n).wait()
        swaps[n].came(total.at[k])
        add_blocks(blocks, total.at[k], [stage.at[n % 2]])
        if n + 2 < RING:
            load(n + 2).start()
        if k == 2 and not spread:
            far = send_far()
    if spread:
        ring_low, ring_high, from_last, from_next = buffers[5:9]
        ahead, behind, opposite = ((y + j) % RING * size for j in (1, 3, 2))

        def quarter(start, count):
            return total.at[:, pl.ds(start, count)]

        forth = launch(near["next"], quarter(opposite, low), ring_low)
        back = launch(near["last"], quarter(opposite + low, size - low), ring_high)
        yield
        forth.came(ring_low)
        for k in range(RING):
            add_blocks(low, rows(k, ahead, low), [ring_low.at[k]])
        forth = launch(near["next"], quarter(ahead, size), from_last)
        back.came(ring_high)
        for k in range(RING):
            add_blocks(size - low, rows(k, behind + low, size - low), [ring_high.at[k]])
        back = launch(near["last"], quarter(behind, size), from_next)
        yield
        forth.came(from_last)
        back.came(from_next)
        for k in order:
            add_blocks(size, rows(k, first, size), [from_last.at[k], from_next.at[k]])
            if k == 2:
                far = send_far()
    yield
    far[0].came(far_low)
    add_blocks(low, rows(1, first, low), [far_low])
    up = launch(near["above"], rows(1, first, size), from_below)
    far[1].came(far_high)
    add_blocks(size - low, rows(3, first + low, size - low), [far_high])
    down = launch(near["below"], rows(3, first, size), from_above)
    yield
    up.came(from_below)
    down.came(from_above)
    mine = rows(0, first, size)
    add_blocks(size, mine, [from_below, from_above])
    over_x = links.channel(cross_core)
    on_core(1, lambda: over_x.send(mine, cross))
    finals.append(lambda: on_core(1, lambda: over_x.sent(mine)))
    yield

    def take_x():
        over_x.came(cross)
        add_blocks(size, mine, [cross])

    on_core(0, take_x)
    if spread:
        result = mine
    else:
        ring, result = buffers[5:7]
        piece = result.shape[0]
        over_y = [links.channel(device) for device in others]

        def part(owner):
            return total.at[0, pl.ds((owner * blocks) // RING, piece)]

        def send_y():
            for j in (2, 1, 3):
                over_y[j - 1].send(part((y + j) % RING), ring.at[j - 1])

        on_core(0, send_y)
        finals.append(
            lambda: on_core(0, lambda: [over_y[j].sent(part((y + j + 1) % RING)) for j in range(3)])
        )
        yield

        def take_y():
            for j in range(RING - 1):
                over_y[j].came(ring.at[j])
            own = part(y)

            def step(b, carry):
                value = own[b].astype(jnp.float32)
                for j in range(RING - 1):
                    value = value + ring[j, b].astype(jnp.float32)
                result[b] = value.astype(result.dtype)
                return carry

            lax.fori_loop(0, piece, step, 0)

        on_core(0, take_y)
    shares = [links.channel(device) for device in others]
    keep = pltpu.make_async_copy(result, out.at[y], kept)

    def share():
        for j in (2, 1, 3):
            shares[j - 1].send(result, out.at[y])
        keep.start()

    on_core(0, share)
    finals.append(lambda: on_core(0, lambda: [channel.sent(result) for channel in shares]))
    yield
    hand = links.channel(near["sibling"])

    def pass_on():
        keep.wait()
        for j in (1, 2, 3):
            shares[j - 1].came(out.at[(y + RING - j) % RING])
        hand.send(out, out)

    on_core(0, pass_on)
    finals.append(lambda: on_core(0, lambda: hand.sent(out)))
    yield
    on_core(1, lambda: hand.came(out))
    for action in finals:
        action()


SUM_LINKS = 160


def sum_kernel(shapes, *refs):
    operands, refs = refs[: SUM_OPERANDS], refs[SUM_OPERANDS:]
    count = len(shapes)
    outs, refs = refs[:count], refs[count:]
    filled = sum(1 for shape in shapes if shape[1] is not None)
    wholes, refs = list(refs[:filled]), refs[filled:]
    send, recv, kept, sems, loads = refs[:5]
    narrow_fill, wide_fill, narrow_stage, wide_stage, tall_stage, small_stage = refs[5:11]
    refs = refs[11:]
    links = Links(send, recv)
    z, x, y, c = place()
    near = near_devices()
    greet(
        [near["above"], near["below"], near["sibling"]]
        + [{"group": 2 * z + 1 - x, "rep": 2 * y + 1 - c}]
        + [{"rep": 2 * ((y + j) % RING) + c} for j in range(1, RING)]
    )
    jobs = []
    for i, (left, right, blocks, spread, offset) in enumerate(shapes):
        buffers, refs = refs[:10], refs[10:]
        stage = narrow_stage
        if right is None:
            whole, stage, fill = operands[left], small_stage, (lambda: None)
        else:
            whole = wholes.pop(0)
            space = narrow_fill
            if outs[i].shape[-1] > 2048:
                space, stage = wide_fill, wide_stage
            elif spread:
                stage = tall_stage
            fill = functools.partial(
                product_into, operands[left], operands[right], whole, space, sems
            )
        job = sum_job(
            links, fill, whole, blocks, spread, buffers[0], stage, loads, buffers[1:], outs[i], kept.at[i]
        )
        jobs.append((offset, job))
    tick = 0
    while jobs:
        alive = []
        for offset, job in jobs:
            if offset == tick:
                next(job)
        for offset, job in jobs:
            if offset >= tick:
                alive.append((offset, job))
                continue
            try:
                next(job)
                alive.append((offset, job))
            except StopIteration:
                pass
        jobs = alive
        tick += 1


SUM_OPERANDS = 11


def sum_gradients(operands, shapes):
    dma, vmem, hbm = pltpu.SemaphoreType.DMA, pl.BlockSpec(memory_space=pltpu.VMEM), pl.BlockSpec(memory_space=pl.ANY)
    bf16 = jnp.bfloat16
    count = len(shapes)
    outs, wholes, scratch = [], [], []
    narrow_width = min(operands[right].shape[1] for _, right, *_ in shapes if right is not None)
    wide_width = max(operands[right].shape[1] for _, right, *_ in shapes if right is not None)
    for left, right, blocks, spread, _ in shapes:
        if right is None:
            width, dtype = operands[left].shape[-1], operands[left].dtype
        else:
            width, dtype = operands[right].shape[1], bf16
            wholes.append(jax.ShapeDtypeStruct((8 * blocks, 8, width), dtype))
        piece = piece_rows(blocks)
        outs.append(jax.ShapeDtypeStruct((RING, piece, 8, width), dtype))
        size = blocks // RING if spread else blocks
        low = size // 2
        leads = [(RING, blocks), (low,), (size - low,), (size,), (size,), (size,)]
        if spread:
            leads += [(RING, low), (RING, size - low), (RING, size), (RING, size)]
        else:
            leads += [(RING - 1, piece), (piece,), (1,), (1,)]
        scratch += [pltpu.VMEM(lead + (8, width), dtype) for lead in leads]
    blocks = {spread: b for _, right, b, spread, _ in shapes if right is not None}
    small_shape = operands[-1].shape
    return pl.pallas_call(
        functools.partial(sum_kernel, shapes),
        out_shape=outs + wholes,
        in_specs=[vmem] * (len(operands) - 1) + [hbm],
        out_specs=[hbm] * (count + len(wholes)),
        scratch_shapes=[
            dma((SUM_LINKS,)),
            dma((SUM_LINKS,)),
            dma((count,)),
            dma((2,)),
            dma((2,)),
            pltpu.VMEM((2, TILE // 8, 8, narrow_width), bf16),
            pltpu.VMEM((2, TILE // 8, 8, wide_width), bf16),
            pltpu.VMEM((2, blocks[False], 8, narrow_width), bf16),
            pltpu.VMEM((2, blocks[False], 8, wide_width), bf16),
            pltpu.VMEM((2, blocks[True], 8, narrow_width), bf16),
            pltpu.VMEM((2, small_shape[0] // 8) + small_shape[1:], operands[-1].dtype),
        ]
        + scratch,
        compiler_params=pltpu.CompilerParams(
            collective_id=1, has_side_effects=True, vmem_limit_bytes=62 * 1024 * 1024
        ),
        name="sum_gradients",
    )(*operands)[:count]


def assemble(pieces, blocks):
    starts = [i * blocks // RING for i in range(RING + 1)]
    joined = jnp.concatenate(
        [pieces[i, : starts[i + 1] - starts[i]] for i in range(RING)], 0
    ).astype(jnp.float32)
    return joined.reshape(-1, pieces.shape[-1])


def lane_head(shape):
    return lax.broadcasted_iota(jnp.int32, shape, len(shape) - 1) // HEAD


def one_head(matrix, head):
    return jnp.where(lane_head(matrix.shape) == head, matrix, jnp.zeros_like(matrix))


def over_lanes(left, right):
    return lax.dot_general(left, right, (((1,), (1,)), ((), ())), preferred_element_type=jnp.float32)


def over_rows(left, right):
    return lax.dot_general(left, right, (((0,), (0,)), ((), ())), preferred_element_type=jnp.float32)


def plain(left, right):
    return jnp.dot(left, right, preferred_element_type=jnp.float32)


def half_selector(first):
    rows = lax.broadcasted_iota(jnp.int32, (HEAD, LANES), 0)
    lanes = lax.broadcasted_iota(jnp.int32, (HEAD, LANES), 1)
    return (rows + first == lanes).astype(jnp.bfloat16)


def widen(matrix, first):
    return plain(matrix, half_selector(first)).astype(jnp.bfloat16)


def narrow(matrix, first):
    return over_lanes(matrix, half_selector(first)).astype(jnp.bfloat16)


def soft_columns(key_rows, queries, first_query, length):
    scores = over_lanes(key_rows, queries) * HEAD ** (-0.5)
    key_pos = lax.broadcasted_iota(jnp.int32, scores.shape, 0)
    query_pos = first_query + lax.broadcasted_iota(jnp.int32, scores.shape, 1)
    scores = jnp.where((key_pos <= query_pos) & (key_pos < length), scores, MASKED)
    exponent = jnp.exp(scores - jnp.max(scores, 0, keepdims=True))
    return exponent * (1.0 / jnp.sum(exponent, 0, keepdims=True))


def peers(count):
    member = lax.axis_index("group")
    ahead = [(member + j) % count for j in range(1, count)]
    return (member, ahead)


def normalize(inputs):
    average = jnp.mean(inputs, -1, keepdims=True)
    centered = inputs - average
    variance = jnp.mean(centered * centered, -1, keepdims=True)
    scale = lax.rsqrt(variance + EPSILON)
    return (centered * scale, scale)


def norm_back(unit, scale, gain, grad):
    scaled = grad * gain
    pulled = scaled - jnp.mean(scaled, -1, keepdims=True)
    pulled = pulled - unit * jnp.mean(scaled * unit, -1, keepdims=True)
    return (
        pulled * scale,
        jnp.sum(grad * unit, 0, keepdims=True),
        jnp.sum(grad, 0, keepdims=True),
    )


GELU_IN, GELU_CUBE = 0.7978845608028654, 0.044715


def gelu_parts(value):
    square = value * value
    bent = jnp.tanh(GELU_IN * value * (1.0 + GELU_CUBE * square))
    half = 0.5 * (1.0 + bent)
    slope = half + 0.5 * value * (1.0 - bent * bent) * GELU_IN * (1.0 + 3.0 * GELU_CUBE * square)
    return (value * half, slope)


def column_chunks(width, most):
    return [(first, min(most, width - first)) for first in range(0, width, most)]


FORWARD_WEIGHTS = ("q", "k", "v", "proj", "up", "down")


def forward_kernel(
    lengths, inputs, vectors, up_bias, wq, wk, wv, wproj, wup, wdown,
    output, hidden_out, pre_act, attn_mixed, last_q, kept, kept_last,
    vq, vk, vv, vproj, vup, vdown, pack, last_kv, held, held_last, staged, mixed,
    send, recv, send_last, recv_last, send_back, recv_back, local, loaded,
):
    count, micros, _, rows, lanes = pack.shape
    member, ahead = peers(count)
    wide = count * lanes
    sources, places = (wq, wk, wv, wproj, wup, wdown), (vq, vk, vv, vproj, vup, vdown)
    loads = [
        pltpu.make_async_copy(sources[i], places[i], loaded.at[i]) for i in range(len(sources))
    ]
    for load in loads:
        load.start()
    greet([{"group": peer} for peer in ahead])

    def out(m, j):
        return remote(
            pack.at[ahead[j], m], held.at[member, m], send.at[m, j], recv.at[m, j], {"group": ahead[j]}
        )

    def out_last(m, j):
        return remote(
            last_kv.at[m],
            held_last.at[member, m],
            send_last.at[m, j],
            recv_last.at[m, j],
            {"group": ahead[j]},
        )

    def back(m, j):
        return remote(
            staged.at[ahead[j], m],
            mixed.at[member, m],
            send_back.at[m, j],
            recv_back.at[m, j],
            {"group": ahead[j]},
        )

    def own(m):
        return (
            pltpu.make_async_copy(pack.at[member, m], held.at[member, m], local.at[m, 0]),
            pltpu.make_async_copy(last_kv.at[m], held_last.at[member, m], local.at[m, 1]),
        )

    def own_back(m):
        return pltpu.make_async_copy(staged.at[member, m], mixed.at[member, m], local.at[m, 2])

    def keep():
        return (
            pltpu.make_async_copy(held, kept, local.at[0, 3]),
            pltpu.make_async_copy(held_last, kept_last, local.at[1, 3]),
        )

    peer_range = range(count - 1)
    unit, _ = normalize(inputs[...])
    normed = (unit * vectors[0:1] + vectors[1:2]).astype(jnp.bfloat16)
    lasts = []
    for third, (weight, bias) in enumerate(((vq, 2), (vk, None), (vv, 3))):
        loads[third].wait()
        product = plain(normed, weight[...])
        if bias is not None:
            product = product + vectors[bias : bias + 1]
        product = product.astype(jnp.bfloat16)
        for d in range(count):
            for m in range(micros):
                pack[d, m, third] = product[m * rows : (m + 1) * rows, d * lanes : (d + 1) * lanes]
        lasts.append(product[:, wide:])
    wide_q = widen(lasts[0], 0)
    both_last = widen(lasts[1], 0) + widen(lasts[2], HEAD)
    for m in range(micros):
        last_q[m] = wide_q[m * rows : (m + 1) * rows]
        last_kv[m] = both_last[m * rows : (m + 1) * rows]
    for m in range(micros):
        for j in peer_range:
            out(m, j).start()
            out_last(m, j).start()
        for copy in own(m):
            copy.start()

    def micro(m):
        for copy in own(m):
            copy.wait()
        for j in peer_range:
            out(m, j).wait_recv()
            out_last(m, j).wait_recv()
        length = lengths[m]
        span = 2
        for block in range(count // span):
            reach = span * (block + 1)
            queries = held[span * block : reach, m, 0].reshape(span * rows, lanes)
            key_rows = held[0:reach, m, 1].reshape(reach * rows, lanes)
            values = held[0:reach, m, 2].reshape(reach * rows, lanes)

            def head_step(head, total):
                probs = soft_columns(
                    key_rows, one_head(queries, head), span * block * rows, length
                ).astype(jnp.bfloat16)
                return total + over_rows(one_head(values, head), probs)

            total = lax.fori_loop(0, 2, head_step, jnp.zeros((lanes, span * rows), jnp.float32))
            staged[span * block : reach, m] = (
                total.T.astype(jnp.bfloat16).reshape(span, rows, lanes)
            )
        for j in peer_range:
            back(m, j).start()
        own_back(m).start()
        both = held_last[:, m].reshape(count * rows, lanes)
        probs = soft_columns(both, last_q[m], member * rows, length).astype(jnp.bfloat16)
        last_out = over_rows(both, probs).T.astype(jnp.bfloat16)
        attn_mixed[m * rows : (m + 1) * rows, wide:] = narrow(last_out, HEAD)

    for m in range(micros):
        micro(m)
    for copy in keep():
        copy.start()
    for m in range(micros):
        own_back(m).wait()
        for j in peer_range:
            back(m, j).wait_recv()
        for d in range(count):
            attn_mixed[m * rows : (m + 1) * rows, d * lanes : (d + 1) * lanes] = mixed[d, m]
    loads[3].wait()
    hidden = inputs[...] + plain(attn_mixed[...], vproj[...]) + vectors[4:5]
    hidden_out[...] = hidden
    unit, _ = normalize(hidden)
    normed = (unit * vectors[5:6] + vectors[6:7]).astype(jnp.bfloat16)
    output[...] = hidden + vectors[7:8]
    loads[4].wait()
    for first, size in column_chunks(pre_act.shape[1], 1152):
        columns = slice(first, first + size)
        value = plain(normed, vup[:, columns]) + up_bias[:, columns]
        pre_act[:, columns] = value
        activated, _ = gelu_parts(value)
        if first == 0:
            loads[5].wait()
        output[...] += plain(activated.astype(jnp.bfloat16), vdown[columns, :])
    for m in range(micros):
        for j in peer_range:
            out(m, j).wait_send()
            out_last(m, j).wait_send()
            back(m, j).wait_send()
    for copy in keep():
        copy.wait()


def forward_layer(lengths, inputs, vectors, up_bias, weights, count, micros):
    total, width = inputs.shape
    rows, lanes = total // micros, LANES
    hidden = weights[4].shape[1]
    bf16, f32 = jnp.bfloat16, jnp.float32
    vmem, hbm = pl.BlockSpec(memory_space=pltpu.VMEM), pl.BlockSpec(memory_space=pl.ANY)
    dma = pltpu.SemaphoreType.DMA
    pack, blocks = (count, micros, 3, rows, lanes), (count, micros, rows, lanes)
    return pl.pallas_call(
        forward_kernel,
        out_shape=[
            jax.ShapeDtypeStruct((total, width), f32),
            jax.ShapeDtypeStruct((total, width), f32),
            jax.ShapeDtypeStruct((total, hidden), f32),
            jax.ShapeDtypeStruct((total, width), bf16),
            jax.ShapeDtypeStruct((micros, rows, lanes), bf16),
            jax.ShapeDtypeStruct(pack, bf16),
            jax.ShapeDtypeStruct(blocks, bf16),
        ],
        in_specs=[pl.BlockSpec(memory_space=pltpu.SMEM)] + [vmem] * 3 + [hbm] * 6,
        out_specs=[vmem] * 5 + [hbm] * 2,
        scratch_shapes=[pltpu.VMEM(w.shape, bf16) for w in weights]
        + [
            pltpu.VMEM(pack, bf16),
            pltpu.VMEM((micros, rows, lanes), bf16),
            pltpu.VMEM(pack, bf16),
            pltpu.VMEM(blocks, bf16),
            pltpu.VMEM(blocks, bf16),
            pltpu.VMEM(blocks, bf16),
        ]
        + [dma((micros, count - 1))] * 6
        + [dma((micros, 4)), dma((6,))],
        compiler_params=pltpu.CompilerParams(
            collective_id=2, has_side_effects=True, vmem_limit_bytes=60 * 1024 * 1024
        ),
        name="forward_layer",
    )(lengths, inputs, vectors, up_bias, *weights)


def backward_kernel(
    lengths, grad_output, inputs, hidden, vectors, pre_act, held, held_last, last_q,
    wq, wk, wv, wproj, wup, wdown,
    grad_in, grad_q, grad_k, grad_v, grad_one, grad_pre, activated, normed_one, normed_two,
    vector_grads, bias_grads,
    vproj, vup, vdown, vqkv, grad_norm, grad_pack, last_grad, came, staged, staged_last, grads, parts_last,
    key_total, value_total, last_query_grad,
    send, recv, send_back, recv_back, send_last, recv_last, local, loaded,
):
    count, micros, _, rows, lanes = held.shape
    member, ahead = peers(count)
    wide = count * lanes
    scale = HEAD ** (-0.5)
    loads = [
        pltpu.make_async_copy(source, target, loaded.at[i])
        for i, (source, target) in enumerate(
            (
                (wdown, vdown),
                (wup, vup),
                (wproj, vproj),
                (wq, vqkv.at[0]),
                (wk, vqkv.at[1]),
                (wv, vqkv.at[2]),
            )
        )
    ]
    for load in loads:
        load.start()
    greet([{"group": peer} for peer in ahead])

    def out(m, j):
        return remote(
            grad_pack.at[ahead[j], m],
            came.at[member, m],
            send.at[m, j],
            recv.at[m, j],
            {"group": ahead[j]},
        )

    def back(m, j):
        return remote(
            staged.at[ahead[j], m],
            grads.at[member, m],
            send_back.at[m, j],
            recv_back.at[m, j],
            {"group": ahead[j]},
        )

    def back_last(m, j):
        return remote(
            staged_last.at[ahead[j], m],
            parts_last.at[member, m],
            send_last.at[m, j],
            recv_last.at[m, j],
            {"group": ahead[j]},
        )

    def own(m):
        return pltpu.make_async_copy(grad_pack.at[member, m], came.at[member, m], local.at[m, 0])

    def own_back(m):
        return (
            pltpu.make_async_copy(staged.at[member, m], grads.at[member, m], local.at[m, 1]),
            pltpu.make_async_copy(
                staged_last.at[member, m], parts_last.at[member, m], local.at[m, 2]
            ),
        )

    def column_sum(matrix):
        return jnp.sum(matrix.astype(jnp.float32), 0, keepdims=True)

    peer_range = range(count - 1)
    grad_two = grad_output[...].astype(jnp.bfloat16)
    vector_grads[7:8] = column_sum(grad_two)
    loads[0].wait()
    for first, size in column_chunks(pre_act.shape[1], 1152):
        columns = slice(first, first + size)
        value, slope = gelu_parts(pre_act[:, columns])
        activated[:, columns] = value.astype(jnp.bfloat16)
        part = (slope * over_lanes(grad_two, vdown[columns, :])).astype(jnp.bfloat16)
        grad_pre[:, columns] = part
        bias_grads[:, columns] = column_sum(part)
        if first == 0:
            loads[1].wait()
            grad_norm[...] = over_lanes(part, vup[:, columns])
        else:
            grad_norm[...] += over_lanes(part, vup[:, columns])
    unit, deviation = normalize(hidden[...])
    normed_two[...] = (unit * vectors[5:6] + vectors[6:7]).astype(jnp.bfloat16)
    from_norm, gain_sum, bias_sum = norm_back(unit, deviation, vectors[5:6], grad_norm[...])
    vector_grads[5:6] = gain_sum
    vector_grads[6:7] = bias_sum
    grad_hidden = grad_output[...] + from_norm
    grad_norm[...] = grad_hidden
    one = grad_hidden.astype(jnp.bfloat16)
    grad_one[...] = one
    vector_grads[4:5] = column_sum(one)
    loads[2].wait()
    grad_mixed = over_lanes(one, vproj[...]).astype(jnp.bfloat16)
    for m in range(micros):
        for d in range(count):
            grad_pack[d, m] = grad_mixed[m * rows : (m + 1) * rows, d * lanes : (d + 1) * lanes]
        for j in peer_range:
            out(m, j).start()
        own(m).start()
    wide_last = widen(grad_mixed[:, wide:], HEAD)
    for m in range(micros):
        last_grad[m] = wide_last[m * rows : (m + 1) * rows]

    def last_head(m):
        length = lengths[m]
        both = held_last[:, m].reshape(count * rows, lanes)
        probs = soft_columns(both, last_q[m], member * rows, length)
        grad_probs = over_lanes(both, last_grad[m])
        inner = jnp.sum(probs * grad_probs, 0, keepdims=True)
        grad_scores = (probs * (grad_probs - inner)).astype(jnp.bfloat16)
        query_grad = (scale * over_rows(both, grad_scores)).T.astype(jnp.bfloat16)
        grad_q[m * rows : (m + 1) * rows, wide:] = narrow(query_grad, 0)
        both_grad = scale * plain(grad_scores, last_q[m]) + plain(
            probs.astype(jnp.bfloat16), last_grad[m]
        )
        staged_last[:, m] = both_grad.astype(jnp.bfloat16).reshape(count, rows, lanes)
        for j in peer_range:
            back_last(m, j).start()

    def micro(m):
        length = lengths[m]
        own(m).wait()
        for j in peer_range:
            out(m, j).wait_recv()
        key_total[...] = jnp.zeros_like(key_total)
        value_total[...] = jnp.zeros_like(value_total)
        span = 2
        for block in range(count // span):
            reach = span * (block + 1)
            queries = held[span * block : reach, m, 0].reshape(span * rows, lanes)
            grad_out = came[span * block : reach, m].reshape(span * rows, lanes)
            key_rows = held[0:reach, m, 1].reshape(reach * rows, lanes)
            values = held[0:reach, m, 2].reshape(reach * rows, lanes)

            def head_step(head, total):
                head_queries, head_grad = one_head(queries, head), one_head(grad_out, head)
                probs = soft_columns(key_rows, head_queries, span * block * rows, length)
                grad_probs = over_lanes(values, head_grad)
                inner = jnp.sum(probs * grad_probs, 0, keepdims=True)
                grad_scores = (probs * (grad_probs - inner)).astype(jnp.bfloat16)
                value_total[0 : reach * rows] += plain(probs.astype(jnp.bfloat16), head_grad)
                key_total[0 : reach * rows] += plain(grad_scores, head_queries)
                return total + over_rows(one_head(key_rows, head), grad_scores)

            total = lax.fori_loop(0, 2, head_step, jnp.zeros((lanes, span * rows), jnp.float32))
            staged[span * block : reach, m, 0] = (
                (scale * total).T.astype(jnp.bfloat16).reshape(span, rows, lanes)
            )
        staged[:, m, 1] = (scale * key_total[...]).astype(jnp.bfloat16).reshape(count, rows, lanes)
        staged[:, m, 2] = value_total[...].astype(jnp.bfloat16).reshape(count, rows, lanes)
        for j in peer_range:
            back(m, j).start()
        for copy in own_back(m):
            copy.start()

    for m in range(micros):
        last_head(m)
    for m in range(micros):
        micro(m)
    unit, deviation = normalize(inputs[...])
    normed_one[...] = (unit * vectors[0:1] + vectors[1:2]).astype(jnp.bfloat16)
    for m in range(micros):
        here = slice(m * rows, (m + 1) * rows)
        for copy in own_back(m):
            copy.wait()
        for j in peer_range:
            back_last(m, j).wait_recv()
            back(m, j).wait_recv()
        last = jnp.sum(parts_last[:, m].astype(jnp.float32), 0).astype(jnp.bfloat16)
        grad_k[here, wide:] = narrow(last, 0)
        grad_v[here, wide:] = narrow(last, HEAD)
        for third, target in enumerate((grad_q, grad_k, grad_v)):
            for d in range(count):
                target[here, d * lanes : (d + 1) * lanes] = grads[d, m, third]
    vector_grads[2:3] = column_sum(grad_q[...])
    vector_grads[3:4] = column_sum(grad_v[...])
    for i in (3, 4, 5):
        loads[i].wait()
    pulled = over_lanes(grad_q[...], vqkv[0])
    pulled += over_lanes(grad_k[...], vqkv[1])
    pulled += over_lanes(grad_v[...], vqkv[2])
    from_norm, gain_sum, bias_sum = norm_back(unit, deviation, vectors[0:1], pulled)
    vector_grads[0:1] = gain_sum
    vector_grads[1:2] = bias_sum
    grad_in[...] = grad_norm[...] + from_norm
    for m in range(micros):
        for j in peer_range:
            out(m, j).wait_send()
            back_last(m, j).wait_send()
            back(m, j).wait_send()


def backward_layer(lengths, grad_output, saved, vectors, weights):
    inputs, hidden, pre_act, held, held_last, last_q = saved
    count, micros, _, rows, lanes = held.shape
    total, width = inputs.shape
    bf16, f32 = jnp.bfloat16, jnp.float32
    vmem, hbm = pl.BlockSpec(memory_space=pltpu.VMEM), pl.BlockSpec(memory_space=pl.ANY)
    dma = pltpu.SemaphoreType.DMA
    narrow_out, wide_out = (total, width), pre_act.shape
    blocks, pack = (count, micros, rows, lanes), (count, micros, 3, rows, lanes)
    return pl.pallas_call(
        backward_kernel,
        out_shape=[
            jax.ShapeDtypeStruct(shape, dtype)
            for shape, dtype in (
                (narrow_out, f32),
                (narrow_out, bf16),
                (narrow_out, bf16),
                (narrow_out, bf16),
                (narrow_out, bf16),
                (wide_out, bf16),
                (wide_out, bf16),
                (narrow_out, bf16),
                (narrow_out, bf16),
                ((8, width), f32),
                ((1, pre_act.shape[1]), f32),
            )
        ],
        in_specs=[pl.BlockSpec(memory_space=pltpu.SMEM)] + [vmem] * 8 + [hbm] * 6,
        out_specs=[vmem] * 11,
        scratch_shapes=[
            pltpu.VMEM(weights[3].shape, bf16),
            pltpu.VMEM(weights[4].shape, bf16),
            pltpu.VMEM(weights[5].shape, bf16),
            pltpu.VMEM((3,) + weights[0].shape, bf16),
            pltpu.VMEM(narrow_out, f32),
            pltpu.VMEM(blocks, bf16),
            pltpu.VMEM((micros, rows, lanes), bf16),
            pltpu.VMEM(blocks, bf16),
            pltpu.VMEM(pack, bf16),
            pltpu.VMEM(blocks, bf16),
            pltpu.VMEM(pack, bf16),
            pltpu.VMEM(blocks, bf16),
            pltpu.VMEM((count * rows, lanes), f32),
            pltpu.VMEM((count * rows, lanes), f32),
            pltpu.VMEM((micros, rows, lanes), bf16),
        ]
        + [dma((micros, count - 1))] * 6
        + [dma((micros, 3)), dma((6,))],
        compiler_params=pltpu.CompilerParams(
            collective_id=3, has_side_effects=True, vmem_limit_bytes=62 * 1024 * 1024
        ),
        name="backward_layer",
    )(lengths, grad_output, inputs, hidden, vectors, pre_act, held, held_last, last_q, *weights)


def in_blocks(matrix):
    return matrix.reshape(matrix.shape[0] // 8, 8, matrix.shape[1])


def body(
    block_input, out_grad, w_qkv, w_proj, w_up, w_down, vectors, b_up, seq_lengths, slot_of_seq
):
    section = lax.axis_index("pipe")
    replica = lax.axis_index("rep")
    member = lax.axis_index("group")
    rep_count = lax.axis_size("rep")
    count = lax.axis_size("group")
    micros, rows, width = block_input.shape[0], block_input.shape[2], block_input.shape[3]
    slot_ids = jnp.arange(seq_lengths.shape[0], dtype=jnp.int32)
    slot_len = jnp.sum(
        seq_lengths[:, None] * (slot_of_seq[:, None] == slot_ids[None, :]).astype(jnp.int32), axis=0
    )
    mine = jnp.arange(micros, dtype=jnp.int32) * rep_count + replica
    lengths = jnp.sum(
        slot_len[None, :] * (slot_ids[None, :] == mine[:, None]).astype(jnp.int32), axis=1
    )
    query_pos = member * rows + jnp.arange(rows, dtype=jnp.int32)
    valid = (query_pos[None, :] < lengths[:, None]).astype(jnp.float32)[:, :, None]
    cotangent = (out_grad[:, 0].astype(jnp.float32) * valid).reshape(micros * rows, width)

    bias_rows = b_up.shape[1] // vectors.shape[2]
    small = jnp.concatenate(
        [
            vectors[0],
            b_up[0].reshape(bias_rows, -1),
            jnp.zeros((8 - bias_rows, vectors.shape[2]), vectors.dtype),
        ],
        0,
    )
    thirds = [w_qkv[0][:, i * width : (i + 1) * width] for i in range(3)]
    small_full, *full = gather_weights(
        [in_blocks(array) for array in (small, *thirds, w_proj[0], w_up[0], w_down[0])],
        (
            (6, 0, 68, True),
            (5, 0, 16, True),
            (0, 0, 2, False),
            (1, 0, 17, False),
            (2, 0, 17, False),
            (3, 0, 17, False),
            (4, 0, 17, False),
            (5, 16, 1, False),
        ),
    )
    vector_rows = small_full[:, 0].transpose(1, 0, 2).reshape(8, width).astype(jnp.float32)
    up_bias = small_full[:, 1, :bias_rows].reshape(1, -1).astype(jnp.float32)
    weights = [array.reshape(-1, array.shape[-1]) for array in full]

    def forward(inputs):
        return forward_layer(lengths, inputs, vector_rows, up_bias, weights, count, micros)

    first_in = block_input[:, 0].reshape(micros * rows, width).astype(jnp.float32)
    first_out = forward(first_in)[0]
    arrived = lax.ppermute(first_out.astype(jnp.bfloat16), "pipe", [(0, 1)])
    inputs = jnp.where(section == 0, first_in, arrived.astype(jnp.float32))
    output, hidden, pre_act, attn_mixed, last_q, held, held_last = forward(inputs)
    saved = (inputs, hidden, pre_act, held, held_last, last_q)
    last_grad = backward_layer(lengths, cotangent, saved, vector_rows, weights)[0]
    arrived = lax.ppermute(last_grad.astype(jnp.bfloat16), "pipe", [(1, 0)])
    grad_output = jnp.where(section == 1, cotangent, arrived.astype(jnp.float32))
    (
        grad_in, grad_q, grad_k, grad_v, grad_one, grad_pre, activated, normed_one, normed_two,
        grad_vectors, grad_bias,
    ) = backward_layer(lengths, grad_output, saved, vector_rows, weights)

    small_grads = jnp.concatenate(
        [
            grad_vectors.reshape(8, count, -1).transpose(1, 0, 2),
            grad_bias.reshape(count, bias_rows, -1),
            jnp.zeros((count, 24 - bias_rows, width // count), jnp.float32),
        ],
        1,
    ).reshape(count * RING, 8, width // count)
    blocks = width // count // 8
    tall = grad_pre.shape[1] // count // 8
    sums = sum_gradients(
        (
            normed_one, grad_q, grad_k, grad_v, attn_mixed, grad_one, normed_two, grad_pre, activated,
            grad_output.astype(jnp.bfloat16), small_grads,
        ),
        (
            (0, 1, blocks, False, 0),
            (8, 9, tall, True, 0),
            (6, 7, blocks, False, 1),
            (0, 2, blocks, False, 2),
            (0, 3, blocks, False, 3),
            (4, 5, blocks, False, 4),
            (10, None, RING, False, 5),
        ),
    )
    grad_q, down, up, grad_k, grad_v, proj = (
        assemble(total, tall if i == 1 else blocks) for i, total in enumerate(sums[:6])
    )
    small_total = sums[6].reshape(RING * 8, -1)
    edges = jnp.where(section == 0, grad_in, output).reshape(1, micros, 1, rows, width)
    return (
        edges,
        jnp.concatenate([grad_q, grad_k, grad_v], 1)[None],
        proj[None],
        up[None],
        down[None],
        small_total[None, :8],
        small_total[8 : 8 + bias_rows].reshape(1, -1),
    )


def solution(mesh):
    in_specs = (
        P(None, "rep", "group", None),
        P(None, "rep", "group", None),
        P("pipe", "group", None),
        P("pipe", "group", None),
        P("pipe", "group", None),
        P("pipe", "group", None),
        P("pipe", None, "group"),
        P("pipe", "group"),
        P(),
        P(),
    )
    out_specs = (
        P("pipe", None, "rep", "group", None),
        P("pipe", "group", None),
        P("pipe", "group", None),
        P("pipe", "group", None),
        P("pipe", "group", None),
        P("pipe", None, "group"),
        P("pipe", "group"),
    )
    return jax.shard_map(body, mesh=mesh, in_specs=in_specs, out_specs=out_specs, check_vma=False)
```

```python
import functools
import jax
import jax.numpy as jnp
from jax import lax
from jax.experimental import pallas as pl
from jax.experimental.pallas import tpu as pltpu
from jax.sharding import PartitionSpec as P

HEAD = 64
LANES = 128
EPSILON = 1e-05
MASKED = -1e30
MESH = pl.DeviceIdType.MESH
RING = 4


def remote(src, dst, send_sem, recv_sem, device):
    return pltpu.make_async_remote_copy(
        src_ref=src,
        dst_ref=dst,
        send_sem=send_sem,
        recv_sem=recv_sem,
        device_id=device,
        device_id_type=MESH,
    )


def greet(devices):
    barrier = pltpu.get_barrier_semaphore()
    for device in devices:
        pl.semaphore_signal(barrier, inc=1, device_id=device, device_id_type=MESH)
    pl.semaphore_wait(barrier, len(devices))


def place():
    member, replica = lax.axis_index("group"), lax.axis_index("rep")
    return (member // 2, member % 2, replica // 2, replica % 2)


class Links:
    def __init__(self, send, recv):
        self.send, self.recv, self.used = send, recv, 0

    def channel(self, device):
        self.used += 1
        return Channel(self.send.at[self.used - 1], self.recv.at[self.used - 1], device)


class Channel:
    def __init__(self, send, recv, device):
        self.send_sem, self.recv_sem, self.device = send, recv, device

    def copy(self, src, dst):
        return remote(src, dst, self.send_sem, self.recv_sem, self.device)

    def send(self, src, dst):
        self.copy(src, dst).start()

    def sent(self, src):
        self.copy(src, src).wait_send()

    def came(self, dst):
        self.copy(dst, dst).wait_recv()


def near_devices():
    z, x, y, c = place()
    return {
        "above": {"group": 2 * ((z + 1) % RING) + x},
        "below": {"group": 2 * ((z + 3) % RING) + x},
        "partner": {"group": 2 * z + 1 - x},
        "sibling": {"rep": 2 * y + 1 - c},
        "next": {"rep": 2 * ((y + 1) % RING) + c},
        "last": {"rep": 2 * ((y + 3) % RING) + c},
    }


def gather_job(links, shard, full, first, size, spread):
    z, x, y, c = place()
    near = near_devices()
    xc = (x + c) % 2
    me = 2 * z + x
    base, above, below, across = (2 * ((z + k) % RING) + xc for k in (0, 1, 3, 2))
    piece = size // RING if spread else size
    low = piece - piece // 2
    finals = []

    def region(slot, owner, part=""):
        start = first + owner * piece if spread else first
        if part == "low":
            return full.at[slot, pl.ds(start, low)]
        if part == "high":
            return full.at[slot, pl.ds(start + low, piece - low)]
        return full.at[slot, pl.ds(start, piece)]

    def on_core(core, action):
        pl.when(c == core)(action)

    def always(action):
        action()

    def relay(channel, ref, run):
        run(lambda: channel.send(ref, ref))
        finals.append(lambda: run(lambda: channel.sent(ref)))

    def hand(slot, owner, run, part=""):
        channel = links.channel(near["sibling"])
        relay(channel, region(slot, owner, part), run)
        other = region(slot + 1 - 2 * xc, owner, part)
        get = (lambda action: on_core(0, action)) if run is not always else always
        finals.append(lambda: get(lambda: channel.came(other)))

    across_x = links.channel(near["partner"])
    up, down = links.channel(near["above"]), links.channel(near["below"])
    far_up, far_down = links.channel(near["above"]), links.channel(near["below"])
    own = shard.at[pl.ds(first + y * piece if spread else first, piece)]
    second = lambda action: on_core(1, action)

    def first_core():
        up.send(own, region(base, y))
        down.send(own, region(base, y))

    if spread:
        on_core(0, first_core)
    on_core(1, lambda: across_x.send(own, region(me, y)))
    finals.append(lambda: on_core(1, lambda: across_x.sent(own)))
    finals.append(lambda: up.sent(own))
    finals.append(lambda: down.sent(own))
    yield

    rings = []

    def pass_on(slot, run):
        if spread:
            forth, back = links.channel(near["next"]), links.channel(near["last"])
            relay(forth, region(slot, y), run)
            relay(back, region(slot, y), run)
            rings.append((slot, run, forth, back))
        hand(slot, y, run)

    def second_core():
        across_x.came(region(base, y))
        up.send(region(base, y), region(base, y))
        down.send(region(base, y), region(base, y))

    if not spread:
        on_core(0, first_core)
    on_core(1, second_core)
    pass_on(base, second)
    yield

    up.came(region(below, y))
    relay(far_up, region(below, y, "low"), always)
    pass_on(below, always)
    down.came(region(above, y))
    if piece > low:
        relay(far_down, region(above, y, "high"), always)
    pass_on(above, always)
    yield

    far_up.came(region(across, y, "low"))
    if piece > low:
        far_down.came(region(across, y, "high"))
    pass_on(across, always)
    yield

    if spread:
        ends = []
        for slot, run, forth, back in rings:
            far_forth, far_back = links.channel(near["next"]), links.channel(near["last"])
            behind, ahead = (y + 3) % RING, (y + 1) % RING
            run(lambda: forth.came(region(slot, behind)))
            relay(far_forth, region(slot, behind, "low"), run)
            hand(slot, behind, run)
            run(lambda: back.came(region(slot, ahead)))
            if piece > low:
                relay(far_back, region(slot, ahead, "high"), run)
            hand(slot, ahead, run)
            ends.append((slot, run, far_forth, far_back))
        yield
        for slot, run, far_forth, far_back in ends:
            far = (y + 2) % RING
            run(lambda: far_forth.came(region(slot, far, "low")))
            if piece > low:
                run(lambda: far_back.came(region(slot, far, "high")))
            hand(slot, far, run)
        yield
    for action in finals:
        action()


MAX_LINKS = 160


ORDER = "SPSSSPSPSP"


def gather_kernel(plan, count, *refs):
    ins, outs = refs[:count], refs[count : 2 * count]
    links = Links(*refs[2 * count :])
    member = lax.axis_index("group")
    greet(list(near_devices().values()))
    spread = [gather_job(links, ins[i], outs[i], *rest) for i, *rest in plan if rest[-1]]
    whole = [gather_job(links, ins[i], outs[i], *rest) for i, *rest in plan if not rest[-1]]
    owns = [links.channel(near_devices()["sibling"]) for _ in range(count)]
    for step, which in enumerate(ORDER):
        for job in spread if which == "S" else whole:
            next(job)
        if step == 1:
            for i in range(count):
                owns[i].send(ins[i], outs[i].at[member])
    for job in spread + whole:
        for _ in job:
            pass
    for i in range(count):
        owns[i].came(outs[i].at[member])
        owns[i].sent(ins[i])


def gather_weights(shards, plan):
    count = len(shards)
    dma = pltpu.SemaphoreType.DMA
    return pl.pallas_call(
        functools.partial(gather_kernel, plan, count),
        out_shape=[jax.ShapeDtypeStruct((8,) + s.shape, s.dtype) for s in shards],
        in_specs=[pl.BlockSpec(memory_space=pl.ANY)] * count,
        out_specs=[pl.BlockSpec(memory_space=pl.ANY)] * count,
        scratch_shapes=[dma((MAX_LINKS,)), dma((MAX_LINKS,))],
        compiler_params=pltpu.CompilerParams(collective_id=0, has_side_effects=True),
        name="gather_weights",
    )(*shards)


def piece_rows(blocks):
    starts = [i * blocks // RING for i in range(RING + 1)]
    return max(starts[i + 1] - starts[i] for i in range(RING))


def add_blocks(count, dst, terms):
    def step(b, carry):
        total = dst[b].astype(jnp.float32)
        for term in terms:
            total = total + term[b].astype(jnp.float32)
        dst[b] = total.astype(dst.dtype)
        return carry

    lax.fori_loop(0, count, step, 0)


TILE = 256


def product_into(left, right, whole, stage, sems):
    def copy(tile, first, size):
        src = stage.at[tile % 2, pl.ds(0, size // 8)]
        return pltpu.make_async_copy(src, whole.at[pl.ds(first // 8, size // 8)], sems.at[tile % 2])

    tiles = [(t, *chunk) for t, chunk in enumerate(column_chunks(left.shape[1], TILE))]
    for t, first, size in tiles:
        if t >= 2:
            copy(*tiles[t - 2]).wait()
        for column, width in column_chunks(right.shape[1], 1152):
            tile = over_rows(left[:, first : first + size], right[:, column : column + width])
            stage[t % 2, 0 : size // 8, :, column : column + width] = tile.reshape(
                size // 8, 8, width
            ).astype(stage.dtype)
        copy(t, first, size).start()
    for tile in tiles[-2:]:
        copy(*tile).wait()


def sum_job(links, fill, whole, chunk, spread, total, stage, loads, buffers, out, kept):
    z, x, y, c = place()
    near = near_devices()
    shard_blocks, chunk_first, blocks = chunk
    xc = (x + c) % 2
    cross_core = {"group": 2 * z + 1 - x, "rep": 2 * y + 1 - c}
    others = [{"rep": 2 * ((y + j) % RING) + c} for j in range(1, RING)]
    far_low, far_high, from_below, from_above, cross = buffers[:5]
    size = blocks // RING if spread else blocks
    first = y * size if spread else 0
    low = size // 2
    order = (2, 1, 3, 0)
    finals = []

    def on_core(core, action):
        def run():
            action()

        pl.when(c == core)(run)

    def launch(device, src, dst):
        channel = links.channel(device)
        channel.send(src, dst)
        finals.append(lambda: channel.sent(src))
        return channel

    def shard(k, column):
        slot = 2 * ((z + k) % RING) + column
        return whole.at[pl.ds(slot * shard_blocks + chunk_first, blocks)]

    def rows(k, start, count):
        return total.at[k, pl.ds(start, count)]

    fill()
    swaps = [launch(near["sibling"], shard(k, 1 - xc), total.at[k]) for k in order]
    yield

    def load(n):
        space = stage.at[n % 2, pl.ds(0, blocks)]
        return pltpu.make_async_copy(shard(order[n], xc), space, loads.at[n % 2])

    def send_far():
        up = launch(near["above"], rows(2, first, low), far_low)
        down = launch(near["below"], rows(2, first + low, size - low), far_high)
        return (up, down)

    load(0).start()
    load(1).start()
    for n, k in enumerate(order):
        load(n).wait()
        swaps[n].came(total.at[k])
        add_blocks(blocks, total.at[k], [stage.at[n % 2]])
        if n + 2 < RING:
            load(n + 2).start()
        if k == 2 and not spread:
            far = send_far()
    if spread:
        ring_low, ring_high, from_last, from_next = buffers[5:9]
        ahead, behind, opposite = ((y + j) % RING * size for j in (1, 3, 2))

        def quarter(start, count):
            return total.at[:, pl.ds(start, count)]

        forth = launch(near["next"], quarter(opposite, low), ring_low)
        back = launch(near["last"], quarter(opposite + low, size - low), ring_high)
        yield
        forth.came(ring_low)
        for k in range(RING):
            add_blocks(low, rows(k, ahead, low), [ring_low.at[k]])
        forth = launch(near["next"], quarter(ahead, size), from_last)
        back.came(ring_high)
        for k in range(RING):
            add_blocks(size - low, rows(k, behind + low, size - low), [ring_high.at[k]])
        back = launch(near["last"], quarter(behind, size), from_next)
        yield
        forth.came(from_last)
        back.came(from_next)
        for k in order:
            add_blocks(size, rows(k, first, size), [from_last.at[k], from_next.at[k]])
            if k == 2:
                far = send_far()
    yield
    far[0].came(far_low)
    add_blocks(low, rows(1, first, low), [far_low])
    up = launch(near["above"], rows(1, first, size), from_below)
    far[1].came(far_high)
    add_blocks(size - low, rows(3, first + low, size - low), [far_high])
    down = launch(near["below"], rows(3, first, size), from_above)
    yield
    up.came(from_below)
    down.came(from_above)
    mine = rows(0, first, size)
    add_blocks(size, mine, [from_below, from_above])
    over_x = links.channel(cross_core)
    on_core(1, lambda: over_x.send(mine, cross))
    finals.append(lambda: on_core(1, lambda: over_x.sent(mine)))
    yield

    def take_x():
        over_x.came(cross)
        add_blocks(size, mine, [cross])

    on_core(0, take_x)
    if spread:
        result = mine
    else:
        ring, result = buffers[5:7]
        piece = result.shape[0]
        over_y = [links.channel(device) for device in others]

        def part(owner):
            return total.at[0, pl.ds((owner * blocks) // RING, piece)]

        def send_y():
            for j in (2, 1, 3):
                over_y[j - 1].send(part((y + j) % RING), ring.at[j - 1])

        on_core(0, send_y)
        finals.append(
            lambda: on_core(0, lambda: [over_y[j].sent(part((y + j + 1) % RING)) for j in range(3)])
        )
        yield

        def take_y():
            for j in range(RING - 1):
                over_y[j].came(ring.at[j])
            own = part(y)

            def step(b, carry):
                value = own[b].astype(jnp.float32)
                for j in range(RING - 1):
                    value = value + ring[j, b].astype(jnp.float32)
                result[b] = value.astype(result.dtype)
                return carry

            lax.fori_loop(0, piece, step, 0)

        on_core(0, take_y)
    shares = [links.channel(device) for device in others]
    keep = pltpu.make_async_copy(result, out.at[y], kept)

    def share():
        for j in (2, 1, 3):
            shares[j - 1].send(result, out.at[y])
        keep.start()

    on_core(0, share)
    finals.append(lambda: on_core(0, lambda: [channel.sent(result) for channel in shares]))
    yield
    hand = links.channel(near["sibling"])

    def pass_on():
        keep.wait()
        for j in (1, 2, 3):
            shares[j - 1].came(out.at[(y + RING - j) % RING])
        hand.send(out, out)

    on_core(0, pass_on)
    finals.append(lambda: on_core(0, lambda: hand.sent(out)))
    yield
    on_core(1, lambda: hand.came(out))
    for action in finals:
        action()


SUM_LINKS = 200
SUM_ORDER = "KQDKUQKuQDVKUdDKQuPVQUSudDVPKSQdKUQKQUudDUVuUPSdVuUDVDuPSVudDVPSdDPSdPSdPS"
SUM_OPERANDS = 11


def sum_kernel(arrays, order, *refs):
    operands, refs = refs[:SUM_OPERANDS], refs[SUM_OPERANDS:]
    count = len(arrays)
    outs, refs = refs[:count], refs[count:]
    pairs = product_pairs(arrays)
    wholes, refs = dict(zip(pairs, refs)), refs[len(pairs) :]
    send, recv, kept, sems, loads = refs[:5]
    narrow_fill, wide_fill, narrow_stage, wide_stage, tall_stage, small_stage = refs[5:11]
    refs = refs[11:]
    links = Links(send, recv)
    z, x, y, c = place()
    near = near_devices()
    greet(
        [near["above"], near["below"], near["sibling"]]
        + [{"group": 2 * z + 1 - x, "rep": 2 * y + 1 - c}]
        + [{"rep": 2 * ((y + j) % RING) + c} for j in range(1, RING)]
    )
    jobs = {}
    for i, (name, (left, right, chunk, spread)) in enumerate(arrays.items()):
        buffers, refs = refs[:10], refs[10:]
        stage, fill = narrow_stage, lambda: None
        if right is None:
            whole, stage = operands[left], small_stage
        else:
            whole, space = wholes[left, right], narrow_fill
            if outs[i].shape[-1] > 2048:
                space, stage = wide_fill, wide_stage
            elif spread:
                stage = tall_stage
            if chunk[1] == 0:
                fill = functools.partial(
                    product_into, operands[left], operands[right], whole, space, sems
                )
        jobs[name] = sum_job(
            links, fill, whole, chunk, spread, buffers[0], stage, loads, buffers[1:], outs[i], kept.at[i]
        )
    for name in order:
        next(jobs[name], None)
    for job in jobs.values():
        for _ in job:
            pass


def product_pairs(arrays):
    return list(dict.fromkeys((a[0], a[1]) for a in arrays.values() if a[1] is not None))


def sum_gradients(operands, arrays, order):
    dma = pltpu.SemaphoreType.DMA
    vmem, hbm = pl.BlockSpec(memory_space=pltpu.VMEM), pl.BlockSpec(memory_space=pl.ANY)
    bf16 = jnp.bfloat16
    outs, wholes, scratch, deepest = [], {}, [], {}
    for left, right, chunk, spread in arrays.values():
        shard_blocks, _, blocks = chunk
        if right is None:
            width, dtype = operands[left].shape[-1], operands[left].dtype
        else:
            width, dtype = operands[right].shape[1], bf16
            wholes[left, right] = jax.ShapeDtypeStruct((8 * shard_blocks, 8, width), dtype)
            kind = (width, spread)
            deepest[kind] = max(blocks, deepest.get(kind, 0))
        piece = piece_rows(blocks)
        outs.append(jax.ShapeDtypeStruct((RING, piece, 8, width), dtype))
        size = blocks // RING if spread else blocks
        low = size // 2
        leads = [(RING, blocks), (low,), (size - low,), (size,), (size,), (size,)]
        if spread:
            leads += [(RING, low), (RING, size - low), (RING, size), (RING, size)]
        else:
            leads += [(RING - 1, piece), (piece,), (1,), (1,)]
        scratch += [pltpu.VMEM(lead + (8, width), dtype) for lead in leads]
    narrow_width, wide_width = (pick(width for width, _ in deepest) for pick in (min, max))
    small_shape = operands[-1].shape
    stages = [(narrow_width, False), (wide_width, False), (narrow_width, True)]
    return pl.pallas_call(
        functools.partial(sum_kernel, arrays, order),
        out_shape=outs + list(wholes.values()),
        in_specs=[vmem] * (len(operands) - 1) + [hbm],
        out_specs=[hbm] * (len(outs) + len(wholes)),
        scratch_shapes=[
            dma((SUM_LINKS,)),
            dma((SUM_LINKS,)),
            dma((len(outs),)),
            dma((2,)),
            dma((2,)),
            pltpu.VMEM((2, TILE // 8, 8, narrow_width), bf16),
            pltpu.VMEM((2, TILE // 8, 8, wide_width), bf16),
        ]
        + [pltpu.VMEM((2, deepest[kind], 8, kind[0]), bf16) for kind in stages]
        + [pltpu.VMEM((2, small_shape[0] // 8) + small_shape[1:], operands[-1].dtype)]
        + scratch,
        compiler_params=pltpu.CompilerParams(
            collective_id=1, has_side_effects=True, vmem_limit_bytes=62 * 1024 * 1024
        ),
        name="sum_gradients",
    )(*operands)[: len(outs)]


def assemble_kernel(names, places, *refs):
    outs = refs[len(names) :]
    for name, ref in zip(names, refs):
        output, row, column, blocks = places[name]
        width = ref.shape[-1]
        for i in range(RING):
            first, end = i * blocks // RING, (i + 1) * blocks // RING
            value = ref[i, 0 : end - first].astype(jnp.float32).reshape((end - first) * 8, width)
            outs[output][row + first * 8 : row + end * 8, column : column + width] = value


def assemble(sums, places, shapes):
    names = tuple(places)
    vmem = pl.BlockSpec(memory_space=pltpu.VMEM)
    return pl.pallas_call(
        functools.partial(assemble_kernel, names, places),
        out_shape=[jax.ShapeDtypeStruct(shape, jnp.float32) for shape in shapes],
        in_specs=[vmem] * len(names),
        out_specs=[vmem] * len(shapes),
        compiler_params=pltpu.CompilerParams(vmem_limit_bytes=48 * 1024 * 1024),
        name="assemble",
    )(*(sums[name] for name in names))


def lane_head(shape):
    return lax.broadcasted_iota(jnp.int32, shape, len(shape) - 1) // HEAD


def one_head(matrix, head):
    return jnp.where(lane_head(matrix.shape) == head, matrix, jnp.zeros_like(matrix))


def over_lanes(left, right):
    return lax.dot_general(left, right, (((1,), (1,)), ((), ())), preferred_element_type=jnp.float32)


def over_rows(left, right):
    return lax.dot_general(left, right, (((0,), (0,)), ((), ())), preferred_element_type=jnp.float32)


def plain(left, right):
    return jnp.dot(left, right, preferred_element_type=jnp.float32)


def half_selector(first):
    rows = lax.broadcasted_iota(jnp.int32, (HEAD, LANES), 0)
    lanes = lax.broadcasted_iota(jnp.int32, (HEAD, LANES), 1)
    return (rows + first == lanes).astype(jnp.bfloat16)


def widen(matrix, first):
    return plain(matrix, half_selector(first)).astype(jnp.bfloat16)


def narrow(matrix, first):
    return over_lanes(matrix, half_selector(first)).astype(jnp.bfloat16)


def soft_columns(key_rows, queries, first_query, length):
    scores = over_lanes(key_rows, queries) * HEAD ** (-0.5)
    key_pos = lax.broadcasted_iota(jnp.int32, scores.shape, 0)
    query_pos = first_query + lax.broadcasted_iota(jnp.int32, scores.shape, 1)
    scores = jnp.where((key_pos <= query_pos) & (key_pos < length), scores, MASKED)
    exponent = jnp.exp(scores - jnp.max(scores, 0, keepdims=True))
    return exponent * (1.0 / jnp.sum(exponent, 0, keepdims=True))


def peers(count):
    member = lax.axis_index("group")
    ahead = [(member + j) % count for j in range(1, count)]
    return (member, ahead)


def normalize(inputs):
    average = jnp.mean(inputs, -1, keepdims=True)
    centered = inputs - average
    variance = jnp.mean(centered * centered, -1, keepdims=True)
    scale = lax.rsqrt(variance + EPSILON)
    return (centered * scale, scale)


def norm_back(unit, scale, gain, grad):
    scaled = grad * gain
    pulled = scaled - jnp.mean(scaled, -1, keepdims=True)
    pulled = pulled - unit * jnp.mean(scaled * unit, -1, keepdims=True)
    return (
        pulled * scale,
        jnp.sum(grad * unit, 0, keepdims=True),
        jnp.sum(grad, 0, keepdims=True),
    )


GELU_IN, GELU_CUBE = 0.7978845608028654, 0.044715


def gelu_parts(value):
    square = value * value
    bent = jnp.tanh(GELU_IN * value * (1.0 + GELU_CUBE * square))
    half = 0.5 * (1.0 + bent)
    slope = half + 0.5 * value * (1.0 - bent * bent) * GELU_IN * (1.0 + 3.0 * GELU_CUBE * square)
    return (value * half, slope)


def column_chunks(width, most):
    return [(first, min(most, width - first)) for first in range(0, width, most)]


FORWARD_WEIGHTS = ("q", "k", "v", "proj", "up", "down")


def shipment(source, arrived, send, recv):
    device = {"pipe": 1 - lax.axis_index("pipe")}
    return lambda m: remote(source.at[m], arrived.at[m], send.at[m], recv.at[m], device)


def forward_kernel(
    ship, lengths, inputs, vectors, up_bias, wq, wk, wv, wproj, wup, wdown,
    output, hidden_out, pre_act, attn_mixed, last_q, kept, kept_last, arrived,
    vq, vk, vv, vproj, vup, vdown, pack, last_kv, held, held_last, staged, mixed, leaving,
    send, recv, send_last, recv_last, send_back, recv_back, local, loaded, send_ship, recv_ship,
):
    count, micros, _, rows, lanes = pack.shape
    member, ahead = peers(count)
    wide = count * lanes
    sources, places = (wq, wk, wv, wproj, wup, wdown), (vq, vk, vv, vproj, vup, vdown)
    loads = [
        pltpu.make_async_copy(sources[i], places[i], loaded.at[i]) for i in range(len(sources))
    ]
    for load in loads:
        load.start()
    devices = [{"group": peer} for peer in ahead]
    if ship:
        devices.append({"pipe": 1 - lax.axis_index("pipe")})
    greet(devices)
    ship_copy = shipment(leaving, arrived, send_ship, recv_ship)

    def out(m, j):
        return remote(
            pack.at[ahead[j], m], held.at[member, m], send.at[m, j], recv.at[m, j], {"group": ahead[j]}
        )

    def out_last(m, j):
        return remote(
            last_kv.at[m],
            held_last.at[member, m],
            send_last.at[m, j],
            recv_last.at[m, j],
            {"group": ahead[j]},
        )

    def back(m, j):
        return remote(
            staged.at[ahead[j], m],
            mixed.at[member, m],
            send_back.at[m, j],
            recv_back.at[m, j],
            {"group": ahead[j]},
        )

    def own(m):
        return (
            pltpu.make_async_copy(pack.at[member, m], held.at[member, m], local.at[m, 0]),
            pltpu.make_async_copy(last_kv.at[m], held_last.at[member, m], local.at[m, 1]),
        )

    def own_back(m):
        return pltpu.make_async_copy(staged.at[member, m], mixed.at[member, m], local.at[m, 2])

    def keep():
        return (
            pltpu.make_async_copy(held, kept, local.at[0, 3]),
            pltpu.make_async_copy(held_last, kept_last, local.at[1, 3]),
        )

    peer_range = range(count - 1)
    unit, _ = normalize(inputs[...])
    normed = (unit * vectors[0:1] + vectors[1:2]).astype(jnp.bfloat16)
    lasts = []
    for third, (weight, bias) in enumerate(((vq, 2), (vk, None), (vv, 3))):
        loads[third].wait()
        product = plain(normed, weight[...])
        if bias is not None:
            product = product + vectors[bias : bias + 1]
        product = product.astype(jnp.bfloat16)
        for d in range(count):
            for m in range(micros):
                pack[d, m, third] = product[m * rows : (m + 1) * rows, d * lanes : (d + 1) * lanes]
        lasts.append(product[:, wide:])
    wide_q = widen(lasts[0], 0)
    both_last = widen(lasts[1], 0) + widen(lasts[2], HEAD)
    for m in range(micros):
        last_q[m] = wide_q[m * rows : (m + 1) * rows]
        last_kv[m] = both_last[m * rows : (m + 1) * rows]
    for m in range(micros):
        for j in peer_range:
            out(m, j).start()
            out_last(m, j).start()
        for copy in own(m):
            copy.start()

    def micro(m):
        for copy in own(m):
            copy.wait()
        for j in peer_range:
            out(m, j).wait_recv()
            out_last(m, j).wait_recv()
        length = lengths[m]
        span = 2
        for block in range(count // span):
            reach = span * (block + 1)
            queries = held[span * block : reach, m, 0].reshape(span * rows, lanes)
            key_rows = held[0:reach, m, 1].reshape(reach * rows, lanes)
            values = held[0:reach, m, 2].reshape(reach * rows, lanes)

            def head_step(head, total):
                probs = soft_columns(
                    key_rows, one_head(queries, head), span * block * rows, length
                ).astype(jnp.bfloat16)
                return total + over_rows(one_head(values, head), probs)

            total = lax.fori_loop(0, 2, head_step, jnp.zeros((lanes, span * rows), jnp.float32))
            staged[span * block : reach, m] = (
                total.T.astype(jnp.bfloat16).reshape(span, rows, lanes)
            )
        for j in peer_range:
            back(m, j).start()
        own_back(m).start()
        both = held_last[:, m].reshape(count * rows, lanes)
        probs = soft_columns(both, last_q[m], member * rows, length).astype(jnp.bfloat16)
        last_out = over_rows(both, probs).T.astype(jnp.bfloat16)
        attn_mixed[m * rows : (m + 1) * rows, wide:] = narrow(last_out, HEAD)

    for m in range(micros):
        micro(m)
    for copy in keep():
        copy.start()
    for m in range(micros):
        here = slice(m * rows, (m + 1) * rows)
        own_back(m).wait()
        for j in peer_range:
            back(m, j).wait_recv()
        for d in range(count):
            attn_mixed[here, d * lanes : (d + 1) * lanes] = mixed[d, m]
        if m == 0:
            loads[3].wait()
        hidden = inputs[here] + plain(attn_mixed[here], vproj[...]) + vectors[4:5]
        hidden_out[here] = hidden
        unit, _ = normalize(hidden)
        normed = (unit * vectors[5:6] + vectors[6:7]).astype(jnp.bfloat16)
        output[here] = hidden + vectors[7:8]
        if m == 0:
            loads[4].wait()
            loads[5].wait()
        for first, size in column_chunks(pre_act.shape[1], 1152):
            columns = slice(first, first + size)
            value = plain(normed, vup[:, columns]) + up_bias[:, columns]
            pre_act[here, columns] = value
            activated, _ = gelu_parts(value)
            output[here] += plain(activated.astype(jnp.bfloat16), vdown[columns, :])
        if ship:
            leaving[m] = output[here].astype(jnp.bfloat16)
            ship_copy(m).start()
    for m in range(micros):
        for j in peer_range:
            out(m, j).wait_send()
            out_last(m, j).wait_send()
            back(m, j).wait_send()
        if ship:
            ship_copy(m).wait()
    for copy in keep():
        copy.wait()


def forward_layer(ship, lengths, inputs, vectors, up_bias, weights, count, micros):
    total, width = inputs.shape
    rows, lanes = total // micros, LANES
    hidden = weights[4].shape[1]
    bf16, f32 = jnp.bfloat16, jnp.float32
    vmem, hbm = pl.BlockSpec(memory_space=pltpu.VMEM), pl.BlockSpec(memory_space=pl.ANY)
    dma = pltpu.SemaphoreType.DMA
    pack, blocks = (count, micros, 3, rows, lanes), (count, micros, rows, lanes)
    return pl.pallas_call(
        functools.partial(forward_kernel, ship),
        out_shape=[
            jax.ShapeDtypeStruct((total, width), f32),
            jax.ShapeDtypeStruct((total, width), f32),
            jax.ShapeDtypeStruct((total, hidden), f32),
            jax.ShapeDtypeStruct((total, width), bf16),
            jax.ShapeDtypeStruct((micros, rows, lanes), bf16),
            jax.ShapeDtypeStruct(pack, bf16),
            jax.ShapeDtypeStruct(blocks, bf16),
            jax.ShapeDtypeStruct((micros, rows, width), bf16),
        ],
        in_specs=[pl.BlockSpec(memory_space=pltpu.SMEM)] + [vmem] * 3 + [hbm] * 6,
        out_specs=[vmem] * 5 + [hbm] * 3,
        scratch_shapes=[pltpu.VMEM(w.shape, bf16) for w in weights]
        + [
            pltpu.VMEM(pack, bf16),
            pltpu.VMEM((micros, rows, lanes), bf16),
            pltpu.VMEM(pack, bf16),
            pltpu.VMEM(blocks, bf16),
            pltpu.VMEM(blocks, bf16),
            pltpu.VMEM(blocks, bf16),
            pltpu.VMEM((micros, rows, width), bf16),
        ]
        + [dma((micros, count - 1))] * 6
        + [dma((micros, 4)), dma((6,)), dma((micros,)), dma((micros,))],
        compiler_params=pltpu.CompilerParams(
            collective_id=4 if ship else 2, has_side_effects=True, vmem_limit_bytes=60 * 1024 * 1024
        ),
        name="forward_ship" if ship else "forward_layer",
    )(lengths, inputs, vectors, up_bias, *weights)


def backward_kernel(
    ship, lengths, grad_output, inputs, hidden, vectors, pre_act, held, held_last, last_q,
    wq, wk, wv, wproj, wup, wdown,
    grad_in, grad_q, grad_k, grad_v, grad_one, grad_pre, activated, normed_one, normed_two,
    vector_grads, bias_grads, arrived,
    vproj, vup, vdown, vqkv, grad_norm, grad_pack, last_grad, came, staged, staged_last, grads, parts_last,
    key_total, value_total, last_query_grad, leaving,
    send, recv, send_back, recv_back, send_last, recv_last, local, loaded, send_ship, recv_ship,
):
    count, micros, _, rows, lanes = held.shape
    member, ahead = peers(count)
    wide = count * lanes
    scale = HEAD ** (-0.5)
    loads = [
        pltpu.make_async_copy(source, target, loaded.at[i])
        for i, (source, target) in enumerate(
            (
                (wdown, vdown),
                (wup, vup),
                (wproj, vproj),
                (wq, vqkv.at[0]),
                (wk, vqkv.at[1]),
                (wv, vqkv.at[2]),
            )
        )
    ]
    for load in loads:
        load.start()
    devices = [{"group": peer} for peer in ahead]
    if ship:
        devices.append({"pipe": 1 - lax.axis_index("pipe")})
    greet(devices)
    ship_copy = shipment(leaving, arrived, send_ship, recv_ship)

    def out(m, j):
        return remote(
            grad_pack.at[ahead[j], m],
            came.at[member, m],
            send.at[m, j],
            recv.at[m, j],
            {"group": ahead[j]},
        )

    def back(m, j):
        return remote(
            staged.at[ahead[j], m],
            grads.at[member, m],
            send_back.at[m, j],
            recv_back.at[m, j],
            {"group": ahead[j]},
        )

    def back_last(m, j):
        return remote(
            staged_last.at[ahead[j], m],
            parts_last.at[member, m],
            send_last.at[m, j],
            recv_last.at[m, j],
            {"group": ahead[j]},
        )

    def own(m):
        return pltpu.make_async_copy(grad_pack.at[member, m], came.at[member, m], local.at[m, 0])

    def own_back(m):
        return (
            pltpu.make_async_copy(staged.at[member, m], grads.at[member, m], local.at[m, 1]),
            pltpu.make_async_copy(
                staged_last.at[member, m], parts_last.at[member, m], local.at[m, 2]
            ),
        )

    def column_sum(matrix):
        return jnp.sum(matrix.astype(jnp.float32), 0, keepdims=True)

    peer_range = range(count - 1)
    grad_two = grad_output[...].astype(jnp.bfloat16)
    vector_grads[7:8] = column_sum(grad_two)
    loads[0].wait()
    for first, size in column_chunks(pre_act.shape[1], 1152):
        columns = slice(first, first + size)
        value, slope = gelu_parts(pre_act[:, columns])
        activated[:, columns] = value.astype(jnp.bfloat16)
        part = (slope * over_lanes(grad_two, vdown[columns, :])).astype(jnp.bfloat16)
        grad_pre[:, columns] = part
        bias_grads[:, columns] = column_sum(part)
        if first == 0:
            loads[1].wait()
            grad_norm[...] = over_lanes(part, vup[:, columns])
        else:
            grad_norm[...] += over_lanes(part, vup[:, columns])
    unit, deviation = normalize(hidden[...])
    normed_two[...] = (unit * vectors[5:6] + vectors[6:7]).astype(jnp.bfloat16)
    from_norm, gain_sum, bias_sum = norm_back(unit, deviation, vectors[5:6], grad_norm[...])
    vector_grads[5:6] = gain_sum
    vector_grads[6:7] = bias_sum
    grad_hidden = grad_output[...] + from_norm
    grad_norm[...] = grad_hidden
    one = grad_hidden.astype(jnp.bfloat16)
    grad_one[...] = one
    vector_grads[4:5] = column_sum(one)
    loads[2].wait()
    grad_mixed = over_lanes(one, vproj[...]).astype(jnp.bfloat16)
    for m in range(micros):
        for d in range(count):
            grad_pack[d, m] = grad_mixed[m * rows : (m + 1) * rows, d * lanes : (d + 1) * lanes]
        for j in peer_range:
            out(m, j).start()
        own(m).start()
    wide_last = widen(grad_mixed[:, wide:], HEAD)
    for m in range(micros):
        last_grad[m] = wide_last[m * rows : (m + 1) * rows]

    def last_head(m):
        length = lengths[m]
        both = held_last[:, m].reshape(count * rows, lanes)
        probs = soft_columns(both, last_q[m], member * rows, length)
        grad_probs = over_lanes(both, last_grad[m])
        inner = jnp.sum(probs * grad_probs, 0, keepdims=True)
        grad_scores = (probs * (grad_probs - inner)).astype(jnp.bfloat16)
        query_grad = (scale * over_rows(both, grad_scores)).T.astype(jnp.bfloat16)
        grad_q[m * rows : (m + 1) * rows, wide:] = narrow(query_grad, 0)
        both_grad = scale * plain(grad_scores, last_q[m]) + plain(
            probs.astype(jnp.bfloat16), last_grad[m]
        )
        staged_last[:, m] = both_grad.astype(jnp.bfloat16).reshape(count, rows, lanes)
        for j in peer_range:
            back_last(m, j).start()

    def micro(m):
        length = lengths[m]
        own(m).wait()
        for j in peer_range:
            out(m, j).wait_recv()
        key_total[...] = jnp.zeros_like(key_total)
        value_total[...] = jnp.zeros_like(value_total)
        span = 2
        for block in range(count // span):
            reach = span * (block + 1)
            queries = held[span * block : reach, m, 0].reshape(span * rows, lanes)
            grad_out = came[span * block : reach, m].reshape(span * rows, lanes)
            key_rows = held[0:reach, m, 1].reshape(reach * rows, lanes)
            values = held[0:reach, m, 2].reshape(reach * rows, lanes)

            def head_step(head, total):
                head_queries, head_grad = one_head(queries, head), one_head(grad_out, head)
                probs = soft_columns(key_rows, head_queries, span * block * rows, length)
                grad_probs = over_lanes(values, head_grad)
                inner = jnp.sum(probs * grad_probs, 0, keepdims=True)
                grad_scores = (probs * (grad_probs - inner)).astype(jnp.bfloat16)
                value_total[0 : reach * rows] += plain(probs.astype(jnp.bfloat16), head_grad)
                key_total[0 : reach * rows] += plain(grad_scores, head_queries)
                return total + over_rows(one_head(key_rows, head), grad_scores)

            total = lax.fori_loop(0, 2, head_step, jnp.zeros((lanes, span * rows), jnp.float32))
            staged[span * block : reach, m, 0] = (
                (scale * total).T.astype(jnp.bfloat16).reshape(span, rows, lanes)
            )
        staged[:, m, 1] = (scale * key_total[...]).astype(jnp.bfloat16).reshape(count, rows, lanes)
        staged[:, m, 2] = value_total[...].astype(jnp.bfloat16).reshape(count, rows, lanes)
        for j in peer_range:
            back(m, j).start()
        for copy in own_back(m):
            copy.start()

    for m in range(micros):
        last_head(m)
    for m in range(micros):
        micro(m)
    unit, deviation = normalize(inputs[...])
    normed_one[...] = (unit * vectors[0:1] + vectors[1:2]).astype(jnp.bfloat16)
    for m in range(micros):
        here = slice(m * rows, (m + 1) * rows)
        for copy in own_back(m):
            copy.wait()
        for j in peer_range:
            back_last(m, j).wait_recv()
            back(m, j).wait_recv()
        last = jnp.sum(parts_last[:, m].astype(jnp.float32), 0).astype(jnp.bfloat16)
        grad_k[here, wide:] = narrow(last, 0)
        grad_v[here, wide:] = narrow(last, HEAD)
        for third, target in enumerate((grad_q, grad_k, grad_v)):
            for d in range(count):
                target[here, d * lanes : (d + 1) * lanes] = grads[d, m, third]
        if m == 0:
            for i in (3, 4, 5):
                loads[i].wait()
        pulled = over_lanes(grad_q[here], vqkv[0])
        pulled += over_lanes(grad_k[here], vqkv[1])
        pulled += over_lanes(grad_v[here], vqkv[2])
        from_norm, gain_sum, bias_sum = norm_back(
            unit[here], deviation[here], vectors[0:1], pulled
        )
        total = grad_norm[here] + from_norm
        grad_in[here] = total
        if ship:
            leaving[m] = total.astype(jnp.bfloat16)
            ship_copy(m).start()
        if m == 0:
            vector_grads[0:1] = gain_sum
            vector_grads[1:2] = bias_sum
        else:
            vector_grads[0:1] += gain_sum
            vector_grads[1:2] += bias_sum
    vector_grads[2:3] = column_sum(grad_q[...])
    vector_grads[3:4] = column_sum(grad_v[...])
    for m in range(micros):
        for j in peer_range:
            out(m, j).wait_send()
            back_last(m, j).wait_send()
            back(m, j).wait_send()
        if ship:
            ship_copy(m).wait()


def backward_layer(ship, lengths, grad_output, saved, vectors, weights):
    inputs, hidden, pre_act, held, held_last, last_q = saved
    count, micros, _, rows, lanes = held.shape
    total, width = inputs.shape
    bf16, f32 = jnp.bfloat16, jnp.float32
    vmem, hbm = pl.BlockSpec(memory_space=pltpu.VMEM), pl.BlockSpec(memory_space=pl.ANY)
    dma = pltpu.SemaphoreType.DMA
    narrow_out, wide_out = (total, width), pre_act.shape
    blocks, pack = (count, micros, rows, lanes), (count, micros, 3, rows, lanes)
    return pl.pallas_call(
        functools.partial(backward_kernel, ship),
        out_shape=[
            jax.ShapeDtypeStruct(shape, dtype)
            for shape, dtype in (
                (narrow_out, f32),
                (narrow_out, bf16),
                (narrow_out, bf16),
                (narrow_out, bf16),
                (narrow_out, bf16),
                (wide_out, bf16),
                (wide_out, bf16),
                (narrow_out, bf16),
                (narrow_out, bf16),
                ((8, width), f32),
                ((1, pre_act.shape[1]), f32),
                ((micros, rows, width), bf16),
            )
        ],
        in_specs=[pl.BlockSpec(memory_space=pltpu.SMEM)] + [vmem] * 8 + [hbm] * 6,
        out_specs=[vmem] * 11 + [hbm],
        scratch_shapes=[
            pltpu.VMEM(weights[3].shape, bf16),
            pltpu.VMEM(weights[4].shape, bf16),
            pltpu.VMEM(weights[5].shape, bf16),
            pltpu.VMEM((3,) + weights[0].shape, bf16),
            pltpu.VMEM(narrow_out, f32),
            pltpu.VMEM(blocks, bf16),
            pltpu.VMEM((micros, rows, lanes), bf16),
            pltpu.VMEM(blocks, bf16),
            pltpu.VMEM(pack, bf16),
            pltpu.VMEM(blocks, bf16),
            pltpu.VMEM(pack, bf16),
            pltpu.VMEM(blocks, bf16),
            pltpu.VMEM((count * rows, lanes), f32),
            pltpu.VMEM((count * rows, lanes), f32),
            pltpu.VMEM((micros, rows, lanes), bf16),
            pltpu.VMEM((micros, rows, width), bf16),
        ]
        + [dma((micros, count - 1))] * 6
        + [dma((micros, 3)), dma((6,)), dma((micros,)), dma((micros,))],
        compiler_params=pltpu.CompilerParams(
            collective_id=5 if ship else 3, has_side_effects=True, vmem_limit_bytes=62 * 1024 * 1024
        ),
        name="backward_ship" if ship else "backward_layer",
    )(lengths, grad_output, inputs, hidden, vectors, pre_act, held, held_last, last_q, *weights)


def in_blocks(matrix):
    return matrix.reshape(matrix.shape[0] // 8, 8, matrix.shape[1])


def body(
    block_input, out_grad, w_qkv, w_proj, w_up, w_down, vectors, b_up, seq_lengths, slot_of_seq
):
    section = lax.axis_index("pipe")
    replica = lax.axis_index("rep")
    member = lax.axis_index("group")
    rep_count = lax.axis_size("rep")
    count = lax.axis_size("group")
    micros, rows, width = block_input.shape[0], block_input.shape[2], block_input.shape[3]
    slot_ids = jnp.arange(seq_lengths.shape[0], dtype=jnp.int32)
    slot_len = jnp.sum(
        seq_lengths[:, None] * (slot_of_seq[:, None] == slot_ids[None, :]).astype(jnp.int32), axis=0
    )
    mine = jnp.arange(micros, dtype=jnp.int32) * rep_count + replica
    lengths = jnp.sum(
        slot_len[None, :] * (slot_ids[None, :] == mine[:, None]).astype(jnp.int32), axis=1
    )
    query_pos = member * rows + jnp.arange(rows, dtype=jnp.int32)
    valid = (query_pos[None, :] < lengths[:, None]).astype(jnp.float32)[:, :, None]
    cotangent = (out_grad[:, 0].astype(jnp.float32) * valid).reshape(micros * rows, width)

    bias_rows = b_up.shape[1] // vectors.shape[2]
    small = jnp.concatenate(
        [
            vectors[0],
            b_up[0].reshape(bias_rows, -1),
            jnp.zeros((8 - bias_rows, vectors.shape[2]), vectors.dtype),
        ],
        0,
    )
    thirds = [w_qkv[0][:, i * width : (i + 1) * width] for i in range(3)]
    small_full, *full = gather_weights(
        [in_blocks(array) for array in (small, *thirds, w_proj[0], w_up[0], w_down[0])],
        (
            (6, 0, 68, True),
            (5, 0, 16, True),
            (0, 0, 2, False),
            (1, 0, 17, False),
            (2, 0, 17, False),
            (3, 0, 17, False),
            (4, 0, 17, False),
            (5, 16, 1, False),
        ),
    )
    vector_rows = small_full[:, 0].transpose(1, 0, 2).reshape(8, width).astype(jnp.float32)
    up_bias = small_full[:, 1, :bias_rows].reshape(1, -1).astype(jnp.float32)
    weights = [array.reshape(-1, array.shape[-1]) for array in full]

    def forward(ship, inputs):
        return forward_layer(ship, lengths, inputs, vector_rows, up_bias, weights, count, micros)

    def landed(blocks):
        return blocks.reshape(micros * rows, width).astype(jnp.float32)

    first_in = block_input[:, 0].reshape(micros * rows, width).astype(jnp.float32)
    *_, arrived = forward(True, first_in)
    inputs = jnp.where(section == 0, first_in, landed(arrived))
    output, hidden, pre_act, attn_mixed, last_q, held, held_last, _ = forward(False, inputs)
    saved = (inputs, hidden, pre_act, held, held_last, last_q)
    *_, arrived = backward_layer(True, lengths, cotangent, saved, vector_rows, weights)
    grad_output = jnp.where(section == 1, cotangent, landed(arrived))
    (
        grad_in, grad_q, grad_k, grad_v, grad_one, grad_pre, activated, normed_one, normed_two,
        grad_vectors, grad_bias, _,
    ) = backward_layer(False, lengths, grad_output, saved, vector_rows, weights)

    small_grads = jnp.concatenate(
        [
            grad_vectors.reshape(8, count, -1).transpose(1, 0, 2),
            grad_bias.reshape(count, bias_rows, -1),
            jnp.zeros((count, 24 - bias_rows, width // count), jnp.float32),
        ],
        1,
    ).reshape(count * RING, 8, width // count)
    blocks = width // count // 8
    tall = grad_pre.shape[1] // count // 8
    half, tall_half = (blocks + 1) // 2, tall // 8 * 4 + 4
    arrays = {
        "Q": (0, 1, (blocks, 0, blocks), False),
        "K": (0, 2, (blocks, 0, blocks), False),
        "V": (0, 3, (blocks, 0, blocks), False),
        "P": (4, 5, (blocks, 0, blocks), False),
        "U": (6, 7, (blocks, 0, half), False),
        "u": (6, 7, (blocks, half, blocks - half), False),
        "D": (8, 9, (tall, 0, tall_half), True),
        "d": (8, 9, (tall, tall_half, tall - tall_half), True),
        "S": (10, None, (RING, 0, RING), False),
    }
    sums = sum_gradients(
        (
            normed_one, grad_q, grad_k, grad_v, attn_mixed, grad_one, normed_two, grad_pre, activated,
            grad_output.astype(jnp.bfloat16), small_grads,
        ),
        arrays,
        SUM_ORDER,
    )
    sums = dict(zip(arrays, sums))
    places = {
        "Q": (0, 0, 0, blocks),
        "K": (0, 0, width, blocks),
        "V": (0, 0, 2 * width, blocks),
        "P": (1, 0, 0, blocks),
        "U": (2, 0, 0, half),
        "u": (2, half * 8, 0, blocks - half),
        "D": (3, 0, 0, tall_half),
        "d": (3, tall_half * 8, 0, tall - tall_half),
    }
    grad_shapes = [(w.shape[1], w.shape[2]) for w in (w_qkv, w_proj, w_up, w_down)]
    totals = assemble(sums, places, grad_shapes)
    small_total = sums["S"].reshape(RING * 8, -1)
    edges = jnp.where(section == 0, grad_in, output).reshape(1, micros, 1, rows, width)
    return (
        edges,
        totals[0][None],
        totals[1][None],
        totals[2][None],
        totals[3][None],
        small_total[None, :8],
        small_total[8 : 8 + bias_rows].reshape(1, -1),
    )


def solution(mesh):
    in_specs = (
        P(None, "rep", "group", None),
        P(None, "rep", "group", None),
        P("pipe", "group", None),
        P("pipe", "group", None),
        P("pipe", "group", None),
        P("pipe", "group", None),
        P("pipe", None, "group"),
        P("pipe", "group"),
        P(),
        P(),
    )
    out_specs = (
        P("pipe", None, "rep", "group", None),
        P("pipe", "group", None),
        P("pipe", "group", None),
        P("pipe", "group", None),
        P("pipe", "group", None),
        P("pipe", None, "group"),
        P("pipe", "group"),
    )
    return jax.shard_map(body, mesh=mesh, in_specs=in_specs, out_specs=out_specs, check_vma=False)
```

```python
import functools
import jax
import jax.numpy as jnp
from jax import lax
from jax.experimental import pallas as pl
from jax.experimental.pallas import tpu as pltpu
from jax.sharding import PartitionSpec as P

HEAD = 64
LANES = 128
EPSILON = 1e-05
MASKED = -1e30
MESH = pl.DeviceIdType.MESH
RING = 4


def remote(src, dst, send_sem, recv_sem, device):
    return pltpu.make_async_remote_copy(
        src_ref=src,
        dst_ref=dst,
        send_sem=send_sem,
        recv_sem=recv_sem,
        device_id=device,
        device_id_type=MESH,
    )


def greet(devices):
    barrier = pltpu.get_barrier_semaphore()
    for device in devices:
        pl.semaphore_signal(barrier, inc=1, device_id=device, device_id_type=MESH)
    pl.semaphore_wait(barrier, len(devices))


def place():
    member, replica = lax.axis_index("group"), lax.axis_index("rep")
    return (member // 2, member % 2, replica // 2, replica % 2)


class Links:
    def __init__(self, send, recv):
        self.send, self.recv, self.used = send, recv, 0

    def channel(self, device):
        self.used += 1
        return Channel(self.send.at[self.used - 1], self.recv.at[self.used - 1], device)


class Channel:
    def __init__(self, send, recv, device):
        self.send_sem, self.recv_sem, self.device = send, recv, device

    def copy(self, src, dst):
        return remote(src, dst, self.send_sem, self.recv_sem, self.device)

    def send(self, src, dst):
        self.copy(src, dst).start()

    def sent(self, src):
        self.copy(src, src).wait_send()

    def came(self, dst):
        self.copy(dst, dst).wait_recv()


def near_devices():
    z, x, y, c = place()
    return {
        "above": {"group": 2 * ((z + 1) % RING) + x},
        "below": {"group": 2 * ((z + 3) % RING) + x},
        "partner": {"group": 2 * z + 1 - x},
        "sibling": {"rep": 2 * y + 1 - c},
        "next": {"rep": 2 * ((y + 1) % RING) + c},
        "last": {"rep": 2 * ((y + 3) % RING) + c},
    }


def gather_job(links, shard, full, first, size, spread):
    z, x, y, c = place()
    near = near_devices()
    xc = (x + c) % 2
    me = 2 * z + x
    base, above, below, across = (2 * ((z + k) % RING) + xc for k in (0, 1, 3, 2))
    piece = size // RING if spread else size
    low = piece - piece // 2
    finals = []

    def region(slot, owner, part=""):
        start = first + owner * piece if spread else first
        if part == "low":
            return full.at[slot, pl.ds(start, low)]
        if part == "high":
            return full.at[slot, pl.ds(start + low, piece - low)]
        return full.at[slot, pl.ds(start, piece)]

    def on_core(core, action):
        pl.when(c == core)(action)

    def always(action):
        action()

    def relay(channel, ref, run):
        run(lambda: channel.send(ref, ref))
        finals.append(lambda: run(lambda: channel.sent(ref)))

    def hand(slot, owner, run, part=""):
        channel = links.channel(near["sibling"])
        relay(channel, region(slot, owner, part), run)
        other = region(slot + 1 - 2 * xc, owner, part)
        get = (lambda action: on_core(0, action)) if run is not always else always
        finals.append(lambda: get(lambda: channel.came(other)))

    across_x = links.channel(near["partner"])
    up, down = links.channel(near["above"]), links.channel(near["below"])
    far_up, far_down = links.channel(near["above"]), links.channel(near["below"])
    own = shard.at[pl.ds(first + y * piece if spread else first, piece)]
    second = lambda action: on_core(1, action)

    def first_core():
        up.send(own, region(base, y))
        down.send(own, region(base, y))

    if spread:
        on_core(0, first_core)
    on_core(1, lambda: across_x.send(own, region(me, y)))
    finals.append(lambda: on_core(1, lambda: across_x.sent(own)))
    finals.append(lambda: up.sent(own))
    finals.append(lambda: down.sent(own))
    yield

    rings = []

    def pass_on(slot, run):
        if spread:
            forth, back = links.channel(near["next"]), links.channel(near["last"])
            relay(forth, region(slot, y), run)
            relay(back, region(slot, y), run)
            rings.append((slot, run, forth, back))
        hand(slot, y, run)

    def second_core():
        across_x.came(region(base, y))
        up.send(region(base, y), region(base, y))
        down.send(region(base, y), region(base, y))

    if not spread:
        on_core(0, first_core)
    on_core(1, second_core)
    pass_on(base, second)
    yield

    up.came(region(below, y))
    relay(far_up, region(below, y, "low"), always)
    pass_on(below, always)
    down.came(region(above, y))
    if piece > low:
        relay(far_down, region(above, y, "high"), always)
    pass_on(above, always)
    yield

    far_up.came(region(across, y, "low"))
    if piece > low:
        far_down.came(region(across, y, "high"))
    pass_on(across, always)
    yield

    if spread:
        ends = []
        for slot, run, forth, back in rings:
            far_forth, far_back = links.channel(near["next"]), links.channel(near["last"])
            behind, ahead = (y + 3) % RING, (y + 1) % RING
            run(lambda: forth.came(region(slot, behind)))
            relay(far_forth, region(slot, behind, "low"), run)
            hand(slot, behind, run)
            run(lambda: back.came(region(slot, ahead)))
            if piece > low:
                relay(far_back, region(slot, ahead, "high"), run)
            hand(slot, ahead, run)
            ends.append((slot, run, far_forth, far_back))
        yield
        for slot, run, far_forth, far_back in ends:
            far = (y + 2) % RING
            run(lambda: far_forth.came(region(slot, far, "low")))
            if piece > low:
                run(lambda: far_back.came(region(slot, far, "high")))
            hand(slot, far, run)
        yield
    for action in finals:
        action()


MAX_LINKS = 160


GATHER_ORDER = "SPSPSSPP"


def gather_steps(links, plan, ins, outs):
    member = lax.axis_index("group")
    count = len(ins)
    spread = [gather_job(links, ins[i], outs[i], *rest) for i, *rest in plan if rest[-1]]
    whole = [gather_job(links, ins[i], outs[i], *rest) for i, *rest in plan if not rest[-1]]
    owns = [links.channel(near_devices()["sibling"]) for _ in range(count)]
    for step, which in enumerate(GATHER_ORDER):
        for job in spread if which == "S" else whole:
            next(job)
        if step == 1:
            for i in range(count):
                owns[i].send(ins[i], outs[i].at[member])
    for job in whole:
        for _ in job:
            pass
    for i in range(count):
        owns[i].came(outs[i].at[member])
        owns[i].sent(ins[i])
    yield
    for job in spread:
        next(job)
    yield
    for job in spread:
        for _ in job:
            pass
    yield


def spread_vectors(small, vectors, up_bias):
    members, _, _, columns = small.shape
    bias_rows = up_bias.shape[1] // (members * columns)
    for member in range(members):
        first = member * columns
        vectors[:, first : first + columns] = small[member, 0].astype(jnp.float32)
        for row in range(bias_rows):
            first = (member * bias_rows + row) * columns
            up_bias[:, first : first + columns] = small[member, 1, row : row + 1].astype(jnp.float32)


def piece_rows(blocks):
    starts = [i * blocks // RING for i in range(RING + 1)]
    return max(starts[i + 1] - starts[i] for i in range(RING))


def add_blocks(count, dst, terms):
    def step(b, carry):
        total = dst[b].astype(jnp.float32)
        for term in terms:
            total = total + term[b].astype(jnp.float32)
        dst[b] = total.astype(dst.dtype)
        return carry

    lax.fori_loop(0, count, step, 0)


TILE = 256


def product_into(left, right, whole, stage, sems):
    def copy(tile, first, size):
        src = stage.at[tile % 2, pl.ds(0, size // 8)]
        return pltpu.make_async_copy(src, whole.at[pl.ds(first // 8, size // 8)], sems.at[tile % 2])

    tiles = [(t, *chunk) for t, chunk in enumerate(column_chunks(left.shape[1], TILE))]
    for t, first, size in tiles:
        if t >= 2:
            copy(*tiles[t - 2]).wait()
        for column, width in column_chunks(right.shape[1], 1152):
            tile = over_rows(left[:, first : first + size], right[:, column : column + width])
            stage[t % 2, 0 : size // 8, :, column : column + width] = tile.reshape(
                size // 8, 8, width
            ).astype(stage.dtype)
        copy(t, first, size).start()
    for tile in tiles[-2:]:
        copy(*tile).wait()


def sum_job(links, fill, whole, chunk, spread, total, stage, loads, buffers, out, kept):
    z, x, y, c = place()
    near = near_devices()
    shard_blocks, chunk_first, blocks = chunk
    xc = (x + c) % 2
    cross_core = {"group": 2 * z + 1 - x, "rep": 2 * y + 1 - c}
    others = [{"rep": 2 * ((y + j) % RING) + c} for j in range(1, RING)]
    far_low, far_high, from_below, from_above, cross = buffers[:5]
    size = blocks // RING if spread else blocks
    first = y * size if spread else 0
    low = size // 2
    order = (2, 1, 3, 0)
    finals = []

    def on_core(core, action):
        def run():
            action()

        pl.when(c == core)(run)

    def launch(device, src, dst):
        channel = links.channel(device)
        channel.send(src, dst)
        finals.append(lambda: channel.sent(src))
        return channel

    def shard(k, column):
        slot = 2 * ((z + k) % RING) + column
        return whole.at[pl.ds(slot * shard_blocks + chunk_first, blocks)]

    def rows(k, start, count):
        return total.at[k, pl.ds(start, count)]

    fill()
    swaps = [launch(near["sibling"], shard(k, 1 - xc), total.at[k]) for k in order]
    yield

    def load(n):
        space = stage.at[n % 2, pl.ds(0, blocks)]
        return pltpu.make_async_copy(shard(order[n], xc), space, loads.at[n % 2])

    def send_far():
        up = launch(near["above"], rows(2, first, low), far_low)
        down = launch(near["below"], rows(2, first + low, size - low), far_high)
        return (up, down)

    load(0).start()
    load(1).start()
    for n, k in enumerate(order):
        load(n).wait()
        swaps[n].came(total.at[k])
        add_blocks(blocks, total.at[k], [stage.at[n % 2]])
        if n + 2 < RING:
            load(n + 2).start()
        if k == 2 and not spread:
            far = send_far()
    if spread:
        ring_low, ring_high, from_last, from_next = buffers[5:9]
        ahead, behind, opposite = ((y + j) % RING * size for j in (1, 3, 2))

        def quarter(start, count):
            return total.at[:, pl.ds(start, count)]

        forth = launch(near["next"], quarter(opposite, low), ring_low)
        back = launch(near["last"], quarter(opposite + low, size - low), ring_high)
        yield
        forth.came(ring_low)
        for k in range(RING):
            add_blocks(low, rows(k, ahead, low), [ring_low.at[k]])
        forth = launch(near["next"], quarter(ahead, size), from_last)
        back.came(ring_high)
        for k in range(RING):
            add_blocks(size - low, rows(k, behind + low, size - low), [ring_high.at[k]])
        back = launch(near["last"], quarter(behind, size), from_next)
        yield
        forth.came(from_last)
        back.came(from_next)
        for k in order:
            add_blocks(size, rows(k, first, size), [from_last.at[k], from_next.at[k]])
            if k == 2:
                far = send_far()
    yield
    far[0].came(far_low)
    add_blocks(low, rows(1, first, low), [far_low])
    up = launch(near["above"], rows(1, first, size), from_below)
    far[1].came(far_high)
    add_blocks(size - low, rows(3, first + low, size - low), [far_high])
    down = launch(near["below"], rows(3, first, size), from_above)
    yield
    up.came(from_below)
    down.came(from_above)
    mine = rows(0, first, size)
    add_blocks(size, mine, [from_below, from_above])
    over_x = links.channel(cross_core)
    on_core(1, lambda: over_x.send(mine, cross))
    finals.append(lambda: on_core(1, lambda: over_x.sent(mine)))
    yield

    def take_x():
        over_x.came(cross)
        add_blocks(size, mine, [cross])

    on_core(0, take_x)
    if spread:
        result = mine
    else:
        ring, result = buffers[5:7]
        piece = result.shape[0]
        over_y = [links.channel(device) for device in others]

        def part(owner):
            return total.at[0, pl.ds((owner * blocks) // RING, piece)]

        def send_y():
            for j in (2, 1, 3):
                over_y[j - 1].send(part((y + j) % RING), ring.at[j - 1])

        on_core(0, send_y)
        finals.append(
            lambda: on_core(0, lambda: [over_y[j].sent(part((y + j + 1) % RING)) for j in range(3)])
        )
        yield

        def take_y():
            for j in range(RING - 1):
                over_y[j].came(ring.at[j])
            own = part(y)

            def step(b, carry):
                value = own[b].astype(jnp.float32)
                for j in range(RING - 1):
                    value = value + ring[j, b].astype(jnp.float32)
                result[b] = value.astype(result.dtype)
                return carry

            lax.fori_loop(0, piece, step, 0)

        on_core(0, take_y)
    shares = [links.channel(device) for device in others]
    keep = pltpu.make_async_copy(result, out.at[y], kept)

    def share():
        for j in (2, 1, 3):
            shares[j - 1].send(result, out.at[y])
        keep.start()

    on_core(0, share)
    finals.append(lambda: on_core(0, lambda: [channel.sent(result) for channel in shares]))
    yield
    hand = links.channel(near["sibling"])

    def pass_on():
        keep.wait()
        for j in (1, 2, 3):
            shares[j - 1].came(out.at[(y + RING - j) % RING])
        hand.send(out, out)

    on_core(0, pass_on)
    finals.append(lambda: on_core(0, lambda: hand.sent(out)))
    yield
    on_core(1, lambda: hand.came(out))
    for action in finals:
        action()


SUM_LINKS = 200
SUM_ORDER = ("KQDKUQKuQDVKUdDKQuPVQUSudDVPKSQdKUQKQUud", "DUVuUPSdVuUDVDuPSVudDVPSdDPSdPSdPS")
SUM_OPERANDS = 11


def sum_kernel(arrays, order, *refs):
    operands, refs = refs[:SUM_OPERANDS], refs[SUM_OPERANDS:]
    count = len(arrays)
    outs, refs = refs[:count], refs[count:]
    pairs = product_pairs(arrays)
    wholes, refs = dict(zip(pairs, refs)), refs[len(pairs) :]
    send, recv, kept, sems, loads = refs[:5]
    narrow_fill, wide_fill, narrow_stage, wide_stage, tall_stage, small_stage = refs[5:11]
    refs = refs[11:]
    links = Links(send, recv)
    z, x, y, c = place()
    near = near_devices()
    greet(
        [near["above"], near["below"], near["sibling"]]
        + [{"group": 2 * z + 1 - x, "rep": 2 * y + 1 - c}]
        + [{"rep": 2 * ((y + j) % RING) + c} for j in range(1, RING)]
    )
    jobs = {}
    for i, (name, (left, right, chunk, spread)) in enumerate(arrays.items()):
        buffers, refs = refs[:10], refs[10:]
        stage, fill = narrow_stage, lambda: None
        if right is None:
            whole, stage = operands[left], small_stage
        else:
            whole, space = wholes[left, right], narrow_fill
            if outs[i].shape[-1] > 2048:
                space, stage = wide_fill, wide_stage
            elif spread:
                stage = tall_stage
            if chunk[1] == 0:
                fill = functools.partial(
                    product_into, operands[left], operands[right], whole, space, sems
                )
        jobs[name] = sum_job(
            links, fill, whole, chunk, spread, buffers[0], stage, loads, buffers[1:], outs[i], kept.at[i]
        )
    for name in "".join(order):
        next(jobs[name], None)
    for job in jobs.values():
        for _ in job:
            pass


def product_pairs(arrays):
    return list(dict.fromkeys((a[0], a[1]) for a in arrays.values() if a[1] is not None))


def sum_gradients(operands, arrays, order):
    dma = pltpu.SemaphoreType.DMA
    vmem, hbm = pl.BlockSpec(memory_space=pltpu.VMEM), pl.BlockSpec(memory_space=pl.ANY)
    bf16 = jnp.bfloat16
    outs, wholes, scratch, deepest = [], {}, [], {}
    for left, right, chunk, spread in arrays.values():
        shard_blocks, _, blocks = chunk
        if right is None:
            width, dtype = operands[left].shape[-1], operands[left].dtype
        else:
            width, dtype = operands[right].shape[1], bf16
            wholes[left, right] = jax.ShapeDtypeStruct((8 * shard_blocks, 8, width), dtype)
            kind = (width, spread)
            deepest[kind] = max(blocks, deepest.get(kind, 0))
        piece = piece_rows(blocks)
        outs.append(jax.ShapeDtypeStruct((RING, piece, 8, width), dtype))
        size = blocks // RING if spread else blocks
        low = size // 2
        leads = [(RING, blocks), (low,), (size - low,), (size,), (size,), (size,)]
        if spread:
            leads += [(RING, low), (RING, size - low), (RING, size), (RING, size)]
        else:
            leads += [(RING - 1, piece), (piece,), (1,), (1,)]
        scratch += [pltpu.VMEM(lead + (8, width), dtype) for lead in leads]
    narrow_width, wide_width = (pick(width for width, _ in deepest) for pick in (min, max))
    small_shape = operands[-1].shape
    stages = [(narrow_width, False), (wide_width, False), (narrow_width, True)]
    return pl.pallas_call(
        functools.partial(sum_kernel, arrays, order),
        out_shape=outs + list(wholes.values()),
        in_specs=[vmem] * (len(operands) - 1) + [hbm],
        out_specs=[hbm] * (len(outs) + len(wholes)),
        scratch_shapes=[
            dma((SUM_LINKS,)),
            dma((SUM_LINKS,)),
            dma((len(outs),)),
            dma((2,)),
            dma((2,)),
            pltpu.VMEM((2, TILE // 8, 8, narrow_width), bf16),
            pltpu.VMEM((2, TILE // 8, 8, wide_width), bf16),
        ]
        + [pltpu.VMEM((2, deepest[kind], 8, kind[0]), bf16) for kind in stages]
        + [pltpu.VMEM((2, small_shape[0] // 8) + small_shape[1:], operands[-1].dtype)]
        + scratch,
        compiler_params=pltpu.CompilerParams(
            collective_id=1, has_side_effects=True, vmem_limit_bytes=62 * 1024 * 1024
        ),
        name="sum_gradients",
    )(*operands)[: len(outs)]


def assemble_kernel(names, places, *refs):
    sources, refs = refs[: len(names)], refs[len(names) :]
    loaded, sems = refs[-1 - len(names) : -1], refs[-1]
    outs = refs[: -1 - len(names)]
    loads = [
        pltpu.make_async_copy(source, ref, sems.at[i])
        for i, (source, ref) in enumerate(zip(sources, loaded))
    ]
    for load in loads:
        load.start()
    for name, ref, load in zip(names, loaded, loads):
        load.wait()
        output, row, column, blocks = places[name]
        width = ref.shape[-1]
        for i in range(RING):
            first, end = i * blocks // RING, (i + 1) * blocks // RING
            value = ref[i, 0 : end - first].astype(jnp.float32).reshape((end - first) * 8, width)
            outs[output][row + first * 8 : row + end * 8, column : column + width] = value


def assemble(sums, places, shapes):
    names = tuple(places)
    vmem, hbm = pl.BlockSpec(memory_space=pltpu.VMEM), pl.BlockSpec(memory_space=pl.ANY)
    return pl.pallas_call(
        functools.partial(assemble_kernel, names, places),
        out_shape=[jax.ShapeDtypeStruct(shape, jnp.float32) for shape in shapes],
        in_specs=[hbm] * len(names),
        out_specs=[vmem] * len(shapes),
        scratch_shapes=[pltpu.VMEM(sums[name].shape, sums[name].dtype) for name in names]
        + [pltpu.SemaphoreType.DMA((len(names),))],
        compiler_params=pltpu.CompilerParams(vmem_limit_bytes=62 * 1024 * 1024),
        name="assemble",
    )(*(sums[name] for name in names))


def lane_head(shape):
    return lax.broadcasted_iota(jnp.int32, shape, len(shape) - 1) // HEAD


def one_head(matrix, head):
    return jnp.where(lane_head(matrix.shape) == head, matrix, jnp.zeros_like(matrix))


def over_lanes(left, right):
    return lax.dot_general(left, right, (((1,), (1,)), ((), ())), preferred_element_type=jnp.float32)


def over_rows(left, right):
    return lax.dot_general(left, right, (((0,), (0,)), ((), ())), preferred_element_type=jnp.float32)


def plain(left, right):
    return jnp.dot(left, right, preferred_element_type=jnp.float32)


def half_selector(first):
    rows = lax.broadcasted_iota(jnp.int32, (HEAD, LANES), 0)
    lanes = lax.broadcasted_iota(jnp.int32, (HEAD, LANES), 1)
    return (rows + first == lanes).astype(jnp.bfloat16)


def widen(matrix, first):
    return plain(matrix, half_selector(first)).astype(jnp.bfloat16)


def narrow(matrix, first):
    return over_lanes(matrix, half_selector(first)).astype(jnp.bfloat16)


def soft_columns(key_rows, queries, first_query, length):
    scores = over_lanes(key_rows, queries) * HEAD ** (-0.5)
    key_pos = lax.broadcasted_iota(jnp.int32, scores.shape, 0)
    query_pos = first_query + lax.broadcasted_iota(jnp.int32, scores.shape, 1)
    scores = jnp.where((key_pos <= query_pos) & (key_pos < length), scores, MASKED)
    exponent = jnp.exp(scores - jnp.max(scores, 0, keepdims=True))
    return exponent * (1.0 / jnp.sum(exponent, 0, keepdims=True))


def peers(count):
    member = lax.axis_index("group")
    ahead = [(member + j) % count for j in range(1, count)]
    return (member, ahead)


def normalize(inputs):
    average = jnp.mean(inputs, -1, keepdims=True)
    centered = inputs - average
    variance = jnp.mean(centered * centered, -1, keepdims=True)
    scale = lax.rsqrt(variance + EPSILON)
    return (centered * scale, scale)


def norm_back(unit, scale, gain, grad):
    scaled = grad * gain
    pulled = scaled - jnp.mean(scaled, -1, keepdims=True)
    pulled = pulled - unit * jnp.mean(scaled * unit, -1, keepdims=True)
    return (
        pulled * scale,
        jnp.sum(grad * unit, 0, keepdims=True),
        jnp.sum(grad, 0, keepdims=True),
    )


GELU_IN, GELU_CUBE = 0.7978845608028654, 0.044715


def gelu_parts(value):
    square = value * value
    bent = jnp.tanh(GELU_IN * value * (1.0 + GELU_CUBE * square))
    half = 0.5 * (1.0 + bent)
    slope = half + 0.5 * value * (1.0 - bent * bent) * GELU_IN * (1.0 + 3.0 * GELU_CUBE * square)
    return (value * half, slope)


def column_chunks(width, most):
    return [(first, min(most, width - first)) for first in range(0, width, most)]


FORWARD_WEIGHTS = ("q", "k", "v", "proj", "up", "down")


def first_kernel(plan, count, *refs):
    lengths, inputs = refs[:2]
    shards, fulls = refs[2 : 2 + count], refs[2 + count : 2 + 2 * count]
    arrived, refs = refs[2 + 2 * count], refs[3 + 2 * count :]
    vectors, up_bias, small, send, recv, loaded, *refs = refs
    near = near_devices()
    member, ahead = peers(8)
    greet(
        [{"group": peer} for peer in ahead]
        + [near[name] for name in ("sibling", "next", "last")]
        + [{"pipe": 1 - lax.axis_index("pipe")}]
    )
    steps = gather_steps(Links(send, recv), plan, shards, fulls)
    next(steps)
    load = pltpu.make_async_copy(fulls[0], small, loaded)
    load.start()
    load.wait()
    spread_vectors(small, vectors, up_bias)
    outputs, scratch = refs[:7], refs[7:]
    forward_kernel(
        steps, lengths, inputs, vectors, up_bias, *fulls[1:], *outputs, arrived, *scratch
    )


def first_layer(lengths, inputs, shards, plan, count, micros):
    total, width = inputs.shape
    rows, lanes, hidden = total // micros, LANES, shards[5].shape[2]
    bf16, f32 = jnp.bfloat16, jnp.float32
    vmem, hbm = pl.BlockSpec(memory_space=pltpu.VMEM), pl.BlockSpec(memory_space=pl.ANY)
    dma = pltpu.SemaphoreType.DMA
    pack, blocks = (count, micros, 3, rows, lanes), (count, micros, rows, lanes)
    return pl.pallas_call(
        functools.partial(first_kernel, plan, len(shards)),
        out_shape=[jax.ShapeDtypeStruct((8,) + s.shape, s.dtype) for s in shards]
        + [jax.ShapeDtypeStruct((micros, rows, width), bf16)],
        in_specs=[pl.BlockSpec(memory_space=pltpu.SMEM), vmem] + [hbm] * len(shards),
        out_specs=[hbm] * (len(shards) + 1),
        scratch_shapes=[
            pltpu.VMEM((8, width), f32),
            pltpu.VMEM((1, hidden), f32),
            pltpu.VMEM((8,) + shards[0].shape, bf16),
            dma((MAX_LINKS,)),
            dma((MAX_LINKS,)),
            dma,
            pltpu.VMEM((total, width), f32),
            pltpu.VMEM((total, width), f32),
            pltpu.VMEM((total, hidden), f32),
            pltpu.VMEM((total, width), bf16),
            pltpu.VMEM((micros, rows, lanes), bf16),
            pltpu.VMEM((8, 8), f32),
            pltpu.VMEM((8, 8), f32),
        ]
        + [pltpu.VMEM((s.shape[0] * 64, s.shape[2]), bf16) for s in shards[1:]]
        + [
            pltpu.VMEM(pack, bf16),
            pltpu.VMEM((micros, rows, lanes), bf16),
            pltpu.VMEM(pack, bf16),
            pltpu.VMEM(blocks, bf16),
            pltpu.VMEM(blocks, bf16),
            pltpu.VMEM(blocks, bf16),
            pltpu.VMEM((micros, rows, width), bf16),
        ]
        + [dma((micros, count - 1))] * 6
        + [dma((micros, 4)), dma((6,)), dma((micros,)), dma((micros,))],
        compiler_params=pltpu.CompilerParams(
            collective_id=0, has_side_effects=True, vmem_limit_bytes=62 * 1024 * 1024
        ),
        name="gather_forward",
    )(lengths, inputs, *shards)


def shipment(source, arrived, send, recv):
    device = {"pipe": 1 - lax.axis_index("pipe")}
    return lambda m: remote(source.at[m], arrived.at[m], send.at[m], recv.at[m], device)


def forward_kernel(
    ship, lengths, inputs, vectors, up_bias, wq, wk, wv, wproj, wup, wdown,
    output, hidden_out, pre_act, attn_mixed, last_q, kept, kept_last, arrived,
    vq, vk, vv, vproj, vup, vdown, pack, last_kv, held, held_last, staged, mixed, leaving,
    send, recv, send_last, recv_last, send_back, recv_back, local, loaded, send_ship, recv_ship,
):
    count, micros, _, rows, lanes = pack.shape
    member, ahead = peers(count)
    wide = count * lanes
    sources, places = (wq, wk, wv, wproj, wup, wdown), (vq, vk, vv, vproj, vup, vdown)
    loads = [
        pltpu.make_async_copy(sources[i].reshape(places[i].shape), places[i], loaded.at[i])
        if ship
        else pltpu.make_async_copy(sources[i], places[i], loaded.at[i])
        for i in range(len(sources))
    ]
    for load in loads[:4] if ship else loads:
        load.start()
    if not ship:
        greet([{"group": peer} for peer in ahead])
    ship_copy = shipment(leaving, arrived, send_ship, recv_ship)

    def out(m, j):
        return remote(
            pack.at[ahead[j], m], held.at[member, m], send.at[m, j], recv.at[m, j], {"group": ahead[j]}
        )

    def out_last(m, j):
        return remote(
            last_kv.at[m],
            held_last.at[member, m],
            send_last.at[m, j],
            recv_last.at[m, j],
            {"group": ahead[j]},
        )

    def back(m, j):
        return remote(
            staged.at[ahead[j], m],
            mixed.at[member, m],
            send_back.at[m, j],
            recv_back.at[m, j],
            {"group": ahead[j]},
        )

    def own(m):
        return (
            pltpu.make_async_copy(pack.at[member, m], held.at[member, m], local.at[m, 0]),
            pltpu.make_async_copy(last_kv.at[m], held_last.at[member, m], local.at[m, 1]),
        )

    def own_back(m):
        return pltpu.make_async_copy(staged.at[member, m], mixed.at[member, m], local.at[m, 2])

    def keep():
        return (
            pltpu.make_async_copy(held, kept, local.at[0, 3]),
            pltpu.make_async_copy(held_last, kept_last, local.at[1, 3]),
        )

    peer_range = range(count - 1)
    unit, _ = normalize(inputs[...])
    normed = (unit * vectors[0:1] + vectors[1:2]).astype(jnp.bfloat16)
    lasts = []
    for third, (weight, bias) in enumerate(((vq, 2), (vk, None), (vv, 3))):
        loads[third].wait()
        product = plain(normed, weight[...])
        if bias is not None:
            product = product + vectors[bias : bias + 1]
        product = product.astype(jnp.bfloat16)
        for d in range(count):
            for m in range(micros):
                pack[d, m, third] = product[m * rows : (m + 1) * rows, d * lanes : (d + 1) * lanes]
        lasts.append(product[:, wide:])
    wide_q = widen(lasts[0], 0)
    both_last = widen(lasts[1], 0) + widen(lasts[2], HEAD)
    for m in range(micros):
        last_q[m] = wide_q[m * rows : (m + 1) * rows]
        last_kv[m] = both_last[m * rows : (m + 1) * rows]
    for m in range(micros):
        for j in peer_range:
            out(m, j).start()
            out_last(m, j).start()
        for copy in own(m):
            copy.start()

    def micro(m):
        for copy in own(m):
            copy.wait()
        for j in peer_range:
            out(m, j).wait_recv()
            out_last(m, j).wait_recv()
        length = lengths[m]
        span = 2
        for block in range(count // span):
            reach = span * (block + 1)
            queries = held[span * block : reach, m, 0].reshape(span * rows, lanes)
            key_rows = held[0:reach, m, 1].reshape(reach * rows, lanes)
            values = held[0:reach, m, 2].reshape(reach * rows, lanes)

            def head_step(head, total):
                probs = soft_columns(
                    key_rows, one_head(queries, head), span * block * rows, length
                ).astype(jnp.bfloat16)
                return total + over_rows(one_head(values, head), probs)

            total = lax.fori_loop(0, 2, head_step, jnp.zeros((lanes, span * rows), jnp.float32))
            staged[span * block : reach, m] = (
                total.T.astype(jnp.bfloat16).reshape(span, rows, lanes)
            )
        for j in peer_range:
            back(m, j).start()
        own_back(m).start()
        both = held_last[:, m].reshape(count * rows, lanes)
        probs = soft_columns(both, last_q[m], member * rows, length).astype(jnp.bfloat16)
        last_out = over_rows(both, probs).T.astype(jnp.bfloat16)
        attn_mixed[m * rows : (m + 1) * rows, wide:] = narrow(last_out, HEAD)

    for m in range(micros):
        if ship and m == 0:
            next(ship)
        micro(m)
        if ship and m == 0:
            next(ship)
            for load in loads[4:]:
                load.start()
    for copy in () if ship else keep():
        copy.start()
    for m in range(micros):
        here = slice(m * rows, (m + 1) * rows)
        own_back(m).wait()
        for j in peer_range:
            back(m, j).wait_recv()
        for d in range(count):
            attn_mixed[here, d * lanes : (d + 1) * lanes] = mixed[d, m]
        if m == 0:
            loads[3].wait()
        hidden = inputs[here] + plain(attn_mixed[here], vproj[...]) + vectors[4:5]
        hidden_out[here] = hidden
        unit, _ = normalize(hidden)
        normed = (unit * vectors[5:6] + vectors[6:7]).astype(jnp.bfloat16)
        output[here] = hidden + vectors[7:8]
        if m == 0:
            loads[4].wait()
            loads[5].wait()
        for first, size in column_chunks(pre_act.shape[1], 1152):
            columns = slice(first, first + size)
            value = plain(normed, vup[:, columns]) + up_bias[:, columns]
            pre_act[here, columns] = value
            activated, _ = gelu_parts(value)
            output[here] += plain(activated.astype(jnp.bfloat16), vdown[columns, :])
        if ship:
            leaving[m] = output[here].astype(jnp.bfloat16)
            ship_copy(m).start()
    for m in range(micros):
        for j in peer_range:
            out(m, j).wait_send()
            out_last(m, j).wait_send()
            back(m, j).wait_send()
        if ship:
            ship_copy(m).wait()
    for copy in () if ship else keep():
        copy.wait()


def results_in_scratch(kernel, inputs, results):
    def run(*refs):
        before, last, rest = refs[:inputs], refs[inputs], refs[inputs + 1 :]
        kernel(*before, *rest[: results - 1], last, *rest[results - 1 :])

    return run


def layer_call(kernel, ship, operands, in_specs, results, spaces, scratch, **options):
    kernel = functools.partial(kernel, ship)
    if ship:
        kernel = results_in_scratch(kernel, len(operands), len(results))
        scratch = [pltpu.VMEM(r.shape, r.dtype) for r in results[:-1]] + scratch
        results, spaces = results[-1:], spaces[-1:]
    return pl.pallas_call(
        kernel,
        out_shape=results,
        in_specs=in_specs,
        out_specs=spaces,
        scratch_shapes=scratch,
        **options,
    )(*operands)


def forward_layer(lengths, inputs, vectors, up_bias, weights, count, micros):
    total, width = inputs.shape
    rows, lanes = total // micros, LANES
    hidden = weights[4].shape[1]
    bf16, f32 = jnp.bfloat16, jnp.float32
    vmem, hbm = pl.BlockSpec(memory_space=pltpu.VMEM), pl.BlockSpec(memory_space=pl.ANY)
    dma = pltpu.SemaphoreType.DMA
    pack, blocks = (count, micros, 3, rows, lanes), (count, micros, rows, lanes)
    return layer_call(
        forward_kernel,
        False,
        (lengths, inputs, vectors, up_bias, *weights),
        [pl.BlockSpec(memory_space=pltpu.SMEM)] + [vmem] * 3 + [hbm] * 6,
        [
            jax.ShapeDtypeStruct((total, width), f32),
            jax.ShapeDtypeStruct((total, width), f32),
            jax.ShapeDtypeStruct((total, hidden), f32),
            jax.ShapeDtypeStruct((total, width), bf16),
            jax.ShapeDtypeStruct((micros, rows, lanes), bf16),
            jax.ShapeDtypeStruct(pack, bf16),
            jax.ShapeDtypeStruct(blocks, bf16),
            jax.ShapeDtypeStruct((micros, rows, width), bf16),
        ],
        [vmem] * 5 + [hbm] * 3,
        [pltpu.VMEM(w.shape, bf16) for w in weights]
        + [
            pltpu.VMEM(pack, bf16),
            pltpu.VMEM((micros, rows, lanes), bf16),
            pltpu.VMEM(pack, bf16),
            pltpu.VMEM(blocks, bf16),
            pltpu.VMEM(blocks, bf16),
            pltpu.VMEM(blocks, bf16),
            pltpu.VMEM((micros, rows, width), bf16),
        ]
        + [dma((micros, count - 1))] * 6
        + [dma((micros, 4)), dma((6,)), dma((micros,)), dma((micros,))],
        compiler_params=pltpu.CompilerParams(
            collective_id=2, has_side_effects=True, vmem_limit_bytes=60 * 1024 * 1024
        ),
        name="forward_layer",
    )


def backward_kernel(
    ship, lengths, grad_output, inputs, hidden, vectors, pre_act, held, held_last, last_q,
    wq, wk, wv, wproj, wup, wdown,
    grad_in, grad_q, grad_k, grad_v, grad_one, grad_pre, activated, normed_one, normed_two,
    vector_grads, bias_grads, arrived,
    vproj, vup, vdown, vqkv, grad_norm, grad_pack, last_grad, came, staged, staged_last, grads, parts_last,
    key_total, value_total, last_query_grad, leaving,
    send, recv, send_back, recv_back, send_last, recv_last, local, loaded, send_ship, recv_ship,
):
    count, micros, _, rows, lanes = held.shape
    member, ahead = peers(count)
    wide = count * lanes
    scale = HEAD ** (-0.5)
    loads = [
        pltpu.make_async_copy(source, target, loaded.at[i])
        for i, (source, target) in enumerate(
            (
                (wdown, vdown),
                (wup, vup),
                (wproj, vproj),
                (wq, vqkv.at[0]),
                (wk, vqkv.at[1]),
                (wv, vqkv.at[2]),
            )
        )
    ]
    for load in loads:
        load.start()
    devices = [{"group": peer} for peer in ahead]
    if ship:
        devices.append({"pipe": 1 - lax.axis_index("pipe")})
    greet(devices)
    ship_copy = shipment(leaving, arrived, send_ship, recv_ship)

    def out(m, j):
        return remote(
            grad_pack.at[ahead[j], m],
            came.at[member, m],
            send.at[m, j],
            recv.at[m, j],
            {"group": ahead[j]},
        )

    def back(m, j):
        return remote(
            staged.at[ahead[j], m],
            grads.at[member, m],
            send_back.at[m, j],
            recv_back.at[m, j],
            {"group": ahead[j]},
        )

    def back_last(m, j):
        return remote(
            staged_last.at[ahead[j], m],
            parts_last.at[member, m],
            send_last.at[m, j],
            recv_last.at[m, j],
            {"group": ahead[j]},
        )

    def own(m):
        return pltpu.make_async_copy(grad_pack.at[member, m], came.at[member, m], local.at[m, 0])

    def own_back(m):
        return (
            pltpu.make_async_copy(staged.at[member, m], grads.at[member, m], local.at[m, 1]),
            pltpu.make_async_copy(
                staged_last.at[member, m], parts_last.at[member, m], local.at[m, 2]
            ),
        )

    def column_sum(matrix):
        return jnp.sum(matrix.astype(jnp.float32), 0, keepdims=True)

    peer_range = range(count - 1)
    grad_two = grad_output[...].astype(jnp.bfloat16)
    vector_grads[7:8] = column_sum(grad_two)
    loads[0].wait()
    for first, size in column_chunks(pre_act.shape[1], 1152):
        columns = slice(first, first + size)
        value, slope = gelu_parts(pre_act[:, columns])
        activated[:, columns] = value.astype(jnp.bfloat16)
        part = (slope * over_lanes(grad_two, vdown[columns, :])).astype(jnp.bfloat16)
        grad_pre[:, columns] = part
        bias_grads[:, columns] = column_sum(part)
        if first == 0:
            loads[1].wait()
            grad_norm[...] = over_lanes(part, vup[:, columns])
        else:
            grad_norm[...] += over_lanes(part, vup[:, columns])
    unit, deviation = normalize(hidden[...])
    normed_two[...] = (unit * vectors[5:6] + vectors[6:7]).astype(jnp.bfloat16)
    from_norm, gain_sum, bias_sum = norm_back(unit, deviation, vectors[5:6], grad_norm[...])
    vector_grads[5:6] = gain_sum
    vector_grads[6:7] = bias_sum
    grad_hidden = grad_output[...] + from_norm
    grad_norm[...] = grad_hidden
    one = grad_hidden.astype(jnp.bfloat16)
    grad_one[...] = one
    vector_grads[4:5] = column_sum(one)
    loads[2].wait()
    grad_mixed = over_lanes(one, vproj[...]).astype(jnp.bfloat16)
    for m in range(micros):
        for d in range(count):
            grad_pack[d, m] = grad_mixed[m * rows : (m + 1) * rows, d * lanes : (d + 1) * lanes]
        for j in peer_range:
            out(m, j).start()
        own(m).start()
    wide_last = widen(grad_mixed[:, wide:], HEAD)
    for m in range(micros):
        last_grad[m] = wide_last[m * rows : (m + 1) * rows]

    def last_head(m):
        length = lengths[m]
        both = held_last[:, m].reshape(count * rows, lanes)
        probs = soft_columns(both, last_q[m], member * rows, length)
        grad_probs = over_lanes(both, last_grad[m])
        inner = jnp.sum(probs * grad_probs, 0, keepdims=True)
        grad_scores = (probs * (grad_probs - inner)).astype(jnp.bfloat16)
        query_grad = (scale * over_rows(both, grad_scores)).T.astype(jnp.bfloat16)
        grad_q[m * rows : (m + 1) * rows, wide:] = narrow(query_grad, 0)
        both_grad = scale * plain(grad_scores, last_q[m]) + plain(
            probs.astype(jnp.bfloat16), last_grad[m]
        )
        staged_last[:, m] = both_grad.astype(jnp.bfloat16).reshape(count, rows, lanes)
        for j in peer_range:
            back_last(m, j).start()

    def micro(m):
        length = lengths[m]
        own(m).wait()
        for j in peer_range:
            out(m, j).wait_recv()
        key_total[...] = jnp.zeros_like(key_total)
        value_total[...] = jnp.zeros_like(value_total)
        span = 2
        for block in range(count // span):
            reach = span * (block + 1)
            queries = held[span * block : reach, m, 0].reshape(span * rows, lanes)
            grad_out = came[span * block : reach, m].reshape(span * rows, lanes)
            key_rows = held[0:reach, m, 1].reshape(reach * rows, lanes)
            values = held[0:reach, m, 2].reshape(reach * rows, lanes)

            def head_step(head, total):
                head_queries, head_grad = one_head(queries, head), one_head(grad_out, head)
                probs = soft_columns(key_rows, head_queries, span * block * rows, length)
                grad_probs = over_lanes(values, head_grad)
                inner = jnp.sum(probs * grad_probs, 0, keepdims=True)
                grad_scores = (probs * (grad_probs - inner)).astype(jnp.bfloat16)
                value_total[0 : reach * rows] += plain(probs.astype(jnp.bfloat16), head_grad)
                key_total[0 : reach * rows] += plain(grad_scores, head_queries)
                return total + over_rows(one_head(key_rows, head), grad_scores)

            total = lax.fori_loop(0, 2, head_step, jnp.zeros((lanes, span * rows), jnp.float32))
            staged[span * block : reach, m, 0] = (
                (scale * total).T.astype(jnp.bfloat16).reshape(span, rows, lanes)
            )
        staged[:, m, 1] = (scale * key_total[...]).astype(jnp.bfloat16).reshape(count, rows, lanes)
        staged[:, m, 2] = value_total[...].astype(jnp.bfloat16).reshape(count, rows, lanes)
        for j in peer_range:
            back(m, j).start()
        for copy in own_back(m):
            copy.start()

    for m in range(micros):
        last_head(m)
    for m in range(micros):
        micro(m)
    unit, deviation = normalize(inputs[...])
    normed_one[...] = (unit * vectors[0:1] + vectors[1:2]).astype(jnp.bfloat16)
    for m in range(micros):
        here = slice(m * rows, (m + 1) * rows)
        for copy in own_back(m):
            copy.wait()
        for j in peer_range:
            back_last(m, j).wait_recv()
            back(m, j).wait_recv()
        last = jnp.sum(parts_last[:, m].astype(jnp.float32), 0).astype(jnp.bfloat16)
        grad_k[here, wide:] = narrow(last, 0)
        grad_v[here, wide:] = narrow(last, HEAD)
        for third, target in enumerate((grad_q, grad_k, grad_v)):
            for d in range(count):
                target[here, d * lanes : (d + 1) * lanes] = grads[d, m, third]
        if m == 0:
            for i in (3, 4, 5):
                loads[i].wait()
        pulled = over_lanes(grad_q[here], vqkv[0])
        pulled += over_lanes(grad_k[here], vqkv[1])
        pulled += over_lanes(grad_v[here], vqkv[2])
        from_norm, gain_sum, bias_sum = norm_back(
            unit[here], deviation[here], vectors[0:1], pulled
        )
        total = grad_norm[here] + from_norm
        grad_in[here] = total
        if ship:
            leaving[m] = total.astype(jnp.bfloat16)
            ship_copy(m).start()
        if m == 0:
            vector_grads[0:1] = gain_sum
            vector_grads[1:2] = bias_sum
        else:
            vector_grads[0:1] += gain_sum
            vector_grads[1:2] += bias_sum
    vector_grads[2:3] = column_sum(grad_q[...])
    vector_grads[3:4] = column_sum(grad_v[...])
    for m in range(micros):
        for j in peer_range:
            out(m, j).wait_send()
            back_last(m, j).wait_send()
            back(m, j).wait_send()
        if ship:
            ship_copy(m).wait()


def backward_layer(ship, lengths, grad_output, saved, vectors, weights):
    inputs, hidden, pre_act, held, held_last, last_q = saved
    count, micros, _, rows, lanes = held.shape
    total, width = inputs.shape
    bf16, f32 = jnp.bfloat16, jnp.float32
    vmem, hbm = pl.BlockSpec(memory_space=pltpu.VMEM), pl.BlockSpec(memory_space=pl.ANY)
    dma = pltpu.SemaphoreType.DMA
    narrow_out, wide_out = (total, width), pre_act.shape
    blocks, pack = (count, micros, rows, lanes), (count, micros, 3, rows, lanes)
    return layer_call(
        backward_kernel,
        ship,
        (
            lengths, grad_output, inputs, hidden, vectors, pre_act, held, held_last, last_q,
            *weights,
        ),
        [pl.BlockSpec(memory_space=pltpu.SMEM)] + [vmem] * 8 + [hbm] * 6,
        [
            jax.ShapeDtypeStruct(shape, dtype)
            for shape, dtype in (
                (narrow_out, f32),
                (narrow_out, bf16),
                (narrow_out, bf16),
                (narrow_out, bf16),
                (narrow_out, bf16),
                (wide_out, bf16),
                (wide_out, bf16),
                (narrow_out, bf16),
                (narrow_out, bf16),
                ((8, width), f32),
                ((1, pre_act.shape[1]), f32),
                ((micros, rows, width), bf16),
            )
        ],
        [vmem] * 11 + [hbm],
        [
            pltpu.VMEM(weights[3].shape, bf16),
            pltpu.VMEM(weights[4].shape, bf16),
            pltpu.VMEM(weights[5].shape, bf16),
            pltpu.VMEM((3,) + weights[0].shape, bf16),
            pltpu.VMEM(narrow_out, f32),
            pltpu.VMEM(blocks, bf16),
            pltpu.VMEM((micros, rows, lanes), bf16),
            pltpu.VMEM(blocks, bf16),
            pltpu.VMEM(pack, bf16),
            pltpu.VMEM(blocks, bf16),
            pltpu.VMEM(pack, bf16),
            pltpu.VMEM(blocks, bf16),
            pltpu.VMEM((count * rows, lanes), f32),
            pltpu.VMEM((count * rows, lanes), f32),
            pltpu.VMEM((micros, rows, lanes), bf16),
            pltpu.VMEM((micros, rows, width), bf16),
        ]
        + [dma((micros, count - 1))] * 6
        + [dma((micros, 3)), dma((6,)), dma((micros,)), dma((micros,))],
        compiler_params=pltpu.CompilerParams(
            collective_id=5 if ship else 3, has_side_effects=True, vmem_limit_bytes=62 * 1024 * 1024
        ),
        name="backward_ship" if ship else "backward_layer",
    )


def in_blocks(matrix):
    return matrix.reshape(matrix.shape[0] // 8, 8, matrix.shape[1])


def body(
    block_input, out_grad, w_qkv, w_proj, w_up, w_down, vectors, b_up, seq_lengths, slot_of_seq
):
    section = lax.axis_index("pipe")
    replica = lax.axis_index("rep")
    member = lax.axis_index("group")
    rep_count = lax.axis_size("rep")
    count = lax.axis_size("group")
    micros, rows, width = block_input.shape[0], block_input.shape[2], block_input.shape[3]
    slot_ids = jnp.arange(seq_lengths.shape[0], dtype=jnp.int32)
    slot_len = jnp.sum(
        seq_lengths[:, None] * (slot_of_seq[:, None] == slot_ids[None, :]).astype(jnp.int32), axis=0
    )
    mine = jnp.arange(micros, dtype=jnp.int32) * rep_count + replica
    lengths = jnp.sum(
        slot_len[None, :] * (slot_ids[None, :] == mine[:, None]).astype(jnp.int32), axis=1
    )
    query_pos = member * rows + jnp.arange(rows, dtype=jnp.int32)
    valid = (query_pos[None, :] < lengths[:, None]).astype(jnp.float32)[:, :, None]
    cotangent = (out_grad[:, 0].astype(jnp.float32) * valid).reshape(micros * rows, width)

    bias_rows = b_up.shape[1] // vectors.shape[2]
    small = jnp.concatenate(
        [
            vectors[0],
            b_up[0].reshape(bias_rows, -1),
            jnp.zeros((8 - bias_rows, vectors.shape[2]), vectors.dtype),
        ],
        0,
    )
    thirds = [w_qkv[0][:, i * width : (i + 1) * width] for i in range(3)]
    first_in = block_input[:, 0].reshape(micros * rows, width).astype(jnp.float32)
    small_full, *full, arrived = first_layer(
        lengths,
        first_in,
        [in_blocks(array) for array in (small, *thirds, w_proj[0], w_up[0], w_down[0])],
        (
            (6, 0, 68, True),
            (5, 0, 16, True),
            (0, 0, 2, False),
            (1, 0, 17, False),
            (2, 0, 17, False),
            (3, 0, 17, False),
            (4, 0, 17, False),
            (5, 16, 1, False),
        ),
        count,
        micros,
    )
    vector_rows = small_full[:, 0].transpose(1, 0, 2).reshape(8, width).astype(jnp.float32)
    up_bias = small_full[:, 1, :bias_rows].reshape(1, -1).astype(jnp.float32)
    weights = [array.reshape(-1, array.shape[-1]) for array in full]

    def landed(blocks):
        return blocks.reshape(micros * rows, width).astype(jnp.float32)

    inputs = jnp.where(section == 0, first_in, landed(arrived))
    output, hidden, pre_act, attn_mixed, last_q, held, held_last, _ = forward_layer(
        lengths, inputs, vector_rows, up_bias, weights, count, micros
    )
    saved = (inputs, hidden, pre_act, held, held_last, last_q)
    *_, arrived = backward_layer(True, lengths, cotangent, saved, vector_rows, weights)
    grad_output = jnp.where(section == 1, cotangent, landed(arrived))
    (
        grad_in, grad_q, grad_k, grad_v, grad_one, grad_pre, activated, normed_one, normed_two,
        grad_vectors, grad_bias, _,
    ) = backward_layer(False, lengths, grad_output, saved, vector_rows, weights)

    small_grads = jnp.concatenate(
        [
            grad_vectors.reshape(8, count, -1).transpose(1, 0, 2),
            grad_bias.reshape(count, bias_rows, -1),
            jnp.zeros((count, 24 - bias_rows, width // count), jnp.float32),
        ],
        1,
    ).reshape(count * RING, 8, width // count)
    blocks = width // count // 8
    tall = grad_pre.shape[1] // count // 8
    half, tall_half = (blocks + 1) // 2, tall // 8 * 4 + 4
    arrays = {
        "Q": (0, 1, (blocks, 0, blocks), False),
        "K": (0, 2, (blocks, 0, blocks), False),
        "V": (0, 3, (blocks, 0, blocks), False),
        "P": (4, 5, (blocks, 0, blocks), False),
        "U": (6, 7, (blocks, 0, half), False),
        "u": (6, 7, (blocks, half, blocks - half), False),
        "D": (8, 9, (tall, 0, tall_half), True),
        "d": (8, 9, (tall, tall_half, tall - tall_half), True),
        "S": (10, None, (RING, 0, RING), False),
    }
    sums = sum_gradients(
        (
            normed_one, grad_q, grad_k, grad_v, attn_mixed, grad_one, normed_two, grad_pre, activated,
            grad_output.astype(jnp.bfloat16), small_grads,
        ),
        arrays,
        SUM_ORDER,
    )
    sums = dict(zip(arrays, sums))
    places = {
        "Q": (0, 0, 0, blocks),
        "K": (0, 0, width, blocks),
        "V": (0, 0, 2 * width, blocks),
        "P": (1, 0, 0, blocks),
        "U": (2, 0, 0, half),
        "u": (2, half * 8, 0, blocks - half),
        "D": (3, 0, 0, tall_half),
        "d": (3, tall_half * 8, 0, tall - tall_half),
    }
    grad_shapes = [(w.shape[1], w.shape[2]) for w in (w_qkv, w_proj, w_up, w_down)]
    totals = assemble(sums, places, grad_shapes)
    small_total = sums["S"].reshape(RING * 8, -1)
    edges = jnp.where(section == 0, grad_in, output).reshape(1, micros, 1, rows, width)
    return (
        edges,
        totals[0][None],
        totals[1][None],
        totals[2][None],
        totals[3][None],
        small_total[None, :8],
        small_total[8 : 8 + bias_rows].reshape(1, -1),
    )


def solution(mesh):
    in_specs = (
        P(None, "rep", "group", None),
        P(None, "rep", "group", None),
        P("pipe", "group", None),
        P("pipe", "group", None),
        P("pipe", "group", None),
        P("pipe", "group", None),
        P("pipe", None, "group"),
        P("pipe", "group"),
        P(),
        P(),
    )
    out_specs = (
        P("pipe", None, "rep", "group", None),
        P("pipe", "group", None),
        P("pipe", "group", None),
        P("pipe", "group", None),
        P("pipe", "group", None),
        P("pipe", None, "group"),
        P("pipe", "group"),
    )
    return jax.shard_map(body, mesh=mesh, in_specs=in_specs, out_specs=out_specs, check_vma=False)
```

```python
import functools
import jax
import jax.numpy as jnp
from jax import lax
from jax.experimental import pallas as pl
from jax.experimental.pallas import tpu as pltpu
from jax.sharding import PartitionSpec as P

HEAD = 64
LANES = 128
EPSILON = 1e-05
MASKED = -1e30
MESH = pl.DeviceIdType.MESH
RING = 4


def remote(src, dst, send_sem, recv_sem, device):
    return pltpu.make_async_remote_copy(
        src_ref=src,
        dst_ref=dst,
        send_sem=send_sem,
        recv_sem=recv_sem,
        device_id=device,
        device_id_type=MESH,
    )


def greet(devices):
    barrier = pltpu.get_barrier_semaphore()
    for device in devices:
        pl.semaphore_signal(barrier, inc=1, device_id=device, device_id_type=MESH)
    pl.semaphore_wait(barrier, len(devices))


def place():
    member, replica = lax.axis_index("group"), lax.axis_index("rep")
    return (member // 2, member % 2, replica // 2, replica % 2)


class Links:
    def __init__(self, send, recv):
        self.send, self.recv, self.used = send, recv, 0

    def channel(self, device):
        self.used += 1
        return Channel(self.send.at[self.used - 1], self.recv.at[self.used - 1], device)


class Channel:
    def __init__(self, send, recv, device):
        self.send_sem, self.recv_sem, self.device = send, recv, device

    def copy(self, src, dst):
        return remote(src, dst, self.send_sem, self.recv_sem, self.device)

    def send(self, src, dst):
        self.copy(src, dst).start()

    def sent(self, src):
        self.copy(src, src).wait_send()

    def came(self, dst):
        self.copy(dst, dst).wait_recv()


def near_devices():
    z, x, y, c = place()
    return {
        "above": {"group": 2 * ((z + 1) % RING) + x},
        "below": {"group": 2 * ((z + 3) % RING) + x},
        "partner": {"group": 2 * z + 1 - x},
        "sibling": {"rep": 2 * y + 1 - c},
        "next": {"rep": 2 * ((y + 1) % RING) + c},
        "last": {"rep": 2 * ((y + 3) % RING) + c},
    }


def gather_job(links, shard, full, first, size, spread):
    z, x, y, c = place()
    near = near_devices()
    xc = (x + c) % 2
    me = 2 * z + x
    base, above, below, across = (2 * ((z + k) % RING) + xc for k in (0, 1, 3, 2))
    piece = size // RING if spread else size
    low = piece - piece // 2
    finals = []

    def region(slot, owner, part=""):
        start = first + owner * piece if spread else first
        if part == "low":
            return full.at[slot, pl.ds(start, low)]
        if part == "high":
            return full.at[slot, pl.ds(start + low, piece - low)]
        return full.at[slot, pl.ds(start, piece)]

    def on_core(core, action):
        pl.when(c == core)(action)

    def always(action):
        action()

    def relay(channel, ref, run):
        run(lambda: channel.send(ref, ref))
        finals.append(lambda: run(lambda: channel.sent(ref)))

    def hand(slot, owner, run, part=""):
        channel = links.channel(near["sibling"])
        relay(channel, region(slot, owner, part), run)
        other = region(slot + 1 - 2 * xc, owner, part)
        get = (lambda action: on_core(0, action)) if run is not always else always
        finals.append(lambda: get(lambda: channel.came(other)))

    across_x = links.channel(near["partner"])
    up, down = links.channel(near["above"]), links.channel(near["below"])
    far_up, far_down = links.channel(near["above"]), links.channel(near["below"])
    own = shard.at[pl.ds(first + y * piece if spread else first, piece)]
    second = lambda action: on_core(1, action)

    def first_core():
        up.send(own, region(base, y))
        down.send(own, region(base, y))

    if spread:
        on_core(0, first_core)
    on_core(1, lambda: across_x.send(own, region(me, y)))
    finals.append(lambda: on_core(1, lambda: across_x.sent(own)))
    finals.append(lambda: up.sent(own))
    finals.append(lambda: down.sent(own))
    yield

    rings = []

    def pass_on(slot, run):
        if spread:
            forth, back = links.channel(near["next"]), links.channel(near["last"])
            relay(forth, region(slot, y), run)
            relay(back, region(slot, y), run)
            rings.append((slot, run, forth, back))
        hand(slot, y, run)

    def second_core():
        across_x.came(region(base, y))
        up.send(region(base, y), region(base, y))
        down.send(region(base, y), region(base, y))

    if not spread:
        on_core(0, first_core)
    on_core(1, second_core)
    pass_on(base, second)
    yield

    up.came(region(below, y))
    relay(far_up, region(below, y, "low"), always)
    pass_on(below, always)
    down.came(region(above, y))
    if piece > low:
        relay(far_down, region(above, y, "high"), always)
    pass_on(above, always)
    yield

    far_up.came(region(across, y, "low"))
    if piece > low:
        far_down.came(region(across, y, "high"))
    pass_on(across, always)
    yield

    if spread:
        ends = []
        for slot, run, forth, back in rings:
            far_forth, far_back = links.channel(near["next"]), links.channel(near["last"])
            behind, ahead = (y + 3) % RING, (y + 1) % RING
            run(lambda: forth.came(region(slot, behind)))
            relay(far_forth, region(slot, behind, "low"), run)
            hand(slot, behind, run)
            run(lambda: back.came(region(slot, ahead)))
            if piece > low:
                relay(far_back, region(slot, ahead, "high"), run)
            hand(slot, ahead, run)
            ends.append((slot, run, far_forth, far_back))
        yield
        for slot, run, far_forth, far_back in ends:
            far = (y + 2) % RING
            run(lambda: far_forth.came(region(slot, far, "low")))
            if piece > low:
                run(lambda: far_back.came(region(slot, far, "high")))
            hand(slot, far, run)
        yield
    for action in finals:
        action()


MAX_LINKS = 160


GATHER_ORDER = "SPSPSSPP"


def gather_steps(links, plan, ins, outs):
    member = lax.axis_index("group")
    count = len(ins)
    spread = [gather_job(links, ins[i], outs[i], *rest) for i, *rest in plan if rest[-1]]
    whole = [gather_job(links, ins[i], outs[i], *rest) for i, *rest in plan if not rest[-1]]
    owns = [links.channel(near_devices()["sibling"]) for _ in range(count)]
    for step, which in enumerate(GATHER_ORDER):
        for job in spread if which == "S" else whole:
            next(job)
        if step == 1:
            for i in range(count):
                owns[i].send(ins[i], outs[i].at[member])
    for job in whole:
        for _ in job:
            pass
    for i in range(count):
        owns[i].came(outs[i].at[member])
        owns[i].sent(ins[i])
    yield
    for job in spread:
        next(job)
    yield
    for job in spread:
        for _ in job:
            pass
    yield


def spread_vectors(small, vectors, up_bias):
    members, _, _, columns = small.shape
    bias_rows = up_bias.shape[1] // (members * columns)
    for member in range(members):
        first = member * columns
        vectors[:, first : first + columns] = small[member, 0].astype(jnp.float32)
        for row in range(bias_rows):
            first = (member * bias_rows + row) * columns
            up_bias[:, first : first + columns] = small[member, 1, row : row + 1].astype(jnp.float32)


def piece_rows(blocks):
    starts = [i * blocks // RING for i in range(RING + 1)]
    return max(starts[i + 1] - starts[i] for i in range(RING))


def add_blocks(count, dst, terms):
    def step(b, carry):
        total = dst[b].astype(jnp.float32)
        for term in terms:
            total = total + term[b].astype(jnp.float32)
        dst[b] = total.astype(dst.dtype)
        return carry

    lax.fori_loop(0, count, step, 0)


TILE = 256


def product_into(left, right, whole, stage, sems):
    def copy(tile, first, size):
        src = stage.at[tile % 2, pl.ds(0, size // 8)]
        return pltpu.make_async_copy(src, whole.at[pl.ds(first // 8, size // 8)], sems.at[tile % 2])

    tiles = [(t, *chunk) for t, chunk in enumerate(column_chunks(left.shape[1], TILE))]
    for t, first, size in tiles:
        if t >= 2:
            copy(*tiles[t - 2]).wait()
        for column, width in column_chunks(right.shape[1], 1152):
            tile = over_rows(left[:, first : first + size], right[:, column : column + width])
            stage[t % 2, 0 : size // 8, :, column : column + width] = tile.reshape(
                size // 8, 8, width
            ).astype(stage.dtype)
        copy(t, first, size).start()
    for tile in tiles[-2:]:
        copy(*tile).wait()


def sum_job(links, fill, whole, chunk, spread, total, stage, loads, buffers, out, kept):
    z, x, y, c = place()
    near = near_devices()
    shard_blocks, chunk_first, blocks = chunk
    xc = (x + c) % 2
    cross_core = {"group": 2 * z + 1 - x, "rep": 2 * y + 1 - c}
    others = [{"rep": 2 * ((y + j) % RING) + c} for j in range(1, RING)]
    far_low, far_high, from_below, from_above, cross = buffers[:5]
    size = blocks // RING if spread else blocks
    first = y * size if spread else 0
    low = size // 2
    order = (2, 1, 3, 0)
    finals = []

    def on_core(core, action):
        def run():
            action()

        pl.when(c == core)(run)

    def launch(device, src, dst):
        channel = links.channel(device)
        channel.send(src, dst)
        finals.append(lambda: channel.sent(src))
        return channel

    def shard(k, column):
        slot = 2 * ((z + k) % RING) + column
        return whole.at[pl.ds(slot * shard_blocks + chunk_first, blocks)]

    def rows(k, start, count):
        return total.at[k, pl.ds(start, count)]

    fill()
    swaps = [launch(near["sibling"], shard(k, 1 - xc), total.at[k]) for k in order]
    yield

    def load(n):
        space = stage.at[n % 2, pl.ds(0, blocks)]
        return pltpu.make_async_copy(shard(order[n], xc), space, loads.at[n % 2])

    def send_far():
        up = launch(near["above"], rows(2, first, low), far_low)
        down = launch(near["below"], rows(2, first + low, size - low), far_high)
        return (up, down)

    load(0).start()
    load(1).start()
    for n, k in enumerate(order):
        load(n).wait()
        swaps[n].came(total.at[k])
        add_blocks(blocks, total.at[k], [stage.at[n % 2]])
        if n + 2 < RING:
            load(n + 2).start()
        if k == 2 and not spread:
            far = send_far()
    if spread:
        ring_low, ring_high, from_last, from_next = buffers[5:9]
        ahead, behind, opposite = ((y + j) % RING * size for j in (1, 3, 2))

        def quarter(start, count):
            return total.at[:, pl.ds(start, count)]

        forth = launch(near["next"], quarter(opposite, low), ring_low)
        back = launch(near["last"], quarter(opposite + low, size - low), ring_high)
        yield
        forth.came(ring_low)
        for k in range(RING):
            add_blocks(low, rows(k, ahead, low), [ring_low.at[k]])
        forth = launch(near["next"], quarter(ahead, size), from_last)
        back.came(ring_high)
        for k in range(RING):
            add_blocks(size - low, rows(k, behind + low, size - low), [ring_high.at[k]])
        back = launch(near["last"], quarter(behind, size), from_next)
        yield
        forth.came(from_last)
        back.came(from_next)
        for k in order:
            add_blocks(size, rows(k, first, size), [from_last.at[k], from_next.at[k]])
            if k == 2:
                far = send_far()
    yield
    far[0].came(far_low)
    add_blocks(low, rows(1, first, low), [far_low])
    up = launch(near["above"], rows(1, first, size), from_below)
    far[1].came(far_high)
    add_blocks(size - low, rows(3, first + low, size - low), [far_high])
    down = launch(near["below"], rows(3, first, size), from_above)
    yield
    up.came(from_below)
    down.came(from_above)
    mine = rows(0, first, size)
    add_blocks(size, mine, [from_below, from_above])
    over_x = links.channel(cross_core)
    on_core(1, lambda: over_x.send(mine, cross))
    finals.append(lambda: on_core(1, lambda: over_x.sent(mine)))
    yield

    def take_x():
        over_x.came(cross)
        add_blocks(size, mine, [cross])

    on_core(0, take_x)
    if spread:
        result = mine
    else:
        ring, result = buffers[5:7]
        piece = result.shape[0]
        over_y = [links.channel(device) for device in others]

        def part(owner):
            return total.at[0, pl.ds((owner * blocks) // RING, piece)]

        def send_y():
            for j in (2, 1, 3):
                over_y[j - 1].send(part((y + j) % RING), ring.at[j - 1])

        on_core(0, send_y)
        finals.append(
            lambda: on_core(0, lambda: [over_y[j].sent(part((y + j + 1) % RING)) for j in range(3)])
        )
        yield

        def take_y():
            for j in range(RING - 1):
                over_y[j].came(ring.at[j])
            own = part(y)

            def step(b, carry):
                value = own[b].astype(jnp.float32)
                for j in range(RING - 1):
                    value = value + ring[j, b].astype(jnp.float32)
                result[b] = value.astype(result.dtype)
                return carry

            lax.fori_loop(0, piece, step, 0)

        on_core(0, take_y)
    shares = [links.channel(device) for device in others]
    keep = pltpu.make_async_copy(result, out.at[y], kept)

    def share():
        for j in (2, 1, 3):
            shares[j - 1].send(result, out.at[y])
        keep.start()

    on_core(0, share)
    finals.append(lambda: on_core(0, lambda: [channel.sent(result) for channel in shares]))
    yield
    hand = links.channel(near["sibling"])

    def pass_on():
        keep.wait()
        for j in (1, 2, 3):
            shares[j - 1].came(out.at[(y + RING - j) % RING])
        hand.send(out, out)

    on_core(0, pass_on)
    finals.append(lambda: on_core(0, lambda: hand.sent(out)))
    yield
    on_core(1, lambda: hand.came(out))
    for action in finals:
        action()


SUM_LINKS = 200
SUM_ORDER = ("KQDKUQKuQDVKUdDKQuPVQUSudDVPKSQdKUQKQUud", "DUVuUPSdVuUDVDuPSVudDVPSdDPSdPSdPS")
SUM_OPERANDS = 11


def sum_kernel(arrays, order, *refs):
    operands, refs = refs[:SUM_OPERANDS], refs[SUM_OPERANDS:]
    count = len(arrays)
    outs, refs = refs[:count], refs[count:]
    pairs = product_pairs(arrays)
    wholes, refs = dict(zip(pairs, refs)), refs[len(pairs) :]
    send, recv, kept, sems, loads = refs[:5]
    narrow_fill, wide_fill, narrow_stage, wide_stage, tall_stage, small_stage = refs[5:11]
    refs = refs[11:]
    links = Links(send, recv)
    z, x, y, c = place()
    near = near_devices()
    greet(
        [near["above"], near["below"], near["sibling"]]
        + [{"group": 2 * z + 1 - x, "rep": 2 * y + 1 - c}]
        + [{"rep": 2 * ((y + j) % RING) + c} for j in range(1, RING)]
    )
    jobs = {}
    for i, (name, (left, right, chunk, spread)) in enumerate(arrays.items()):
        buffers, refs = refs[:10], refs[10:]
        stage, fill = narrow_stage, lambda: None
        if right is None:
            whole, stage = operands[left], small_stage
        else:
            whole, space = wholes[left, right], narrow_fill
            if outs[i].shape[-1] > 2048:
                space, stage = wide_fill, wide_stage
            elif spread:
                stage = tall_stage
            if chunk[1] == 0:
                fill = functools.partial(
                    product_into, operands[left], operands[right], whole, space, sems
                )
        jobs[name] = sum_job(
            links, fill, whole, chunk, spread, buffers[0], stage, loads, buffers[1:], outs[i], kept.at[i]
        )
    for name in "".join(order):
        next(jobs[name], None)
    for job in jobs.values():
        for _ in job:
            pass


def product_pairs(arrays):
    return list(dict.fromkeys((a[0], a[1]) for a in arrays.values() if a[1] is not None))


def sum_gradients(operands, arrays, order):
    dma = pltpu.SemaphoreType.DMA
    vmem, hbm = pl.BlockSpec(memory_space=pltpu.VMEM), pl.BlockSpec(memory_space=pl.ANY)
    bf16 = jnp.bfloat16
    outs, wholes, scratch, deepest = [], {}, [], {}
    for left, right, chunk, spread in arrays.values():
        shard_blocks, _, blocks = chunk
        if right is None:
            width, dtype = operands[left].shape[-1], operands[left].dtype
        else:
            width, dtype = operands[right].shape[1], bf16
            wholes[left, right] = jax.ShapeDtypeStruct((8 * shard_blocks, 8, width), dtype)
            kind = (width, spread)
            deepest[kind] = max(blocks, deepest.get(kind, 0))
        piece = piece_rows(blocks)
        outs.append(jax.ShapeDtypeStruct((RING, piece, 8, width), dtype))
        size = blocks // RING if spread else blocks
        low = size // 2
        leads = [(RING, blocks), (low,), (size - low,), (size,), (size,), (size,)]
        if spread:
            leads += [(RING, low), (RING, size - low), (RING, size), (RING, size)]
        else:
            leads += [(RING - 1, piece), (piece,), (1,), (1,)]
        scratch += [pltpu.VMEM(lead + (8, width), dtype) for lead in leads]
    narrow_width, wide_width = (pick(width for width, _ in deepest) for pick in (min, max))
    small_shape = operands[-1].shape
    stages = [(narrow_width, False), (wide_width, False), (narrow_width, True)]
    return pl.pallas_call(
        functools.partial(sum_kernel, arrays, order),
        out_shape=outs + list(wholes.values()),
        in_specs=[vmem] * (len(operands) - 1) + [hbm],
        out_specs=[hbm] * (len(outs) + len(wholes)),
        scratch_shapes=[
            dma((SUM_LINKS,)),
            dma((SUM_LINKS,)),
            dma((len(outs),)),
            dma((2,)),
            dma((2,)),
            pltpu.VMEM((2, TILE // 8, 8, narrow_width), bf16),
            pltpu.VMEM((2, TILE // 8, 8, wide_width), bf16),
        ]
        + [pltpu.VMEM((2, deepest[kind], 8, kind[0]), bf16) for kind in stages]
        + [pltpu.VMEM((2, small_shape[0] // 8) + small_shape[1:], operands[-1].dtype)]
        + scratch,
        compiler_params=pltpu.CompilerParams(
            collective_id=1, has_side_effects=True, vmem_limit_bytes=62 * 1024 * 1024
        ),
        name="sum_gradients",
    )(*operands)[: len(outs)]


def assemble_kernel(names, places, *refs):
    sources, refs = refs[: len(names)], refs[len(names) :]
    loaded, sems = refs[-1 - len(names) : -1], refs[-1]
    outs = refs[: -1 - len(names)]
    loads = [
        pltpu.make_async_copy(source, ref, sems.at[i])
        for i, (source, ref) in enumerate(zip(sources, loaded))
    ]
    for load in loads:
        load.start()
    for name, ref, load in zip(names, loaded, loads):
        load.wait()
        output, row, column, blocks = places[name]
        width = ref.shape[-1]
        for i in range(RING):
            first, end = i * blocks // RING, (i + 1) * blocks // RING
            value = ref[i, 0 : end - first].astype(jnp.float32).reshape((end - first) * 8, width)
            outs[output][row + first * 8 : row + end * 8, column : column + width] = value


def assemble(sums, places, shapes):
    names = tuple(places)
    vmem, hbm = pl.BlockSpec(memory_space=pltpu.VMEM), pl.BlockSpec(memory_space=pl.ANY)
    return pl.pallas_call(
        functools.partial(assemble_kernel, names, places),
        out_shape=[jax.ShapeDtypeStruct(shape, jnp.float32) for shape in shapes],
        in_specs=[hbm] * len(names),
        out_specs=[vmem] * len(shapes),
        scratch_shapes=[pltpu.VMEM(sums[name].shape, sums[name].dtype) for name in names]
        + [pltpu.SemaphoreType.DMA((len(names),))],
        compiler_params=pltpu.CompilerParams(vmem_limit_bytes=62 * 1024 * 1024),
        name="assemble",
    )(*(sums[name] for name in names))


def lane_head(shape):
    return lax.broadcasted_iota(jnp.int32, shape, len(shape) - 1) // HEAD


def one_head(matrix, head):
    return jnp.where(lane_head(matrix.shape) == head, matrix, jnp.zeros_like(matrix))


def over_lanes(left, right):
    return lax.dot_general(left, right, (((1,), (1,)), ((), ())), preferred_element_type=jnp.float32)


def over_rows(left, right):
    return lax.dot_general(left, right, (((0,), (0,)), ((), ())), preferred_element_type=jnp.float32)


def plain(left, right):
    return jnp.dot(left, right, preferred_element_type=jnp.float32)


def half_selector(first):
    rows = lax.broadcasted_iota(jnp.int32, (HEAD, LANES), 0)
    lanes = lax.broadcasted_iota(jnp.int32, (HEAD, LANES), 1)
    return (rows + first == lanes).astype(jnp.bfloat16)


def widen(matrix, first):
    return plain(matrix, half_selector(first)).astype(jnp.bfloat16)


def narrow(matrix, first):
    return over_lanes(matrix, half_selector(first)).astype(jnp.bfloat16)


def soft_columns(key_rows, queries, first_query, length):
    scores = over_lanes(key_rows, queries) * HEAD ** (-0.5)
    key_pos = lax.broadcasted_iota(jnp.int32, scores.shape, 0)
    query_pos = first_query + lax.broadcasted_iota(jnp.int32, scores.shape, 1)
    scores = jnp.where((key_pos <= query_pos) & (key_pos < length), scores, MASKED)
    exponent = jnp.exp(scores - jnp.max(scores, 0, keepdims=True))
    return exponent * (1.0 / jnp.sum(exponent, 0, keepdims=True))


def peers(count):
    member = lax.axis_index("group")
    ahead = [(member + j) % count for j in range(1, count)]
    return (member, ahead)


def normalize(inputs):
    average = jnp.mean(inputs, -1, keepdims=True)
    centered = inputs - average
    variance = jnp.mean(centered * centered, -1, keepdims=True)
    scale = lax.rsqrt(variance + EPSILON)
    return (centered * scale, scale)


def norm_back(unit, scale, gain, grad):
    scaled = grad * gain
    pulled = scaled - jnp.mean(scaled, -1, keepdims=True)
    pulled = pulled - unit * jnp.mean(scaled * unit, -1, keepdims=True)
    return (
        pulled * scale,
        jnp.sum(grad * unit, 0, keepdims=True),
        jnp.sum(grad, 0, keepdims=True),
    )


GELU_IN, GELU_CUBE = 0.7978845608028654, 0.044715


def gelu_parts(value):
    square = value * value
    bent = jnp.tanh(GELU_IN * value * (1.0 + GELU_CUBE * square))
    half = 0.5 * (1.0 + bent)
    slope = half + 0.5 * value * (1.0 - bent * bent) * GELU_IN * (1.0 + 3.0 * GELU_CUBE * square)
    return (value * half, slope)


def column_chunks(width, most):
    return [(first, min(most, width - first)) for first in range(0, width, most)]


FORWARD_WEIGHTS = ("q", "k", "v", "proj", "up", "down")


def first_kernel(plan, count, *refs):
    lengths, inputs = refs[:2]
    shards, fulls = refs[2 : 2 + count], refs[2 + count : 2 + 2 * count]
    arrived, refs = refs[2 + 2 * count], refs[3 + 2 * count :]
    vectors, up_bias, small, send, recv, loaded, *refs = refs
    near = near_devices()
    member, ahead = peers(8)
    greet(
        [{"group": peer} for peer in ahead]
        + [near[name] for name in ("sibling", "next", "last")]
        + [{"pipe": 1 - lax.axis_index("pipe")}]
    )
    steps = gather_steps(Links(send, recv), plan, shards, fulls)
    next(steps)
    load = pltpu.make_async_copy(fulls[0], small, loaded)
    load.start()
    load.wait()
    spread_vectors(small, vectors, up_bias)
    outputs, scratch = refs[:7], refs[7:]
    forward_kernel(
        steps, lengths, inputs, vectors, up_bias, *fulls[1:], *outputs, arrived, *scratch
    )


def first_layer(lengths, inputs, shards, plan, count, micros):
    total, width = inputs.shape
    rows, lanes, hidden = total // micros, LANES, shards[5].shape[2]
    bf16, f32 = jnp.bfloat16, jnp.float32
    vmem, hbm = pl.BlockSpec(memory_space=pltpu.VMEM), pl.BlockSpec(memory_space=pl.ANY)
    dma = pltpu.SemaphoreType.DMA
    pack, blocks = (count, micros, 3, rows, lanes), (count, micros, rows, lanes)
    return pl.pallas_call(
        functools.partial(first_kernel, plan, len(shards)),
        out_shape=[jax.ShapeDtypeStruct((8,) + s.shape, s.dtype) for s in shards]
        + [jax.ShapeDtypeStruct((micros, rows, width), bf16)],
        in_specs=[pl.BlockSpec(memory_space=pltpu.SMEM), vmem] + [hbm] * len(shards),
        out_specs=[hbm] * (len(shards) + 1),
        scratch_shapes=[
            pltpu.VMEM((8, width), f32),
            pltpu.VMEM((1, hidden), f32),
            pltpu.VMEM((8,) + shards[0].shape, bf16),
            dma((MAX_LINKS,)),
            dma((MAX_LINKS,)),
            dma,
            pltpu.VMEM((total, width), f32),
            pltpu.VMEM((total, width), f32),
            pltpu.VMEM((total, hidden), f32),
            pltpu.VMEM((total, width), bf16),
            pltpu.VMEM((micros, rows, lanes), bf16),
            pltpu.VMEM((8, 8), f32),
            pltpu.VMEM((8, 8), f32),
        ]
        + [pltpu.VMEM((s.shape[0] * 64, s.shape[2]), bf16) for s in shards[1:]]
        + [
            pltpu.VMEM(pack, bf16),
            pltpu.VMEM((micros, rows, lanes), bf16),
            pltpu.VMEM(pack, bf16),
            pltpu.VMEM(blocks, bf16),
            pltpu.VMEM(blocks, bf16),
            pltpu.VMEM(blocks, bf16),
            pltpu.VMEM((micros, rows, width), bf16),
        ]
        + [dma((micros, count - 1))] * 6
        + [dma((micros, 4)), dma((6,)), dma((micros,)), dma((micros,))],
        compiler_params=pltpu.CompilerParams(
            collective_id=0, has_side_effects=True, vmem_limit_bytes=62 * 1024 * 1024
        ),
        name="gather_forward",
    )(lengths, inputs, *shards)


def shipment(source, arrived, send, recv):
    device = {"pipe": 1 - lax.axis_index("pipe")}
    return lambda m: remote(source.at[m], arrived.at[m], send.at[m], recv.at[m], device)


def forward_kernel(
    ship, lengths, inputs, vectors, up_bias, wq, wk, wv, wproj, wup, wdown,
    output, hidden_out, pre_act, attn_mixed, last_q, kept, kept_last, arrived,
    vq, vk, vv, vproj, vup, vdown, pack, last_kv, held, held_last, staged, mixed, leaving,
    send, recv, send_last, recv_last, send_back, recv_back, local, loaded, send_ship, recv_ship,
):
    count, micros, _, rows, lanes = pack.shape
    member, ahead = peers(count)
    wide = count * lanes
    sources, places = (wq, wk, wv, wproj, wup, wdown), (vq, vk, vv, vproj, vup, vdown)
    loads = [
        pltpu.make_async_copy(sources[i].reshape(places[i].shape), places[i], loaded.at[i])
        if ship
        else pltpu.make_async_copy(sources[i], places[i], loaded.at[i])
        for i in range(len(sources))
    ]
    for load in loads[:4] if ship else loads:
        load.start()
    if not ship:
        greet([{"group": peer} for peer in ahead])
    ship_copy = shipment(leaving, arrived, send_ship, recv_ship)

    def out(m, j):
        return remote(
            pack.at[ahead[j], m], held.at[member, m], send.at[m, j], recv.at[m, j], {"group": ahead[j]}
        )

    def out_last(m, j):
        return remote(
            last_kv.at[m],
            held_last.at[member, m],
            send_last.at[m, j],
            recv_last.at[m, j],
            {"group": ahead[j]},
        )

    def back(m, j):
        return remote(
            staged.at[ahead[j], m],
            mixed.at[member, m],
            send_back.at[m, j],
            recv_back.at[m, j],
            {"group": ahead[j]},
        )

    def own(m):
        return (
            pltpu.make_async_copy(pack.at[member, m], held.at[member, m], local.at[m, 0]),
            pltpu.make_async_copy(last_kv.at[m], held_last.at[member, m], local.at[m, 1]),
        )

    def own_back(m):
        return pltpu.make_async_copy(staged.at[member, m], mixed.at[member, m], local.at[m, 2])

    def keep():
        return (
            pltpu.make_async_copy(held, kept, local.at[0, 3]),
            pltpu.make_async_copy(held_last, kept_last, local.at[1, 3]),
        )

    peer_range = range(count - 1)
    unit, _ = normalize(inputs[...])
    normed = (unit * vectors[0:1] + vectors[1:2]).astype(jnp.bfloat16)
    lasts = []
    for third, (weight, bias) in enumerate(((vq, 2), (vk, None), (vv, 3))):
        loads[third].wait()
        product = plain(normed, weight[...])
        if bias is not None:
            product = product + vectors[bias : bias + 1]
        product = product.astype(jnp.bfloat16)
        for d in range(count):
            for m in range(micros):
                pack[d, m, third] = product[m * rows : (m + 1) * rows, d * lanes : (d + 1) * lanes]
        lasts.append(product[:, wide:])
    wide_q = widen(lasts[0], 0)
    both_last = widen(lasts[1], 0) + widen(lasts[2], HEAD)
    for m in range(micros):
        last_q[m] = wide_q[m * rows : (m + 1) * rows]
        last_kv[m] = both_last[m * rows : (m + 1) * rows]
    for m in range(micros):
        for j in peer_range:
            out(m, j).start()
            out_last(m, j).start()
        for copy in own(m):
            copy.start()

    def micro(m):
        for copy in own(m):
            copy.wait()
        for j in peer_range:
            out(m, j).wait_recv()
            out_last(m, j).wait_recv()
        length = lengths[m]
        span = 2
        for block in range(count // span):
            reach = span * (block + 1)
            queries = held[span * block : reach, m, 0].reshape(span * rows, lanes)
            key_rows = held[0:reach, m, 1].reshape(reach * rows, lanes)
            values = held[0:reach, m, 2].reshape(reach * rows, lanes)

            def head_step(head, total):
                probs = soft_columns(
                    key_rows, one_head(queries, head), span * block * rows, length
                ).astype(jnp.bfloat16)
                return total + over_rows(one_head(values, head), probs)

            total = lax.fori_loop(0, 2, head_step, jnp.zeros((lanes, span * rows), jnp.float32))
            staged[span * block : reach, m] = (
                total.T.astype(jnp.bfloat16).reshape(span, rows, lanes)
            )
        for j in peer_range:
            back(m, j).start()
        own_back(m).start()
        both = held_last[:, m].reshape(count * rows, lanes)
        probs = soft_columns(both, last_q[m], member * rows, length).astype(jnp.bfloat16)
        last_out = over_rows(both, probs).T.astype(jnp.bfloat16)
        attn_mixed[m * rows : (m + 1) * rows, wide:] = narrow(last_out, HEAD)

    for m in range(micros):
        if ship and m == 0:
            next(ship)
        micro(m)
        if ship and m == 0:
            next(ship)
            for load in loads[4:]:
                load.start()
    for copy in () if ship else keep():
        copy.start()
    for m in range(micros):
        here = slice(m * rows, (m + 1) * rows)
        own_back(m).wait()
        for j in peer_range:
            back(m, j).wait_recv()
        for d in range(count):
            attn_mixed[here, d * lanes : (d + 1) * lanes] = mixed[d, m]
        if m == 0:
            loads[3].wait()
        hidden = inputs[here] + plain(attn_mixed[here], vproj[...]) + vectors[4:5]
        hidden_out[here] = hidden
        unit, _ = normalize(hidden)
        normed = (unit * vectors[5:6] + vectors[6:7]).astype(jnp.bfloat16)
        output[here] = hidden + vectors[7:8]
        if m == 0:
            loads[4].wait()
            loads[5].wait()
        for first, size in column_chunks(pre_act.shape[1], 1152):
            columns = slice(first, first + size)
            value = plain(normed, vup[:, columns]) + up_bias[:, columns]
            pre_act[here, columns] = value
            activated, _ = gelu_parts(value)
            output[here] += plain(activated.astype(jnp.bfloat16), vdown[columns, :])
        if ship:
            leaving[m] = output[here].astype(jnp.bfloat16)
            ship_copy(m).start()
    for m in range(micros):
        for j in peer_range:
            out(m, j).wait_send()
            out_last(m, j).wait_send()
            back(m, j).wait_send()
        if ship:
            ship_copy(m).wait()
    for copy in () if ship else keep():
        copy.wait()


def results_in_scratch(kernel, inputs, results):
    def run(*refs):
        before, last, rest = refs[:inputs], refs[inputs], refs[inputs + 1 :]
        kernel(*before, *rest[: results - 1], last, *rest[results - 1 :])

    return run


def layer_call(kernel, ship, operands, in_specs, results, spaces, scratch, **options):
    kernel = functools.partial(kernel, ship)
    if ship:
        kernel = results_in_scratch(kernel, len(operands), len(results))
        scratch = [pltpu.VMEM(r.shape, r.dtype) for r in results[:-1]] + scratch
        results, spaces = results[-1:], spaces[-1:]
    return pl.pallas_call(
        kernel,
        out_shape=results,
        in_specs=in_specs,
        out_specs=spaces,
        scratch_shapes=scratch,
        **options,
    )(*operands)


def forward_layer(lengths, inputs, vectors, up_bias, weights, count, micros):
    total, width = inputs.shape
    rows, lanes = total // micros, LANES
    hidden = weights[4].shape[1]
    bf16, f32 = jnp.bfloat16, jnp.float32
    vmem, hbm = pl.BlockSpec(memory_space=pltpu.VMEM), pl.BlockSpec(memory_space=pl.ANY)
    dma = pltpu.SemaphoreType.DMA
    pack, blocks = (count, micros, 3, rows, lanes), (count, micros, rows, lanes)
    return layer_call(
        forward_kernel,
        False,
        (lengths, inputs, vectors, up_bias, *weights),
        [pl.BlockSpec(memory_space=pltpu.SMEM)] + [vmem] * 3 + [hbm] * 6,
        [
            jax.ShapeDtypeStruct((total, width), f32),
            jax.ShapeDtypeStruct((total, width), f32),
            jax.ShapeDtypeStruct((total, hidden), f32),
            jax.ShapeDtypeStruct((total, width), bf16),
            jax.ShapeDtypeStruct((micros, rows, lanes), bf16),
            jax.ShapeDtypeStruct(pack, bf16),
            jax.ShapeDtypeStruct(blocks, bf16),
            jax.ShapeDtypeStruct((micros, rows, width), bf16),
        ],
        [vmem] * 5 + [hbm] * 3,
        [pltpu.VMEM(w.shape, bf16) for w in weights]
        + [
            pltpu.VMEM(pack, bf16),
            pltpu.VMEM((micros, rows, lanes), bf16),
            pltpu.VMEM(pack, bf16),
            pltpu.VMEM(blocks, bf16),
            pltpu.VMEM(blocks, bf16),
            pltpu.VMEM(blocks, bf16),
            pltpu.VMEM((micros, rows, width), bf16),
        ]
        + [dma((micros, count - 1))] * 6
        + [dma((micros, 4)), dma((6,)), dma((micros,)), dma((micros,))],
        compiler_params=pltpu.CompilerParams(
            collective_id=2, has_side_effects=True, vmem_limit_bytes=60 * 1024 * 1024
        ),
        name="forward_layer",
    )


def backward_kernel(
    ship, lengths, grad_output, inputs, hidden, vectors, pre_act, held, held_last, last_q,
    wq, wk, wv, wproj, wup, wdown,
    grad_in, grad_q, grad_k, grad_v, grad_one, grad_pre, activated, normed_one, normed_two,
    vector_grads, bias_grads, arrived,
    vproj, vup, vdown, vqkv, grad_norm, grad_pack, last_grad, came, staged, staged_last, grads, parts_last,
    key_total, value_total, last_query_grad, leaving,
    send, recv, send_back, recv_back, send_last, recv_last, local, loaded, send_ship, recv_ship,
):
    count, micros, _, rows, lanes = held.shape
    member, ahead = peers(count)
    wide = count * lanes
    scale = HEAD ** (-0.5)
    loads = [
        pltpu.make_async_copy(source, target, loaded.at[i])
        for i, (source, target) in enumerate(
            (
                (wdown, vdown),
                (wup, vup),
                (wproj, vproj),
                (wq, vqkv.at[0]),
                (wk, vqkv.at[1]),
                (wv, vqkv.at[2]),
            )
        )
    ]
    for load in loads:
        load.start()
    devices = [{"group": peer} for peer in ahead]
    if ship:
        devices.append({"pipe": 1 - lax.axis_index("pipe")})
    greet(devices)
    ship_copy = shipment(leaving, arrived, send_ship, recv_ship)

    def out(m, j):
        return remote(
            grad_pack.at[ahead[j], m],
            came.at[member, m],
            send.at[m, j],
            recv.at[m, j],
            {"group": ahead[j]},
        )

    def back(m, j):
        return remote(
            staged.at[ahead[j], m],
            grads.at[member, m],
            send_back.at[m, j],
            recv_back.at[m, j],
            {"group": ahead[j]},
        )

    def back_last(m, j):
        return remote(
            staged_last.at[ahead[j], m],
            parts_last.at[member, m],
            send_last.at[m, j],
            recv_last.at[m, j],
            {"group": ahead[j]},
        )

    def own(m):
        return pltpu.make_async_copy(grad_pack.at[member, m], came.at[member, m], local.at[m, 0])

    def own_back(m):
        return (
            pltpu.make_async_copy(staged.at[member, m], grads.at[member, m], local.at[m, 1]),
            pltpu.make_async_copy(
                staged_last.at[member, m], parts_last.at[member, m], local.at[m, 2]
            ),
        )

    def column_sum(matrix):
        return jnp.sum(matrix.astype(jnp.float32), 0, keepdims=True)

    peer_range = range(count - 1)
    grad_two = grad_output[...].astype(jnp.bfloat16)
    if not ship:
        vector_grads[7:8] = column_sum(grad_two)
    loads[0].wait()
    for first, size in column_chunks(pre_act.shape[1], 1152):
        columns = slice(first, first + size)
        value, slope = gelu_parts(pre_act[:, columns])
        if not ship:
            activated[:, columns] = value.astype(jnp.bfloat16)
        part = (slope * over_lanes(grad_two, vdown[columns, :])).astype(jnp.bfloat16)
        grad_pre[:, columns] = part
        if not ship:
            bias_grads[:, columns] = column_sum(part)
        if first == 0:
            loads[1].wait()
            grad_norm[...] = over_lanes(part, vup[:, columns])
        else:
            grad_norm[...] += over_lanes(part, vup[:, columns])
    unit, deviation = normalize(hidden[...])
    if not ship:
        normed_two[...] = (unit * vectors[5:6] + vectors[6:7]).astype(jnp.bfloat16)
    from_norm, gain_sum, bias_sum = norm_back(unit, deviation, vectors[5:6], grad_norm[...])
    vector_grads[5:6] = gain_sum
    vector_grads[6:7] = bias_sum
    grad_hidden = grad_output[...] + from_norm
    grad_norm[...] = grad_hidden
    one = grad_hidden.astype(jnp.bfloat16)
    grad_one[...] = one
    if not ship:
        vector_grads[4:5] = column_sum(one)
    loads[2].wait()
    grad_mixed = over_lanes(one, vproj[...]).astype(jnp.bfloat16)
    for m in range(micros):
        for d in range(count):
            grad_pack[d, m] = grad_mixed[m * rows : (m + 1) * rows, d * lanes : (d + 1) * lanes]
        for j in peer_range:
            out(m, j).start()
        own(m).start()
    wide_last = widen(grad_mixed[:, wide:], HEAD)
    for m in range(micros):
        last_grad[m] = wide_last[m * rows : (m + 1) * rows]

    def last_head(m):
        length = lengths[m]
        both = held_last[:, m].reshape(count * rows, lanes)
        probs = soft_columns(both, last_q[m], member * rows, length)
        grad_probs = over_lanes(both, last_grad[m])
        inner = jnp.sum(probs * grad_probs, 0, keepdims=True)
        grad_scores = (probs * (grad_probs - inner)).astype(jnp.bfloat16)
        query_grad = (scale * over_rows(both, grad_scores)).T.astype(jnp.bfloat16)
        grad_q[m * rows : (m + 1) * rows, wide:] = narrow(query_grad, 0)
        both_grad = scale * plain(grad_scores, last_q[m]) + plain(
            probs.astype(jnp.bfloat16), last_grad[m]
        )
        staged_last[:, m] = both_grad.astype(jnp.bfloat16).reshape(count, rows, lanes)
        for j in peer_range:
            back_last(m, j).start()

    def micro(m):
        length = lengths[m]
        own(m).wait()
        for j in peer_range:
            out(m, j).wait_recv()
        key_total[...] = jnp.zeros_like(key_total)
        value_total[...] = jnp.zeros_like(value_total)
        span = 2
        for block in range(count // span):
            reach = span * (block + 1)
            queries = held[span * block : reach, m, 0].reshape(span * rows, lanes)
            grad_out = came[span * block : reach, m].reshape(span * rows, lanes)
            key_rows = held[0:reach, m, 1].reshape(reach * rows, lanes)
            values = held[0:reach, m, 2].reshape(reach * rows, lanes)

            def head_step(head, total):
                head_queries, head_grad = one_head(queries, head), one_head(grad_out, head)
                probs = soft_columns(key_rows, head_queries, span * block * rows, length)
                grad_probs = over_lanes(values, head_grad)
                inner = jnp.sum(probs * grad_probs, 0, keepdims=True)
                grad_scores = (probs * (grad_probs - inner)).astype(jnp.bfloat16)
                value_total[0 : reach * rows] += plain(probs.astype(jnp.bfloat16), head_grad)
                key_total[0 : reach * rows] += plain(grad_scores, head_queries)
                return total + over_rows(one_head(key_rows, head), grad_scores)

            total = lax.fori_loop(0, 2, head_step, jnp.zeros((lanes, span * rows), jnp.float32))
            staged[span * block : reach, m, 0] = (
                (scale * total).T.astype(jnp.bfloat16).reshape(span, rows, lanes)
            )
        staged[:, m, 1] = (scale * key_total[...]).astype(jnp.bfloat16).reshape(count, rows, lanes)
        staged[:, m, 2] = value_total[...].astype(jnp.bfloat16).reshape(count, rows, lanes)
        for j in peer_range:
            back(m, j).start()
        for copy in own_back(m):
            copy.start()

    for m in range(micros):
        last_head(m)
    for m in range(micros):
        micro(m)
    unit, deviation = normalize(inputs[...])
    if not ship:
        normed_one[...] = (unit * vectors[0:1] + vectors[1:2]).astype(jnp.bfloat16)
    for m in range(micros):
        here = slice(m * rows, (m + 1) * rows)
        for copy in own_back(m):
            copy.wait()
        for j in peer_range:
            back_last(m, j).wait_recv()
            back(m, j).wait_recv()
        last = jnp.sum(parts_last[:, m].astype(jnp.float32), 0).astype(jnp.bfloat16)
        grad_k[here, wide:] = narrow(last, 0)
        grad_v[here, wide:] = narrow(last, HEAD)
        for third, target in enumerate((grad_q, grad_k, grad_v)):
            for d in range(count):
                target[here, d * lanes : (d + 1) * lanes] = grads[d, m, third]
        if m == 0:
            for i in (3, 4, 5):
                loads[i].wait()
        pulled = over_lanes(grad_q[here], vqkv[0])
        pulled += over_lanes(grad_k[here], vqkv[1])
        pulled += over_lanes(grad_v[here], vqkv[2])
        from_norm, gain_sum, bias_sum = norm_back(
            unit[here], deviation[here], vectors[0:1], pulled
        )
        total = grad_norm[here] + from_norm
        grad_in[here] = total
        if ship:
            leaving[m] = total.astype(jnp.bfloat16)
            ship_copy(m).start()
        if m == 0:
            vector_grads[0:1] = gain_sum
            vector_grads[1:2] = bias_sum
        else:
            vector_grads[0:1] += gain_sum
            vector_grads[1:2] += bias_sum
    if not ship:
        vector_grads[2:3] = column_sum(grad_q[...])
    if not ship:
        vector_grads[3:4] = column_sum(grad_v[...])
    for m in range(micros):
        for j in peer_range:
            out(m, j).wait_send()
            back_last(m, j).wait_send()
            back(m, j).wait_send()
        if ship:
            ship_copy(m).wait()


def backward_layer(ship, lengths, grad_output, saved, vectors, weights):
    inputs, hidden, pre_act, held, held_last, last_q = saved
    count, micros, _, rows, lanes = held.shape
    total, width = inputs.shape
    bf16, f32 = jnp.bfloat16, jnp.float32
    vmem, hbm = pl.BlockSpec(memory_space=pltpu.VMEM), pl.BlockSpec(memory_space=pl.ANY)
    dma = pltpu.SemaphoreType.DMA
    narrow_out, wide_out = (total, width), pre_act.shape
    blocks, pack = (count, micros, rows, lanes), (count, micros, 3, rows, lanes)
    return layer_call(
        backward_kernel,
        ship,
        (
            lengths, grad_output, inputs, hidden, vectors, pre_act, held, held_last, last_q,
            *weights,
        ),
        [pl.BlockSpec(memory_space=pltpu.SMEM)] + [vmem] * 8 + [hbm] * 6,
        [
            jax.ShapeDtypeStruct(shape, dtype)
            for shape, dtype in (
                (narrow_out, f32),
                (narrow_out, bf16),
                (narrow_out, bf16),
                (narrow_out, bf16),
                (narrow_out, bf16),
                (wide_out, bf16),
                (wide_out, bf16),
                (narrow_out, bf16),
                (narrow_out, bf16),
                ((8, width), f32),
                ((1, pre_act.shape[1]), f32),
                ((micros, rows, width), bf16),
            )
        ],
        [vmem] * 11 + [hbm],
        [
            pltpu.VMEM(weights[3].shape, bf16),
            pltpu.VMEM(weights[4].shape, bf16),
            pltpu.VMEM(weights[5].shape, bf16),
            pltpu.VMEM((3,) + weights[0].shape, bf16),
            pltpu.VMEM(narrow_out, f32),
            pltpu.VMEM(blocks, bf16),
            pltpu.VMEM((micros, rows, lanes), bf16),
            pltpu.VMEM(blocks, bf16),
            pltpu.VMEM(pack, bf16),
            pltpu.VMEM(blocks, bf16),
            pltpu.VMEM(pack, bf16),
            pltpu.VMEM(blocks, bf16),
            pltpu.VMEM((count * rows, lanes), f32),
            pltpu.VMEM((count * rows, lanes), f32),
            pltpu.VMEM((micros, rows, lanes), bf16),
            pltpu.VMEM((micros, rows, width), bf16),
        ]
        + [dma((micros, count - 1))] * 6
        + [dma((micros, 3)), dma((6,)), dma((micros,)), dma((micros,))],
        compiler_params=pltpu.CompilerParams(
            collective_id=5 if ship else 3, has_side_effects=True, vmem_limit_bytes=62 * 1024 * 1024
        ),
        name="backward_ship" if ship else "backward_layer",
    )


def in_blocks(matrix):
    return matrix.reshape(matrix.shape[0] // 8, 8, matrix.shape[1])


def body(
    block_input, out_grad, w_qkv, w_proj, w_up, w_down, vectors, b_up, seq_lengths, slot_of_seq
):
    section = lax.axis_index("pipe")
    replica = lax.axis_index("rep")
    member = lax.axis_index("group")
    rep_count = lax.axis_size("rep")
    count = lax.axis_size("group")
    micros, rows, width = block_input.shape[0], block_input.shape[2], block_input.shape[3]
    slot_ids = jnp.arange(seq_lengths.shape[0], dtype=jnp.int32)
    slot_len = jnp.sum(
        seq_lengths[:, None] * (slot_of_seq[:, None] == slot_ids[None, :]).astype(jnp.int32), axis=0
    )
    mine = jnp.arange(micros, dtype=jnp.int32) * rep_count + replica
    lengths = jnp.sum(
        slot_len[None, :] * (slot_ids[None, :] == mine[:, None]).astype(jnp.int32), axis=1
    )
    query_pos = member * rows + jnp.arange(rows, dtype=jnp.int32)
    valid = (query_pos[None, :] < lengths[:, None]).astype(jnp.float32)[:, :, None]
    cotangent = (out_grad[:, 0].astype(jnp.float32) * valid).reshape(micros * rows, width)

    bias_rows = b_up.shape[1] // vectors.shape[2]
    small = jnp.concatenate(
        [
            vectors[0],
            b_up[0].reshape(bias_rows, -1),
            jnp.zeros((8 - bias_rows, vectors.shape[2]), vectors.dtype),
        ],
        0,
    )
    thirds = [w_qkv[0][:, i * width : (i + 1) * width] for i in range(3)]
    first_in = block_input[:, 0].reshape(micros * rows, width).astype(jnp.float32)
    small_full, *full, arrived = first_layer(
        lengths,
        first_in,
        [in_blocks(array) for array in (small, *thirds, w_proj[0], w_up[0], w_down[0])],
        (
            (6, 0, 68, True),
            (5, 0, 16, True),
            (0, 0, 2, False),
            (1, 0, 17, False),
            (2, 0, 17, False),
            (3, 0, 17, False),
            (4, 0, 17, False),
            (5, 16, 1, False),
        ),
        count,
        micros,
    )
    vector_rows = small_full[:, 0].transpose(1, 0, 2).reshape(8, width).astype(jnp.float32)
    up_bias = small_full[:, 1, :bias_rows].reshape(1, -1).astype(jnp.float32)
    weights = [array.reshape(-1, array.shape[-1]) for array in full]

    def landed(blocks):
        return blocks.reshape(micros * rows, width).astype(jnp.float32)

    inputs = jnp.where(section == 0, first_in, landed(arrived))
    output, hidden, pre_act, attn_mixed, last_q, held, held_last, _ = forward_layer(
        lengths, inputs, vector_rows, up_bias, weights, count, micros
    )
    saved = (inputs, hidden, pre_act, held, held_last, last_q)
    *_, arrived = backward_layer(True, lengths, cotangent, saved, vector_rows, weights)
    grad_output = jnp.where(section == 1, cotangent, landed(arrived))
    (
        grad_in, grad_q, grad_k, grad_v, grad_one, grad_pre, activated, normed_one, normed_two,
        grad_vectors, grad_bias, _,
    ) = backward_layer(False, lengths, grad_output, saved, vector_rows, weights)

    small_grads = jnp.concatenate(
        [
            grad_vectors.reshape(8, count, -1).transpose(1, 0, 2),
            grad_bias.reshape(count, bias_rows, -1),
            jnp.zeros((count, 24 - bias_rows, width // count), jnp.float32),
        ],
        1,
    ).reshape(count * RING, 8, width // count)
    blocks = width // count // 8
    tall = grad_pre.shape[1] // count // 8
    half, tall_half = (blocks + 1) // 2, tall // 8 * 4 + 4
    arrays = {
        "Q": (0, 1, (blocks, 0, blocks), False),
        "K": (0, 2, (blocks, 0, blocks), False),
        "V": (0, 3, (blocks, 0, blocks), False),
        "P": (4, 5, (blocks, 0, blocks), False),
        "U": (6, 7, (blocks, 0, half), False),
        "u": (6, 7, (blocks, half, blocks - half), False),
        "D": (8, 9, (tall, 0, tall_half), True),
        "d": (8, 9, (tall, tall_half, tall - tall_half), True),
        "S": (10, None, (RING, 0, RING), False),
    }
    sums = sum_gradients(
        (
            normed_one, grad_q, grad_k, grad_v, attn_mixed, grad_one, normed_two, grad_pre, activated,
            grad_output.astype(jnp.bfloat16), small_grads,
        ),
        arrays,
        SUM_ORDER,
    )
    sums = dict(zip(arrays, sums))
    places = {
        "Q": (0, 0, 0, blocks),
        "K": (0, 0, width, blocks),
        "V": (0, 0, 2 * width, blocks),
        "P": (1, 0, 0, blocks),
        "U": (2, 0, 0, half),
        "u": (2, half * 8, 0, blocks - half),
        "D": (3, 0, 0, tall_half),
        "d": (3, tall_half * 8, 0, tall - tall_half),
    }
    grad_shapes = [(w.shape[1], w.shape[2]) for w in (w_qkv, w_proj, w_up, w_down)]
    totals = assemble(sums, places, grad_shapes)
    small_total = sums["S"].reshape(RING * 8, -1)
    edges = jnp.where(section == 0, grad_in, output).reshape(1, micros, 1, rows, width)
    return (
        edges,
        totals[0][None],
        totals[1][None],
        totals[2][None],
        totals[3][None],
        small_total[None, :8],
        small_total[8 : 8 + bias_rows].reshape(1, -1),
    )


def solution(mesh):
    in_specs = (
        P(None, "rep", "group", None),
        P(None, "rep", "group", None),
        P("pipe", "group", None),
        P("pipe", "group", None),
        P("pipe", "group", None),
        P("pipe", "group", None),
        P("pipe", None, "group"),
        P("pipe", "group"),
        P(),
        P(),
    )
    out_specs = (
        P("pipe", None, "rep", "group", None),
        P("pipe", "group", None),
        P("pipe", "group", None),
        P("pipe", "group", None),
        P("pipe", "group", None),
        P("pipe", None, "group"),
        P("pipe", "group"),
    )
    return jax.shard_map(body, mesh=mesh, in_specs=in_specs, out_specs=out_specs, check_vma=False)
```
